32 devices in a mesh: groups: 2 (over x), facet: 16 (over z, y, core).
Axes of the slice: x: 2, y: 2, z: 4, core: 2. Of those that a mesh axis runs over, the one named last changes fastest.
Arguments:
- facets: bfloat16 [32, 2, 512, 512], P(('groups', 'facet')), parts along dimension 0, may hold values from -6 to 6
- facet_offsets: int32 [32, 2], P(('groups', 'facet')), parts along dimension 0, may hold values from 0 to 511
- subgrid_offsets: int32 [32, 2], P('groups'), parts along dimension 0, may hold values from 0 to 511
- w_terms: float32 [32], P(('groups', 'facet')), parts along dimension 0, may hold values from 2 to 16
- tile_count: int32 [32], P(('groups', 'facet')), parts along dimension 0, may hold values from 1 to 16, as said below
- tile_offsets: int32 [512, 2], P(('groups', 'facet')), parts along dimension 0, may hold values from 0 to 256
- observed: bfloat16 [512, 2, 128, 128], P(('groups', 'facet')), parts along dimension 0, may hold values from -6 to 6
Outputs:
- residual: bfloat16 [512, 2, 128, 128], P(('groups', 'facet')), parts along dimension 0
- facet_update: bfloat16 [32, 2, 512, 512], P(('groups', 'facet')), parts along dimension 0
The draws below stay inside these ranges and needn't reach their ends.
There are 2 independent parts, one for each index of `groups`. The reference program is written for one: setup_inputs(seed, part) draws one part's arguments, and reference() takes and returns one part's arrays. A program takes and returns all parts, laid end to end along the dimension named above; each array names one. Nothing has to cross between parts.
Inputs may be any that keep to these rules, and one draw needn't show every extreme that they name: `tile_count`: live tile slots of each subgrid; some subgrid has all 16 slots live in every draw.
All inputs are finite; a program needn't handle non-finite values.
Results may differ from the reference program's by a relative error of at most 0.017.
Values may be sent and summed in bfloat16 or wider, within the bound.
No kernel may reach another device: no remote copies, remote signals or barrier semaphores. Data moves between devices by JAX's collectives and lax.ppermute only.
A program may use at most 64 MiB of HBM per device.

```python
import math
import jax
import jax.numpy as jnp
from jax import lax

F = 512
M = 128
SG = 512
TV = 128
TCAP = 16
FACETS = 16
TILES = 256


def draw_tile_count(key, part):
    keys = jax.random.split(key, 4)
    light = jax.random.randint(keys[0], (FACETS,), 1, max(2, TCAP // 4 + 1))
    heavy = jax.random.randint(keys[1], (FACETS,), max(1, TCAP // 2), TCAP + 1)
    chosen = jax.random.randint(keys[2], (FACETS,), 0, 8) == 0
    counts = jnp.where(chosen, heavy, light)
    fullest = jax.random.randint(keys[3], (), 0, FACETS)
    counts = jnp.where(jnp.arange(FACETS) == fullest, TCAP, counts)
    return counts.astype(jnp.int32)


def plant(array, key, smallest, high):
    longest = array.shape.index(max(array.shape))
    spots = []
    for shift in (0, 1):
        where = [jax.random.randint(jax.random.fold_in(key, axis), (), 0, length) for axis, length in enumerate(array.shape)]
        where[longest] = (where[longest] + shift) % array.shape[longest]
        spots.append(tuple(where))
    return array.at[spots[0]].set(smallest).at[spots[1]].set(high)


def shard_levels(key, extent, cuts, least, largest):
    level = 1.0
    for axis_at, parts in cuts:
        heights = jax.random.uniform(jax.random.fold_in(jax.random.fold_in(key, 6), axis_at), (parts,), jnp.float32, least / len(cuts), largest / len(cuts))
        level = level * jnp.repeat(jnp.exp(heights), extent[axis_at] // parts).reshape((-1,) + (1,) * (len(extent) - 1 - axis_at))
    return level


def scatter_about(rng, dims, scale, bound, cuts=(), kind=jnp.bfloat16):
    drawn = scale * jax.random.normal(rng, dims, jnp.float32)
    if cuts:
        drawn = drawn * shard_levels(rng, dims, cuts, -0.22, 0.18)
    return jnp.clip(drawn, -bound, bound).astype(kind)


def setup_inputs(seed: int = 0, part: int = 0) -> dict:
    key_list = jax.random.split(jax.random.key(seed), 8)
    part_splits = jax.random.split(jax.random.fold_in(key_list[7], part), 8)
    facets = scatter_about(part_splits[0], (FACETS, 2, F, F), 1.0, 6.0, ((0, 16),))
    facet_offsets = plant(jax.random.randint(part_splits[1], (FACETS, 2), 0, F), jax.random.fold_in(part_splits[1], 1), 0, F - 1).astype(jnp.int32)
    subgrid_offsets = plant(jax.random.randint(part_splits[2], (FACETS, 2), 0, F), jax.random.fold_in(part_splits[2], 1), 0, F - 1).astype(jnp.int32)
    w_terms = jnp.clip(jnp.exp(math.log(16.0) - 2.0794415 * jax.random.uniform(part_splits[3], (FACETS,), jnp.float32) ** shard_levels(part_splits[3], (FACETS,), ((0, 16),), -0.2, 0.2)), 2.0, 16.0)
    tile_count = draw_tile_count(jax.random.fold_in(jax.random.fold_in(key_list[7], part), 71), part)
    tile_offsets = plant(jax.random.randint(part_splits[5], (TILES, 2), 0, SG - 2 * TV + 1), jax.random.fold_in(part_splits[5], 1), 0, SG - 2 * TV).astype(jnp.int32)
    observed = scatter_about(part_splits[6], (TILES, 2, TV, TV), 1.0, 6.0, ((0, 16),))
    return {"facets": facets, "facet_offsets": facet_offsets, "subgrid_offsets": subgrid_offsets, "w_terms": w_terms, "tile_count": tile_count, "tile_offsets": tile_offsets, "observed": observed}


TWO_PI = 2.0 * math.pi

def basis_tables():
    index_f = jnp.arange(F, dtype=jnp.int32)
    product = index_f[:, None] * index_f[None, :] % F
    angle = -TWO_PI * product.astype(jnp.float32) / F
    scale = 1.0 / math.sqrt(F)
    return ((jnp.cos(angle) * scale).astype(jnp.bfloat16), (jnp.sin(angle) * scale).astype(jnp.bfloat16))

def padding_tables(facet_count):
    rows = jnp.arange(SG, dtype=jnp.int32)
    columns = jnp.arange(M, dtype=jnp.int32)
    product = rows[:, None] * columns[None, :] % SG
    angle = TWO_PI * product.astype(jnp.float32) / SG
    scale = (M * math.sqrt(facet_count)) ** (-0.5)
    return ((jnp.cos(angle) * scale).astype(jnp.bfloat16), (jnp.sin(angle) * scale).astype(jnp.bfloat16))

def taper_square():
    position = jnp.arange(M, dtype=jnp.float32)
    taper = 0.6 + 0.4 * jnp.sin(math.pi * (position + 0.5) / M)
    return taper[:, None] * taper[None, :]

def kernel_table():
    rows = jnp.arange(TV, dtype=jnp.float32)[:, None]
    columns = jnp.arange(2 * TV, dtype=jnp.float32)[None, :]
    distance = columns - 2.0 * rows - 1.0
    value = 0.75 * jnp.exp(-(distance / 1.5) * (distance / 1.5))
    return jnp.where(jnp.abs(distance) <= 4.0, value, jnp.zeros_like(value)).astype(jnp.bfloat16)

def facet_phase(offset):
    index_m = jnp.arange(M, dtype=jnp.int32)
    total = ((index_m * offset[0])[:, None] + (index_m * offset[1])[None, :]) % F
    angle = TWO_PI * total.astype(jnp.float32) / F
    return (jnp.cos(angle), jnp.sin(angle))

def screen_table(w_value):
    centred = jnp.arange(SG, dtype=jnp.float32) - SG / 2.0
    radius = (centred[:, None] * centred[:, None] + centred[None, :] * centred[None, :]) / (SG * SG)
    angle = TWO_PI * w_value * (jnp.sqrt(1.0 + radius) - 1.0)
    return (jnp.cos(angle), jnp.sin(angle))

def matmul(left, right):
    return jnp.dot(left, right, preferred_element_type=jnp.float32)

def complex_dot(left_real, left_imag, right_real, right_imag):
    real_part = matmul(left_real, right_real) - matmul(left_imag, right_imag)
    imag_part = matmul(left_real, right_imag) + matmul(left_imag, right_real)
    return (real_part, imag_part)

def facet_spectrum(facet, basis_real, basis_imag):
    half_real, half_imag = complex_dot(facet[0], facet[1], basis_real.T, basis_imag.T)
    return complex_dot(basis_real, basis_imag, half_real.astype(jnp.bfloat16), half_imag.astype(jnp.bfloat16))

def extract(spectrum_real, spectrum_imag, offsets, phase_cos, phase_sin, taper2):
    stacked = jnp.stack([spectrum_real, spectrum_imag])
    padded = jnp.concatenate([stacked, stacked[:, :M, :]], axis=1)
    padded = jnp.concatenate([padded, padded[:, :, :M]], axis=2)
    zero = jnp.zeros((), jnp.int32)

    def window(offset):
        return lax.dynamic_slice(padded, (zero, offset[0].astype(jnp.int32), offset[1].astype(jnp.int32)), (2, M, M))
    windows = jax.vmap(window)(offsets)
    real_part = taper2 * (phase_cos * windows[:, 0] - phase_sin * windows[:, 1])
    imag_part = taper2 * (phase_cos * windows[:, 1] + phase_sin * windows[:, 0])
    return jnp.stack([real_part, imag_part], axis=1).astype(jnp.bfloat16)

def subgrid_model(summed, pad_real, pad_imag, screen_cos, screen_sin):
    inner_real, inner_imag = complex_dot(pad_real, pad_imag, summed[0], summed[1])
    image_real, image_imag = complex_dot(inner_real.astype(jnp.bfloat16), inner_imag.astype(jnp.bfloat16), pad_real.T, pad_imag.T)
    model_real = screen_cos * image_real - screen_sin * image_imag
    model_imag = screen_cos * image_imag + screen_sin * image_real
    return jnp.stack([model_real, model_imag]).astype(jnp.bfloat16)

def tile_terms(model, observed_tile, offset, kernel):
    zero = jnp.zeros((), jnp.int32)
    window = lax.dynamic_slice(model, (zero, offset[0].astype(jnp.int32), offset[1].astype(jnp.int32)), (2, 2 * TV, 2 * TV))
    kernel32 = kernel.astype(jnp.float32)
    left = jnp.einsum('jq,cqk->cjk', kernel32, window.astype(jnp.float32)).astype(jnp.bfloat16)
    predicted = jnp.einsum('cjk,lk->cjl', left.astype(jnp.float32), kernel32)
    residual = (observed_tile.astype(jnp.float32) - predicted).astype(jnp.bfloat16)
    back = jnp.einsum('cjl,lk->cjk', residual.astype(jnp.float32), kernel32).astype(jnp.bfloat16)
    spread = jnp.einsum('jq,cjk->cqk', kernel32, back.astype(jnp.float32))
    return (residual, spread)

def add_window(adjoint, spread, offset):
    zero = jnp.zeros((), jnp.int32)
    start = (zero, offset[0].astype(jnp.int32), offset[1].astype(jnp.int32))
    current = lax.dynamic_slice(adjoint, start, spread.shape)
    return lax.dynamic_update_slice(adjoint, current + spread, start)

def back_coefficients(adjoint, pad_real, pad_imag, screen_cos, screen_sin):
    screened_real = (screen_cos * adjoint[0] + screen_sin * adjoint[1]).astype(jnp.bfloat16)
    screened_imag = (screen_cos * adjoint[1] - screen_sin * adjoint[0]).astype(jnp.bfloat16)
    reduced_real = (matmul(pad_real.T, screened_real) + matmul(pad_imag.T, screened_imag)).astype(jnp.bfloat16)
    reduced_imag = (matmul(pad_real.T, screened_imag) - matmul(pad_imag.T, screened_real)).astype(jnp.bfloat16)
    coef_real = matmul(reduced_real, pad_real) + matmul(reduced_imag, pad_imag)
    coef_imag = matmul(reduced_imag, pad_real) - matmul(reduced_real, pad_imag)
    return jnp.stack([coef_real, coef_imag]).astype(jnp.bfloat16)

def facet_back(back_spectrum, basis_real, basis_imag):
    half_real = (matmul(basis_real, back_spectrum[0]) + matmul(basis_imag, back_spectrum[1])).astype(jnp.bfloat16)
    half_imag = (matmul(basis_real, back_spectrum[1]) - matmul(basis_imag, back_spectrum[0])).astype(jnp.bfloat16)
    update_real = matmul(half_real, basis_real) + matmul(half_imag, basis_imag)
    update_imag = matmul(half_imag, basis_real) - matmul(half_real, basis_imag)
    return jnp.stack([update_real, update_imag]).astype(jnp.bfloat16)

def reference(facets, facet_offsets, subgrid_offsets, w_terms, tile_count, tile_offsets, observed):
    facet_count = facets.shape[0]
    basis_real, basis_imag = basis_tables()
    pad_real, pad_imag = padding_tables(facet_count)
    taper2 = taper_square()
    kernel = kernel_table()

    def forward_step(total, inputs):
        facet, offset = inputs
        spectrum_real, spectrum_imag = facet_spectrum(facet, basis_real, basis_imag)
        phase_cos, phase_sin = facet_phase(offset)
        contribution = extract(spectrum_real, spectrum_imag, subgrid_offsets, phase_cos, phase_sin, taper2)
        return (total + contribution.astype(jnp.float32), None)
    summed, _ = lax.scan(forward_step, jnp.zeros((facet_count, 2, M, M), jnp.float32), (facets, facet_offsets))
    observed_dev = observed.reshape(facet_count, TCAP, 2, TV, TV)
    offsets_dev = tile_offsets.reshape(facet_count, TCAP, 2)

    def subgrid_step(inputs):
        summed_one, w_value, count, tile_obs, tile_off = inputs
        screen_cos, screen_sin = screen_table(w_value)
        model = subgrid_model(summed_one.astype(jnp.bfloat16), pad_real, pad_imag, screen_cos, screen_sin)

        def tile_step(adjoint, tile_in):
            observed_tile, offset, slot = tile_in
            residual, spread = tile_terms(model, observed_tile, offset, kernel)
            live = slot < count
            residual = jnp.where(live, residual, jnp.zeros_like(residual))
            spread = jnp.where(live, spread, jnp.zeros_like(spread))
            return (add_window(adjoint, spread, offset), residual)
        adjoint, residuals = lax.scan(tile_step, jnp.zeros((2, SG, SG), jnp.float32), (tile_obs, tile_off, jnp.arange(TCAP, dtype=jnp.int32)))
        return (residuals, back_coefficients(adjoint, pad_real, pad_imag, screen_cos, screen_sin))
    residuals, coefficients = lax.map(subgrid_step, (summed, w_terms, tile_count, observed_dev, offsets_dev))
    index_m = jnp.arange(M, dtype=jnp.int32)
    row_index = (subgrid_offsets[:, 0:1] + index_m[None, :]) % F
    column_index = (subgrid_offsets[:, 1:2] + index_m[None, :]) % F
    coef32 = coefficients.astype(jnp.float32)

    def backward_step(offset):
        phase_cos, phase_sin = facet_phase(offset)
        values_real = taper2 * (phase_cos * coef32[:, 0] + phase_sin * coef32[:, 1])
        values_imag = taper2 * (phase_cos * coef32[:, 1] - phase_sin * coef32[:, 0])
        values = jnp.stack([values_real, values_imag])
        spectrum = jnp.zeros((2, F, F), jnp.float32).at[:, row_index[:, :, None], column_index[:, None, :]].add(values)
        return facet_back(spectrum.astype(jnp.bfloat16), basis_real, basis_imag)
    updates = lax.map(backward_step, facet_offsets)
    return (residuals.reshape(facet_count * TCAP, 2, TV, TV), updates)
```

```python
import functools
import math

import jax
import jax.numpy as jnp
import ml_dtypes
import numpy as np
from jax import lax
from jax.experimental import pallas as pl
from jax.experimental.pallas import tpu as pltpu
from jax.sharding import PartitionSpec as P

F = 512
M = 128
SG = 512
TV = 128
BF = jnp.bfloat16
F32 = jnp.float32
TWO_PI = 2.0 * math.pi
VMEM_LIMIT = 56 * 1024 * 1024


def basis_tables():
    index = np.arange(F, dtype=np.int64)
    angle = -TWO_PI * ((index[:, None] * index[None, :]) % F) / F
    table = np.stack([np.cos(angle), np.sin(angle)]) / math.sqrt(F)
    return table.astype(ml_dtypes.bfloat16)


def padding_tables(facet_count):
    product = (np.arange(SG)[:, None] * np.arange(M)[None, :]) % SG
    angle = TWO_PI * product / SG
    scale = (M * math.sqrt(facet_count)) ** (-0.5)
    table = np.stack([np.cos(angle), np.sin(angle)]) * scale
    return table.astype(ml_dtypes.bfloat16)


def kernel_table():
    rows = np.arange(TV, dtype=np.float64)[:, None]
    columns = np.arange(2 * TV, dtype=np.float64)[None, :]
    distance = columns - 2.0 * rows - 1.0
    value = 0.75 * np.exp(-((distance / 1.5) ** 2))
    return np.where(np.abs(distance) <= 4.0, value, 0.0).astype(ml_dtypes.bfloat16)


def taper_square():
    position = np.arange(M, dtype=np.float64)
    taper = 0.6 + 0.4 * np.sin(math.pi * (position + 0.5) / M)
    return (taper[:, None] * taper[None, :]).astype(np.float32)


def turn_polynomials():
    nodes = 0.5 * np.cos(math.pi * (np.arange(400) + 0.5) / 800)
    square = nodes * nodes
    powers = np.stack([square**k for k in range(8)], axis=1)
    cos_c = np.linalg.lstsq(powers, np.cos(TWO_PI * nodes), rcond=None)[0]
    sin_c = np.linalg.lstsq(powers, np.sin(TWO_PI * nodes) / nodes, rcond=None)[0]
    return [float(c) for c in cos_c], [float(c) for c in sin_c]


COS_C, SIN_C = turn_polynomials()


def cos_sin_turns(turns):
    rest = turns - jnp.floor(turns + 0.5)
    square = rest * rest
    cos_v = jnp.full_like(square, COS_C[7])
    sin_v = jnp.full_like(square, SIN_C[7])
    for k in range(6, -1, -1):
        cos_v = cos_v * square + COS_C[k]
        sin_v = sin_v * square + SIN_C[k]
    return cos_v, sin_v * rest


def dot(left, right):
    return jnp.dot(left, right, preferred_element_type=F32)


def dot_nt(left, right):
    return lax.dot_general(left, right, (((1,), (1,)), ((), ())), preferred_element_type=F32)


def phase_taper(fo_ref, taper_ref):
    rows = lax.broadcasted_iota(jnp.int32, (M, M), 0)
    columns = lax.broadcasted_iota(jnp.int32, (M, M), 1)
    total = (rows * fo_ref[0, 0] + columns * fo_ref[0, 1]) & (F - 1)
    cos_v, sin_v = cos_sin_turns(total.astype(F32) * (1.0 / F))
    taper2 = taper_ref[...]
    return cos_v * taper2, sin_v * taper2


def forward_kernel(stages, me_ref, fo_ref, so_ref, facet_ref, basis_ref, taper_ref, *rest):
    outs, (half_ref, spec_ref) = rest[: len(stages)], rest[len(stages) :]
    br, bi = basis_ref[0], basis_ref[1]
    fr, fi = facet_ref[0, 0], facet_ref[0, 1]
    half_ref[0] = (dot(fr, br) - dot(fi, bi)).astype(BF)
    half_ref[1] = (dot(fr, bi) + dot(fi, br)).astype(BF)
    hr, hi = half_ref[0], half_ref[1]
    spectrum = (dot(br, hr) - dot(bi, hi), dot(br, hi) + dot(bi, hr))
    columns = F // M
    for plane in range(2):
        for c in range(columns):
            part = spectrum[plane][:, c * M : (c + 1) * M]
            spec_ref[plane, c, :F] = part
            spec_ref[plane, c, F:] = part[:M]
            if c == 0:
                spec_ref[plane, columns, :F] = part
                spec_ref[plane, columns, F:] = part[:M]
    pc, ps = phase_taper(fo_ref, taper_ref)
    me = me_ref[0]

    def block(out_ref, item, j):
        owner = j ^ me
        sx, sy = so_ref[owner, 0], so_ref[owner, 1]
        lane = sy // M
        shift = (2 * M - (sy & (M - 1))) & (2 * M - 1)
        parts = []
        for plane in range(2):
            left = spec_ref[plane, lane, pl.ds(sx, M), :]
            right = spec_ref[plane, lane + 1, pl.ds(sx, M), :]
            wide = jnp.concatenate([left, right], axis=1)
            parts.append(pltpu.roll(wide, shift, 1)[:, :M])
        wr, wi = parts
        out_ref[item, 0] = (pc * wr - ps * wi).astype(BF)
        out_ref[item, 1] = (pc * wi + ps * wr).astype(BF)

    for out_ref, (count, step, first) in zip(outs, stages):
        if count == 1:
            block(out_ref, 0, first)
        else:

            def body(item, carry, out_ref=out_ref, step=step, first=first):
                block(out_ref, item, item * step + first)
                return carry

            lax.fori_loop(0, count, body, 0)


def subgrid_kernel(
    parts, w_ref, tc_ref, to_ref, *rest
):
    sums = rest[:parts]
    (obs_ref, pad_ref, padt_ref, kern_ref, kt_ref, res_ref, coef_ref) = rest[parts : parts + 7]
    (screen_ref, model_ref, kvt_ref, rows_ref, z_ref) = rest[parts + 7 :]
    slots = obs_ref.shape[0]
    count = tc_ref[0]
    w = w_ref[0]

    row = lax.broadcasted_iota(jnp.int32, (SG, 1), 0).astype(F32) - SG / 2.0
    column = lax.broadcasted_iota(jnp.int32, (1, SG), 1).astype(F32) - SG / 2.0
    row2 = row * row * (1.0 / (SG * SG)) + 1.0
    column2 = column * column * (1.0 / (SG * SG))
    cos_v, sin_v = cos_sin_turns((jnp.sqrt(row2 + column2) - 1.0) * w)
    screen_ref[0] = cos_v
    screen_ref[1] = sin_v

    for t in range(slots):
        band = kt_ref[pl.ds(2 * TV - to_ref[t, 1], SG), :]
        kvt_ref[:, t * TV : (t + 1) * TV] = band.astype(BF)

    def total(plane):
        value = sums[0][0, plane].astype(F32)
        for ref in sums[1:]:
            value = value + ref[0, plane].astype(F32)
        return value.astype(BF)

    sr, si = total(0), total(1)
    pr, pi = pad_ref[0], pad_ref[1]
    inner_r = (dot(pr, sr) - dot(pi, si)).astype(BF)
    inner_i = (dot(pr, si) + dot(pi, sr)).astype(BF)
    tr, ti = padt_ref[0], padt_ref[1]
    image_r = dot(inner_r, tr) - dot(inner_i, ti)
    image_i = dot(inner_r, ti) + dot(inner_i, tr)
    sc, ss = screen_ref[0], screen_ref[1]
    model_ref[:SG] = (sc * image_r - ss * image_i).astype(BF)
    model_ref[SG:] = (sc * image_i + ss * image_r).astype(BF)

    model = model_ref[...]
    kern = kern_ref[...]
    for t0 in range(0, slots, 2):
        pair = dot(model, kvt_ref[:, t0 * TV : (t0 + 2) * TV])
        for t in (t0, t0 + 1):
            rows_ref[t % rows_ref.shape[0]] = pair[:, (t - t0) * TV : (t - t0 + 1) * TV]
        for t in (t0, t0 + 1):
            slot = t % rows_ref.shape[0]
            ou = to_ref[t, 0]
            wr = rows_ref[slot, pl.ds(ou, 2 * TV), :]
            wi = rows_ref[slot, pl.ds(SG + ou, 2 * TV), :]
            window = jnp.concatenate([wr.astype(BF), wi.astype(BF)], axis=1)
            predicted = dot(kern, window)
            live = count > t
            res = []
            for plane in range(2):
                value = obs_ref[t, plane].astype(F32) - predicted[:, plane * TV : (plane + 1) * TV]
                res.append(jnp.where(live, value, 0.0).astype(BF))
                res_ref[t, plane] = res[plane]
            band = kt_ref[pl.ds(2 * TV - ou, SG), :].astype(BF)
            z = dot(band, jnp.concatenate(res, axis=1)).astype(BF)
            z_ref[:SG, t * TV : (t + 1) * TV] = z[:, :TV]
            z_ref[SG:, t * TV : (t + 1) * TV] = z[:, TV:]

    kvt = kvt_ref[...]
    ar = dot_nt(z_ref[:SG], kvt)
    ai = dot_nt(z_ref[SG:], kvt)
    screened_r = (sc * ar + ss * ai).astype(BF)
    screened_i = (sc * ai - ss * ar).astype(BF)
    reduced_r = (dot(tr, screened_r) + dot(ti, screened_i)).astype(BF)
    reduced_i = (dot(tr, screened_i) - dot(ti, screened_r)).astype(BF)
    coef_ref[0, 0] = (dot(reduced_r, pr) + dot(reduced_i, pi)).astype(BF)
    coef_ref[0, 1] = (dot(reduced_i, pr) - dot(reduced_r, pi)).astype(BF)


def backward_kernel(pieces, me_ref, fo_ref, so_ref, basis_ref, taper_ref, *rest):
    ins = rest[: len(pieces)]
    out_ref, grid_ref, half_ref = rest[len(pieces) :]
    grid_ref[...] = jnp.zeros_like(grid_ref)
    pc, ps = phase_taper(fo_ref, taper_ref)
    me = me_ref[0]
    blank = jnp.zeros((M, M), F32)

    def block(in_ref, item, j):
        owner = j ^ me
        sx, sy = so_ref[owner, 0], so_ref[owner, 1]
        lane = sy // M
        shift = sy & (M - 1)
        cr, ci = in_ref[item, 0].astype(F32), in_ref[item, 1].astype(F32)
        values = (pc * cr + ps * ci, pc * ci - ps * cr)
        for plane in range(2):
            wide = pltpu.roll(jnp.concatenate([values[plane], blank], axis=1), shift, 1)
            grid_ref[plane, lane, pl.ds(sx, M), :] += wide[:, :M]
            grid_ref[plane, lane + 1, pl.ds(sx, M), :] += wide[:, M:]

    for in_ref, (count, step, first) in zip(ins, pieces):
        if count == 1:
            block(in_ref, 0, first)
        else:

            def body(item, carry, in_ref=in_ref, step=step, first=first):
                block(in_ref, item, item * step + first)
                return carry

            lax.fori_loop(0, count, body, 0)

    columns = F // M
    folded = []
    for plane in range(2):
        grid_ref[plane, 0] += grid_ref[plane, columns]
        for c in range(columns):
            grid_ref[plane, c, :M] += grid_ref[plane, c, F:]
        strips = [grid_ref[plane, c, :F].astype(BF) for c in range(columns)]
        folded.append(jnp.concatenate(strips, axis=1))
    sr, si = folded
    br, bi = basis_ref[0], basis_ref[1]
    half_ref[0] = (dot(br, sr) + dot(bi, si)).astype(BF)
    half_ref[1] = (dot(br, si) - dot(bi, sr)).astype(BF)
    hr, hi = half_ref[0], half_ref[1]
    out_ref[0, 0] = (dot(hr, br) + dot(hi, bi)).astype(BF)
    out_ref[0, 1] = (dot(hi, br) - dot(hr, bi)).astype(BF)


SMEM = pl.BlockSpec(memory_space=pltpu.SMEM)
VMEM = pl.BlockSpec(memory_space=pltpu.VMEM)
PARAMS = pltpu.CompilerParams(vmem_limit_bytes=VMEM_LIMIT)


def blocks(count):
    return jax.ShapeDtypeStruct((count, 2, M, M), BF)


def exchange(value, bit, n):
    return lax.ppermute(value, "facet", [(i, i ^ bit) for i in range(n)])


def per_device(facets, facet_offsets, subgrid_offsets, w_terms, tile_count, tile_offsets, observed):
    n = lax.axis_size("facet")
    bits = [1 << k for k in range(n.bit_length() - 1)]
    me = lax.axis_index("facet").astype(jnp.int32).reshape(1)
    basis = jnp.asarray(basis_tables())
    taper2 = jnp.asarray(taper_square())
    pad_np = padding_tables(n)
    kern_np = kernel_table()
    kt_np = np.zeros((6 * TV, TV), np.float32)
    kt_np[2 * TV : 4 * TV] = kern_np.astype(np.float32).T

    stages = [(n // (2 * b), 2 * b, b) for b in bits] + [(1, 1, 0)]
    own = pl.pallas_call(
        functools.partial(forward_kernel, stages),
        out_shape=[blocks(count) for count, _, _ in stages],
        in_specs=[SMEM] * 3 + [VMEM] * 3,
        out_specs=[VMEM] * len(stages),
        scratch_shapes=[
            pltpu.VMEM((2, F, F), BF),
            pltpu.VMEM((2, F // M + 1, F + M, M), F32),
        ],
        compiler_params=PARAMS,
        name="forward",
    )(me, facet_offsets, subgrid_offsets, facets, basis, taper2)

    arrived = []
    for k, b in enumerate(bits):
        send = own[k]
        if k:
            total = send.astype(F32)
            for i, got in enumerate(arrived):
                skip = b >> (i + 1)
                pick = got.reshape((got.shape[0] // (2 * skip), 2 * skip) + got.shape[1:])[:, skip]
                total = total + pick.astype(F32)
            send = total.astype(BF)
        arrived.append(exchange(send, b, n))
    sums = [own[-1]] + [got[:1] for got in arrived]

    residual, coefficient = pl.pallas_call(
        functools.partial(subgrid_kernel, len(sums)),
        out_shape=[
            jax.ShapeDtypeStruct(observed.shape, BF),
            blocks(1),
        ],
        in_specs=[SMEM] * 3 + [VMEM] * (len(sums) + 5),
        out_specs=[VMEM] * 2,
        scratch_shapes=[
            pltpu.VMEM((2, SG, SG), F32),
            pltpu.VMEM((2 * SG, SG), BF),
            pltpu.VMEM((SG, observed.shape[0] * TV), BF),
            pltpu.VMEM((8, 2 * SG, TV), F32),
            pltpu.VMEM((2 * SG, observed.shape[0] * TV), BF),
        ],
        compiler_params=PARAMS,
        name="subgrid",
    )(
        w_terms,
        tile_count,
        tile_offsets,
        *sums,
        observed,
        jnp.asarray(pad_np),
        jnp.asarray(pad_np.transpose(0, 2, 1)),
        jnp.asarray(kern_np),
        jnp.asarray(kt_np),
    )

    gathered = coefficient
    held = [coefficient]
    pieces = [(1, 1, 0)]
    for b in reversed(bits):
        got = exchange(gathered, b, n)
        held.append(got)
        pieces.append((got.shape[0], 2 * b, b))
        if b > 1:
            gathered = jnp.stack([gathered, got], axis=1).reshape((-1,) + got.shape[1:])

    update = pl.pallas_call(
        functools.partial(backward_kernel, pieces),
        out_shape=jax.ShapeDtypeStruct(facets.shape, BF),
        in_specs=[SMEM] * 3 + [VMEM] * (2 + len(held)),
        out_specs=VMEM,
        scratch_shapes=[
            pltpu.VMEM((2, F // M + 1, F + M, M), F32),
            pltpu.VMEM((2, F, F), BF),
        ],
        compiler_params=PARAMS,
        name="backward",
    )(me, facet_offsets, subgrid_offsets, basis, taper2, *held)
    return (residual, update)


def solution(mesh):
    placed = (
        P(("groups", "facet"), None, None, None),
        P(("groups", "facet"), None),
        P("groups", None),
        P(("groups", "facet")),
        P(("groups", "facet")),
        P(("groups", "facet"), None),
        P(("groups", "facet"), None, None, None),
    )
    return jax.shard_map(
        per_device,
        mesh=mesh,
        in_specs=placed,
        out_specs=(
            P(("groups", "facet"), None, None, None),
            P(("groups", "facet"), None, None, None),
        ),
        check_vma=False,
    )
```

```python
import functools
import math

import jax
import jax.numpy as jnp
import ml_dtypes
import numpy as np
from jax import lax
from jax.experimental import pallas as pl
from jax.experimental.pallas import tpu as pltpu
from jax.sharding import PartitionSpec as P

F = 512
M = 128
SG = 512
TV = 128
BF = jnp.bfloat16
F32 = jnp.float32
TWO_PI = 2.0 * math.pi


def basis_tables():
    index = np.arange(F, dtype=np.int64)
    angle = -TWO_PI * ((index[:, None] * index[None, :]) % F) / F
    table = np.stack([np.cos(angle), np.sin(angle)]) / math.sqrt(F)
    return table.astype(ml_dtypes.bfloat16)


def padding_tables(facet_count):
    product = (np.arange(SG)[:, None] * np.arange(M)[None, :]) % SG
    angle = TWO_PI * product / SG
    scale = (M * math.sqrt(facet_count)) ** (-0.5)
    table = np.stack([np.cos(angle), np.sin(angle)]) * scale
    return table.astype(ml_dtypes.bfloat16)


def kernel_table():
    rows = np.arange(TV, dtype=np.float64)[:, None]
    columns = np.arange(2 * TV, dtype=np.float64)[None, :]
    distance = columns - 2.0 * rows - 1.0
    value = 0.75 * np.exp(-((distance / 1.5) ** 2))
    return np.where(np.abs(distance) <= 4.0, value, 0.0).astype(ml_dtypes.bfloat16)


def taper_square():
    position = np.arange(M, dtype=np.float64)
    taper = 0.6 + 0.4 * np.sin(math.pi * (position + 0.5) / M)
    return (taper[:, None] * taper[None, :]).astype(np.float32)


def turn_polynomials():
    nodes = 0.5 * np.cos(math.pi * (np.arange(400) + 0.5) / 800)
    square = nodes * nodes
    powers = np.stack([square**k for k in range(8)], axis=1)
    cos_c = np.linalg.lstsq(powers, np.cos(TWO_PI * nodes), rcond=None)[0]
    sin_c = np.linalg.lstsq(powers, np.sin(TWO_PI * nodes) / nodes, rcond=None)[0]
    return [float(c) for c in cos_c], [float(c) for c in sin_c]


COS_C, SIN_C = turn_polynomials()


def cos_sin_turns(turns):
    rest = turns - jnp.floor(turns + 0.5)
    square = rest * rest
    cos_v = jnp.full_like(square, COS_C[7])
    sin_v = jnp.full_like(square, SIN_C[7])
    for k in range(6, -1, -1):
        cos_v = cos_v * square + COS_C[k]
        sin_v = sin_v * square + SIN_C[k]
    return cos_v, sin_v * rest


def dot(left, right):
    return jnp.dot(left, right, preferred_element_type=F32)


def phase_taper(fo_ref, taper_ref):
    rows = lax.broadcasted_iota(jnp.int32, (M, M), 0)
    columns = lax.broadcasted_iota(jnp.int32, (M, M), 1)
    total = (rows * fo_ref[0, 0] + columns * fo_ref[0, 1]) & (F - 1)
    cos_v, sin_v = cos_sin_turns(total.astype(F32) * (1.0 / F))
    taper2 = taper_ref[...]
    return cos_v * taper2, sin_v * taper2


def forward_kernel(sends, me_ref, fo_ref, so_ref, facet_ref, basis_ref, taper_ref, *rest):
    outs, (half_ref, spec_ref) = rest[: len(sends)], rest[len(sends) :]
    br, bi = basis_ref[0], basis_ref[1]
    fr, fi = facet_ref[0, 0], facet_ref[0, 1]
    half_ref[0] = (dot(fr, br) - dot(fi, bi)).astype(BF)
    half_ref[1] = (dot(fr, bi) + dot(fi, br)).astype(BF)
    hr, hi = half_ref[0], half_ref[1]
    spectrum = (dot(br, hr) - dot(bi, hi), dot(br, hi) + dot(bi, hr))
    columns = F // M
    for plane in range(2):
        for c in range(columns):
            part = spectrum[plane][:, c * M : (c + 1) * M]
            spec_ref[plane, c, :F] = part
            spec_ref[plane, c, F:] = part[:M]
            if c == 0:
                spec_ref[plane, columns, :F] = part
                spec_ref[plane, columns, F:] = part[:M]
    pc, ps = phase_taper(fo_ref, taper_ref)
    me = me_ref[0]

    def block(out_ref, item, j):
        owner = j ^ me
        sx, sy = so_ref[0, owner], so_ref[1, owner]
        lane = sy // M
        shift = (2 * M - (sy & (M - 1))) & (2 * M - 1)
        parts = []
        for plane in range(2):
            left = spec_ref[plane, lane, pl.ds(sx, M), :]
            right = spec_ref[plane, lane + 1, pl.ds(sx, M), :]
            wide = jnp.concatenate([left, right], axis=1)
            parts.append(pltpu.roll(wide, shift, 1)[:, :M])
        wr, wi = parts
        out_ref[item, 0] = (pc * wr - ps * wi).astype(BF)
        out_ref[item, 1] = (pc * wi + ps * wr).astype(BF)

    for out_ref, js in zip(outs, sends):
        for_blocks(block, out_ref, js)


def for_blocks(block, ref, js):
    step = js[1] - js[0] if len(js) > 1 else 1
    if len(js) > 1 and js == list(range(js[0], js[0] + step * len(js), step)):

        def body(item, carry):
            block(ref, item, item * step + js[0])
            return carry

        lax.fori_loop(0, len(js), body, 0)
    else:
        for item, j in enumerate(js):
            block(ref, item, j)


def prepare_kernel(w_ref, to_ref, kt_ref, kwide_ref, screen_ref, kvt_ref, kv_ref, kut_ref):
    slots = kut_ref.shape[0]
    w = w_ref[0]
    row = lax.broadcasted_iota(jnp.int32, (SG, 1), 0).astype(F32) - SG / 2.0
    column = lax.broadcasted_iota(jnp.int32, (1, SG), 1).astype(F32) - SG / 2.0
    row2 = row * row * (1.0 / (SG * SG)) + 1.0
    column2 = column * column * (1.0 / (SG * SG))
    cos_v, sin_v = cos_sin_turns((jnp.sqrt(row2 + column2) - 1.0) * w)
    screen_ref[0] = cos_v
    screen_ref[1] = sin_v
    for t in range(slots):
        ou, ov = to_ref[0, t], to_ref[1, t]
        kut_ref[t] = kt_ref[pl.ds(2 * TV - ou, SG), :].astype(BF)
        kvt_ref[:, t * TV : (t + 1) * TV] = kt_ref[pl.ds(2 * TV - ov, SG), :].astype(BF)
        kv_ref[t * TV : (t + 1) * TV] = pltpu.roll(kwide_ref[...], ov, 1).astype(BF)


def subgrid_kernel(picks, tc_ref, to_ref, *rest):
    parts = len(picks)
    sums = rest[:parts]
    (obs_ref, pad_ref, padt_ref, kern_ref) = rest[parts : parts + 4]
    (screen_ref, kvt_ref, kv_ref, kut_ref) = rest[parts + 4 : parts + 8]
    (res_ref, coef_ref, model_ref, rows_ref, z_ref) = rest[parts + 8 :]
    slots = obs_ref.shape[0]
    count = tc_ref[0]

    def total(plane):
        value = sums[0][picks[0], plane].astype(F32)
        for ref, item in zip(sums[1:], picks[1:]):
            value = value + ref[item, plane].astype(F32)
        return value.astype(BF)

    sr, si = total(0), total(1)
    pr, pi = pad_ref[0], pad_ref[1]
    inner_r = (dot(pr, sr) - dot(pi, si)).astype(BF)
    inner_i = (dot(pr, si) + dot(pi, sr)).astype(BF)
    tr, ti = padt_ref[0], padt_ref[1]
    image_r = dot(inner_r, tr) - dot(inner_i, ti)
    image_i = dot(inner_r, ti) + dot(inner_i, tr)
    sc, ss = screen_ref[0], screen_ref[1]
    model_ref[:SG] = (sc * image_r - ss * image_i).astype(BF)
    model_ref[SG:] = (sc * image_i + ss * image_r).astype(BF)

    model = model_ref[...]
    kern = kern_ref[...]
    for t0 in range(0, slots, 2):
        pair = dot(model, kvt_ref[:, t0 * TV : (t0 + 2) * TV])
        for t in (t0, t0 + 1):
            rows_ref[t % rows_ref.shape[0]] = pair[:, (t - t0) * TV : (t - t0 + 1) * TV]
        for t in (t0, t0 + 1):
            slot = t % rows_ref.shape[0]
            ou = to_ref[0, t]
            wr = rows_ref[slot, pl.ds(ou, 2 * TV), :]
            wi = rows_ref[slot, pl.ds(SG + ou, 2 * TV), :]
            window = jnp.concatenate([wr.astype(BF), wi.astype(BF)], axis=1)
            predicted = dot(kern, window)
            live = count > t
            res = []
            for plane in range(2):
                value = obs_ref[t, plane].astype(F32) - predicted[:, plane * TV : (plane + 1) * TV]
                res.append(jnp.where(live, value, 0.0).astype(BF))
                res_ref[t, plane] = res[plane]
            z = dot(kut_ref[t], jnp.concatenate(res, axis=1)).astype(BF)
            z_ref[:SG, t * TV : (t + 1) * TV] = z[:, :TV]
            z_ref[SG:, t * TV : (t + 1) * TV] = z[:, TV:]

    kv = kv_ref[...]
    ar = dot(z_ref[:SG], kv)
    ai = dot(z_ref[SG:], kv)
    screened_r = (sc * ar + ss * ai).astype(BF)
    screened_i = (sc * ai - ss * ar).astype(BF)
    reduced_r = (dot(tr, screened_r) + dot(ti, screened_i)).astype(BF)
    reduced_i = (dot(tr, screened_i) - dot(ti, screened_r)).astype(BF)
    coef_ref[0, 0] = (dot(reduced_r, pr) + dot(reduced_i, pi)).astype(BF)
    coef_ref[0, 1] = (dot(reduced_i, pr) - dot(reduced_r, pi)).astype(BF)


def backward_kernel(pieces, me_ref, fo_ref, so_ref, basis_ref, taper_ref, *rest):
    ins = rest[: len(pieces)]
    out_ref, grid_ref, half_ref = rest[len(pieces) :]
    grid_ref[...] = jnp.zeros_like(grid_ref)
    pc, ps = phase_taper(fo_ref, taper_ref)
    me = me_ref[0]
    blank = jnp.zeros((M, M), F32)

    def block(in_ref, item, j):
        owner = j ^ me
        sx, sy = so_ref[0, owner], so_ref[1, owner]
        lane = sy // M
        shift = sy & (M - 1)
        cr, ci = in_ref[item, 0].astype(F32), in_ref[item, 1].astype(F32)
        values = (pc * cr + ps * ci, pc * ci - ps * cr)
        for plane in range(2):
            wide = pltpu.roll(jnp.concatenate([values[plane], blank], axis=1), shift, 1)
            grid_ref[plane, lane, pl.ds(sx, M), :] += wide[:, :M]
            grid_ref[plane, lane + 1, pl.ds(sx, M), :] += wide[:, M:]

    for in_ref, js in zip(ins, pieces):
        for_blocks(block, in_ref, js)

    columns = F // M
    folded = []
    for plane in range(2):
        grid_ref[plane, 0] += grid_ref[plane, columns]
        for c in range(columns):
            grid_ref[plane, c, :M] += grid_ref[plane, c, F:]
        strips = [grid_ref[plane, c, :F].astype(BF) for c in range(columns)]
        folded.append(jnp.concatenate(strips, axis=1))
    sr, si = folded
    br, bi = basis_ref[0], basis_ref[1]
    half_ref[0] = (dot(br, sr) + dot(bi, si)).astype(BF)
    half_ref[1] = (dot(br, si) - dot(bi, sr)).astype(BF)
    hr, hi = half_ref[0], half_ref[1]
    out_ref[0, 0] = (dot(hr, br) + dot(hi, bi)).astype(BF)
    out_ref[0, 1] = (dot(hi, br) - dot(hr, bi)).astype(BF)


SMEM = pl.BlockSpec(memory_space=pltpu.SMEM)
VMEM = pl.BlockSpec(memory_space=pltpu.VMEM)


def params(mib):
    return pltpu.CompilerParams(vmem_limit_bytes=mib * 1024 * 1024)


def near(value):
    return pltpu.with_memory_space_constraint(value, pltpu.VMEM)


def held(shape, dtype=BF):
    return pltpu.VMEM(shape, dtype)


def exchange(value, mask, n):
    return lax.ppermute(value, "facet", [(i, i ^ mask) for i in range(n)])


def digit_levels(n):
    levels, base = [], 1
    while base < n:
        radix = 2 if base < 4 or n // base < 4 else 4
        levels.append((base, radix))
        base *= radix
    return levels


def reduce_sends(n):
    levels = digit_levels(n)
    sends = []
    for k, (base, radix) in enumerate(levels):
        for g in range(1, radix):
            js = [j for j in range(0, n, base) if (j // base) % radix == g]
            if k + 1 < len(levels):
                after, width = levels[k + 1]
                groups = [[j for j in js if (j // after) % width], [j for j in js if not (j // after) % width]]
            else:
                groups = [js]
            sends += [(group, g * base) for group in groups if group]
    return sends


def pick(value, items):
    step = items[1] - items[0] if len(items) > 1 else 1
    if items == list(range(items[0], items[0] + step * len(items), step)):
        if len(items) == value.shape[0]:
            return value
        return lax.slice_in_dim(value, items[0], items[-1] + 1, step)
    return jnp.concatenate([value[i : i + 1] for i in items])


def per_device(facets, facet_offsets, subgrid_offsets, w_terms, tile_count, tile_offsets, observed):
    n = lax.axis_size("facet")
    slots = observed.shape[0]
    me = lax.axis_index("facet").astype(jnp.int32).reshape(1)
    corners = subgrid_offsets.T
    tile_corners = tile_offsets.T
    basis = near(jnp.asarray(basis_tables()))
    taper2 = near(jnp.asarray(taper_square()))
    pad_np = padding_tables(n)
    kern_np = kernel_table()
    kt_np = np.zeros((6 * TV, TV), np.float32)
    kt_np[2 * TV : 4 * TV] = kern_np.astype(np.float32).T
    kwide_np = np.zeros((TV, SG), np.float32)
    kwide_np[:, : 2 * TV] = kern_np.astype(np.float32)

    sends = reduce_sends(n)
    own = pl.pallas_call(
        functools.partial(forward_kernel, [js for js, _ in sends] + [[0]]),
        out_shape=[held((len(js), 2, M, M)) for js, _ in sends] + [held((1, 2, M, M))],
        in_specs=[SMEM] * 3 + [VMEM] * 3,
        out_specs=[VMEM] * (len(sends) + 1),
        scratch_shapes=[
            pltpu.VMEM((2, F, F), BF),
            pltpu.VMEM((2, F // M + 1, F + M, M), F32),
        ],
        compiler_params=params(16),
        name="forward",
    )(me, facet_offsets, corners, facets, basis, taper2)

    screen, kvt, kv, kut = pl.pallas_call(
        prepare_kernel,
        out_shape=[
            held((2, SG, SG), F32),
            held((SG, slots * TV)),
            held((slots * TV, SG)),
            held((slots, SG, TV)),
        ],
        in_specs=[SMEM] * 2 + [VMEM] * 2,
        out_specs=[VMEM] * 4,
        compiler_params=params(8),
        name="prepare",
    )(w_terms, tile_corners, jnp.asarray(kt_np), jnp.asarray(kwide_np))

    arrived = []
    for (js, mask), value in zip(sends, own):
        terms = []
        for got_js, got in arrived:
            if set(js) <= set(got_js):
                terms.append(pick(got, [got_js.index(j) for j in js]))
            else:
                assert not set(js) & set(got_js)
        if terms:
            total = value.astype(F32)
            for term in terms:
                total = total + term.astype(F32)
            value = total.astype(BF)
        arrived.append(([j ^ mask for j in js], exchange(value, mask, n)))
    last = [(js, got) for js, got in arrived if 0 in js]

    residual, coefficient = pl.pallas_call(
        functools.partial(subgrid_kernel, [0] + [js.index(0) for js, _ in last]),
        out_shape=[held(observed.shape), held((1, 2, M, M))],
        in_specs=[SMEM] * 2 + [VMEM] * (len(last) + 9),
        out_specs=[VMEM] * 2,
        scratch_shapes=[
            pltpu.VMEM((2 * SG, SG), BF),
            pltpu.VMEM((8, 2 * SG, TV), F32),
            pltpu.VMEM((2 * SG, slots * TV), BF),
        ],
        compiler_params=params(24),
        name="subgrid",
    )(
        tile_count,
        tile_corners,
        near(own[-1]),
        *[near(got) for _, got in last],
        near(observed),
        near(jnp.asarray(pad_np)),
        near(jnp.asarray(pad_np.transpose(0, 2, 1))),
        near(jnp.asarray(kern_np)),
        near(screen),
        near(kvt),
        near(kv),
        near(kut),
    )

    pieces = [([0], coefficient)]
    for base, radix in reversed(digit_levels(n)):
        more = []
        for js, value in pieces:
            got = [exchange(value, g * base, n) for g in range(1, radix)]
            got_js = [j ^ (g * base) for g in range(1, radix) for j in js]
            more.append((got_js, got[0] if radix == 2 else jnp.concatenate(got)))
        pieces += more

    update = pl.pallas_call(
        functools.partial(backward_kernel, [js for js, _ in pieces]),
        out_shape=jax.ShapeDtypeStruct(facets.shape, BF),
        in_specs=[SMEM] * 3 + [VMEM] * (2 + len(pieces)),
        out_specs=VMEM,
        scratch_shapes=[
            pltpu.VMEM((2, F // M + 1, F + M, M), F32),
            pltpu.VMEM((2, F, F), BF),
        ],
        compiler_params=params(16),
        name="backward",
    )(me, facet_offsets, corners, basis, taper2, *[near(value) for _, value in pieces])
    return (residual, update)


def solution(mesh):
    placed = (
        P(("groups", "facet"), None, None, None),
        P(("groups", "facet"), None),
        P("groups", None),
        P(("groups", "facet")),
        P(("groups", "facet")),
        P(("groups", "facet"), None),
        P(("groups", "facet"), None, None, None),
    )
    return jax.shard_map(
        per_device,
        mesh=mesh,
        in_specs=placed,
        out_specs=(
            P(("groups", "facet"), None, None, None),
            P(("groups", "facet"), None, None, None),
        ),
        check_vma=False,
    )
```

```python
import functools
import math

import jax
import jax.numpy as jnp
import ml_dtypes
import numpy as np
from jax import lax
from jax.experimental import pallas as pl
from jax.experimental.pallas import tpu as pltpu
from jax.sharding import PartitionSpec as P

F = 512
M = 128
SG = 512
TV = 128
BF = jnp.bfloat16
F32 = jnp.float32
TWO_PI = 2.0 * math.pi


def basis_tables():
    index = np.arange(F, dtype=np.int64)
    angle = -TWO_PI * ((index[:, None] * index[None, :]) % F) / F
    table = np.stack([np.cos(angle), np.sin(angle)]) / math.sqrt(F)
    return table.astype(ml_dtypes.bfloat16)


def padding_tables(facet_count):
    product = (np.arange(SG)[:, None] * np.arange(M)[None, :]) % SG
    angle = TWO_PI * product / SG
    scale = (M * math.sqrt(facet_count)) ** (-0.5)
    table = np.stack([np.cos(angle), np.sin(angle)]) * scale
    return table.astype(ml_dtypes.bfloat16)


def kernel_table():
    rows = np.arange(TV, dtype=np.float64)[:, None]
    columns = np.arange(2 * TV, dtype=np.float64)[None, :]
    distance = columns - 2.0 * rows - 1.0
    value = 0.75 * np.exp(-((distance / 1.5) ** 2))
    return np.where(np.abs(distance) <= 4.0, value, 0.0).astype(ml_dtypes.bfloat16)


def taper_square():
    position = np.arange(M, dtype=np.float64)
    taper = 0.6 + 0.4 * np.sin(math.pi * (position + 0.5) / M)
    return (taper[:, None] * taper[None, :]).astype(np.float32)


def turn_polynomials():
    nodes = 0.5 * np.cos(math.pi * (np.arange(400) + 0.5) / 800)
    square = nodes * nodes
    powers = np.stack([square**k for k in range(8)], axis=1)
    cos_c = np.linalg.lstsq(powers, np.cos(TWO_PI * nodes), rcond=None)[0]
    sin_c = np.linalg.lstsq(powers, np.sin(TWO_PI * nodes) / nodes, rcond=None)[0]
    return [float(c) for c in cos_c], [float(c) for c in sin_c]


COS_C, SIN_C = turn_polynomials()


def cos_sin_turns(turns):
    rest = turns - jnp.floor(turns + 0.5)
    square = rest * rest
    cos_v = jnp.full_like(square, COS_C[7])
    sin_v = jnp.full_like(square, SIN_C[7])
    for k in range(6, -1, -1):
        cos_v = cos_v * square + COS_C[k]
        sin_v = sin_v * square + SIN_C[k]
    return cos_v, sin_v * rest


def dot(left, right):
    return jnp.dot(left, right, preferred_element_type=F32)


def mul_left(left_r, left_i, right_r, right_i):
    left = jnp.concatenate([left_r, left_i], axis=1)
    real = dot(left, jnp.concatenate([right_r, -right_i], axis=0))
    imag = dot(left, jnp.concatenate([right_i, right_r], axis=0))
    return real, imag


def mul_right(left_r, left_i, right_r, right_i):
    right = jnp.concatenate([right_r, right_i], axis=0)
    real = dot(jnp.concatenate([left_r, -left_i], axis=1), right)
    imag = dot(jnp.concatenate([left_i, left_r], axis=1), right)
    return real, imag


def phase_taper(fo_ref):
    rows = lax.broadcasted_iota(jnp.int32, (M, M), 0)
    columns = lax.broadcasted_iota(jnp.int32, (M, M), 1)
    total = (rows * fo_ref[0, 0] + columns * fo_ref[0, 1]) & (F - 1)
    cos_v, sin_v = cos_sin_turns(total.astype(F32) * (1.0 / F))
    row = lax.broadcasted_iota(jnp.int32, (M, 1), 0).astype(F32)
    column = lax.broadcasted_iota(jnp.int32, (1, M), 1).astype(F32)
    _, row_sin = cos_sin_turns((row + 0.5) * (0.5 / M))
    _, column_sin = cos_sin_turns((column + 0.5) * (0.5 / M))
    taper2 = (0.6 + 0.4 * row_sin) * (0.6 + 0.4 * column_sin)
    return cos_v * taper2, sin_v * taper2


def owner_of(j, me):
    return (j & ~3) | ((j ^ me) & 3)


def forward_kernel(sends, me_ref, fo_ref, so_ref, facet_ref, basis_ref, *rest):
    outs, (facet_buf, basis_buf, spec_ref, sems) = rest[: len(sends)], rest[len(sends) :]
    copies = []
    for k in range(2):
        copies.append(pltpu.make_async_copy(basis_ref.at[k], basis_buf.at[k], sems.at[2 * k]))
        copies.append(pltpu.make_async_copy(facet_ref.at[0, k], facet_buf.at[k], sems.at[2 * k + 1]))
    for copy in copies:
        copy.start()
    pc, ps = phase_taper(fo_ref)
    for copy in copies:
        copy.wait()
    br, bi = basis_buf[0], basis_buf[1]
    hr, hi = mul_left(facet_buf[0], facet_buf[1], br, bi)
    spectrum = mul_right(br, bi, hr.astype(BF), hi.astype(BF))
    columns = F // M
    for plane in range(2):
        for c in range(columns):
            part = spectrum[plane][:, c * M : (c + 1) * M]
            spec_ref[plane, c, :F] = part
            spec_ref[plane, c, F:] = part[:M]
            if c == 0:
                spec_ref[plane, columns, :F] = part
                spec_ref[plane, columns, F:] = part[:M]
    me = me_ref[0]

    def block(out_ref, item, j):
        owner = owner_of(j, me)
        sx, sy = so_ref[0, owner], so_ref[1, owner]
        lane = sy // M
        shift = (2 * M - (sy & (M - 1))) & (2 * M - 1)
        parts = []
        for plane in range(2):
            left = spec_ref[plane, lane, pl.ds(sx, M), :]
            right = spec_ref[plane, lane + 1, pl.ds(sx, M), :]
            wide = jnp.concatenate([left, right], axis=1)
            parts.append(pltpu.roll(wide, shift, 1)[:, :M])
        wr, wi = parts
        out_ref[item, 0] = (pc * wr - ps * wi).astype(BF)
        out_ref[item, 1] = (pc * wi + ps * wr).astype(BF)

    for out_ref, js in zip(outs, sends):
        for_blocks(block, out_ref, js)


def for_blocks(block, ref, js):
    step = js[1] - js[0] if len(js) > 1 else 1
    if len(js) > 1 and js == list(range(js[0], js[0] + step * len(js), step)):

        def body(item, carry):
            block(ref, item, item * step + js[0])
            return carry

        lax.fori_loop(0, len(js), body, 0)
    else:
        for item, j in enumerate(js):
            block(ref, item, j)


def prepare_kernel(w_ref, to_ref, kt_ref, kwide_ref, screen_ref, kvt_ref, kv_ref, kut_ref):
    slots = kut_ref.shape[0]
    w = w_ref[0]
    row = lax.broadcasted_iota(jnp.int32, (SG, 1), 0).astype(F32) - SG / 2.0
    column = lax.broadcasted_iota(jnp.int32, (1, SG), 1).astype(F32) - SG / 2.0
    row2 = row * row * (1.0 / (SG * SG)) + 1.0
    column2 = column * column * (1.0 / (SG * SG))
    cos_v, sin_v = cos_sin_turns((jnp.sqrt(row2 + column2) - 1.0) * w)
    screen_ref[0] = cos_v
    screen_ref[1] = sin_v
    for t in range(slots):
        ou, ov = to_ref[0, t], to_ref[1, t]
        kut_ref[t] = kt_ref[pl.ds(2 * TV - ou, SG), :].astype(BF)
        kvt_ref[:, t * TV : (t + 1) * TV] = kt_ref[pl.ds(2 * TV - ov, SG), :].astype(BF)
        kv_ref[t * TV : (t + 1) * TV] = pltpu.roll(kwide_ref[...], ov, 1).astype(BF)


def subgrid_kernel(tc_ref, to_ref, got_ref, obs_ref, pad_ref, padt_ref, kern_ref, *rest):
    (screen_ref, kvt_ref, kv_ref, kut_ref) = rest[:4]
    (out_ref, coef_ref, model_ref, rows_ref, z_ref, res_ref, sems) = rest[4:]
    slots = obs_ref.shape[0]
    count = tc_ref[0]

    def total(plane):
        value = got_ref[0, plane].astype(F32)
        for item in range(1, got_ref.shape[0]):
            value = value + got_ref[item, plane].astype(F32)
        return value.astype(BF)

    pr, pi = pad_ref[0], pad_ref[1]
    inner_r, inner_i = mul_right(pr, pi, total(0), total(1))
    tr, ti = padt_ref[0], padt_ref[1]
    image_r, image_i = mul_left(inner_r.astype(BF), inner_i.astype(BF), tr, ti)
    sc, ss = screen_ref[0], screen_ref[1]
    model_ref[:SG] = (sc * image_r - ss * image_i).astype(BF)
    model_ref[SG:] = (sc * image_i + ss * image_r).astype(BF)

    model = model_ref[...]
    kern = kern_ref[...]
    copies = []
    for t0 in range(0, slots, 2):
        pair = dot(model, kvt_ref[:, t0 * TV : (t0 + 2) * TV])
        for t in (t0, t0 + 1):
            rows_ref[t % rows_ref.shape[0]] = pair[:, (t - t0) * TV : (t - t0 + 1) * TV]
        for t in (t0, t0 + 1):
            slot = t % rows_ref.shape[0]
            ou = to_ref[0, t]
            wr = rows_ref[slot, pl.ds(ou, 2 * TV), :]
            wi = rows_ref[slot, pl.ds(SG + ou, 2 * TV), :]
            window = jnp.concatenate([wr.astype(BF), wi.astype(BF)], axis=1)
            predicted = dot(kern, window)
            live = count > t
            res = []
            for plane in range(2):
                value = obs_ref[t, plane].astype(F32) - predicted[:, plane * TV : (plane + 1) * TV]
                res.append(jnp.where(live, value, 0.0).astype(BF))
                res_ref[t, plane] = res[plane]
            z = dot(kut_ref[t], jnp.concatenate(res, axis=1)).astype(BF)
            z_ref[:SG, t * TV : (t + 1) * TV] = z[:, :TV]
            z_ref[SG:, t * TV : (t + 1) * TV] = z[:, TV:]
        if t0 % 4 == 2:
            copies.append(
                pltpu.make_async_copy(
                    res_ref.at[pl.ds(t0 - 2, 4)], out_ref.at[pl.ds(t0 - 2, 4)], sems.at[t0 // 4]
                )
            )
            copies[-1].start()

    kv = kv_ref[...]
    ar = dot(z_ref[:SG], kv)
    ai = dot(z_ref[SG:], kv)
    screened_r = (sc * ar + ss * ai).astype(BF)
    screened_i = (sc * ai - ss * ar).astype(BF)
    reduced_r, reduced_i = mul_right(tr, -ti, screened_r, screened_i)
    coef_r, coef_i = mul_left(reduced_r.astype(BF), reduced_i.astype(BF), pr, -pi)
    for item in range(coef_ref.shape[0]):
        coef_ref[item, 0] = coef_r.astype(BF)
        coef_ref[item, 1] = coef_i.astype(BF)
    for copy in copies:
        copy.wait()


def grid_blocks(pieces, refs, me_ref, fo_ref, so_ref, grid_ref):
    pc, ps = phase_taper(fo_ref)
    me = me_ref[0]
    blank = jnp.zeros((M, M), F32)

    def block(in_ref, item, j):
        owner = owner_of(j, me)
        sx, sy = so_ref[0, owner], so_ref[1, owner]
        lane = sy // M
        shift = sy & (M - 1)
        cr, ci = in_ref[item, 0].astype(F32), in_ref[item, 1].astype(F32)
        values = (pc * cr + ps * ci, pc * ci - ps * cr)
        for plane in range(2):
            wide = pltpu.roll(jnp.concatenate([values[plane], blank], axis=1), shift, 1)
            grid_ref[plane, lane, pl.ds(sx, M), :] += wide[:, :M]
            grid_ref[plane, lane + 1, pl.ds(sx, M), :] += wide[:, M:]

    for in_ref, js in zip(refs, pieces):
        for_blocks(block, in_ref, js)


def first_grid_kernel(pieces, me_ref, fo_ref, so_ref, *rest):
    grid_ref = rest[-1]
    grid_ref[...] = jnp.zeros_like(grid_ref)
    grid_blocks(pieces, rest[:-1], me_ref, fo_ref, so_ref, grid_ref)


def next_grid_kernel(pieces, me_ref, fo_ref, so_ref, *rest):
    rest[-1][...] = rest[-2][...]
    grid_blocks(pieces, rest[:-2], me_ref, fo_ref, so_ref, rest[-1])


def backward_kernel(pieces, me_ref, fo_ref, so_ref, basis_ref, *rest):
    grid_ref, out_ref, _, out_buf, sems = rest[-5:]
    grid_blocks(pieces, rest[: len(pieces)], me_ref, fo_ref, so_ref, grid_ref)
    columns = F // M
    folded = []
    for plane in range(2):
        strips = []
        for c in range(columns):
            strip = grid_ref[plane, c]
            if c == 0:
                strip = strip + grid_ref[plane, columns]
            top = strip[:M] + strip[F:]
            strips.append(jnp.concatenate([top.astype(BF), strip[M:F].astype(BF)], axis=0))
        folded.append(jnp.concatenate(strips, axis=1))
    br, bi = basis_ref[0], basis_ref[1]
    hr, hi = mul_right(br, -bi, *folded)
    hr, hi = hr.astype(BF), hi.astype(BF)
    half = F // 2
    copies = []
    for k in range(2):
        rows = slice(k * half, (k + 1) * half)
        real, imag = mul_left(hr[rows], hi[rows], br, -bi)
        for plane, value in enumerate((real, imag)):
            out_buf[plane, rows] = value.astype(BF)
            copy = pltpu.make_async_copy(
                out_buf.at[plane, pl.ds(k * half, half)],
                out_ref.at[0, plane, pl.ds(k * half, half)],
                sems.at[2 * k + plane],
            )
            copy.start()
            copies.append(copy)
    for copy in copies:
        copy.wait()


SMEM = pl.BlockSpec(memory_space=pltpu.SMEM)
VMEM = pl.BlockSpec(memory_space=pltpu.VMEM)
ANY = pl.BlockSpec(memory_space=pl.ANY)


def params(mib):
    return pltpu.CompilerParams(vmem_limit_bytes=mib * 1024 * 1024)


def near(value):
    return pltpu.with_memory_space_constraint(value, pltpu.VMEM)


def far(value):
    return pltpu.with_memory_space_constraint(value, pltpu.HBM)


def held(shape, dtype=BF):
    return pltpu.VMEM(shape, dtype)


def exchange(value, mask, n):
    return lax.ppermute(value, "facet", [(i, i ^ mask) for i in range(n)])


def per_device(facets, facet_offsets, subgrid_offsets, w_terms, tile_count, tile_offsets, observed):
    n = lax.axis_size("facet")
    far_n = n // 4
    slots = observed.shape[0]
    me = lax.axis_index("facet").astype(jnp.int32).reshape(1)
    corners = far(subgrid_offsets.T)
    tile_corners = tile_offsets.T
    facet_offsets = far(facet_offsets)
    basis = jnp.asarray(basis_tables())
    pad_np = padding_tables(n)
    kern_np = kernel_table()
    kt_np = np.zeros((6 * TV, TV), np.float32)
    kt_np[2 * TV : 4 * TV] = kern_np.astype(np.float32).T
    kwide_np = np.zeros((TV, SG), np.float32)
    kwide_np[:, : 2 * TV] = kern_np.astype(np.float32)
    columns = [[high * 4 + low for high in range(far_n)] for low in range(4)]
    quarter = [[high * 4 + low for high in range(far_n)] for low in range(4)]

    own0, own1, own2, own3 = pl.pallas_call(
        functools.partial(forward_kernel, quarter),
        out_shape=[held((far_n, 2, M, M))] * 4,
        in_specs=[SMEM] * 3 + [ANY] * 2,
        out_specs=[VMEM] * 4,
        scratch_shapes=[
            pltpu.VMEM((2, F, F), BF),
            pltpu.VMEM((2, F, F), BF),
            pltpu.VMEM((2, F // M + 1, F + M, M), F32),
            pltpu.SemaphoreType.DMA((4,)),
        ],
        compiler_params=params(16),
        name="forward",
    )(me, facet_offsets, corners, far(facets), far(basis))

    screen, kvt, kv, kut = pl.pallas_call(
        prepare_kernel,
        out_shape=[
            held((2, SG, SG), F32),
            held((SG, slots * TV)),
            held((slots * TV, SG)),
            held((slots, SG, TV)),
        ],
        in_specs=[SMEM] * 2 + [VMEM] * 2,
        out_specs=[VMEM] * 4,
        compiler_params=params(8),
        name="prepare",
    )(w_terms, tile_corners, jnp.asarray(kt_np), jnp.asarray(kwide_np))

    def plus(*terms):
        return sum(term.astype(F32) for term in terms).astype(BF)

    def spread(value):
        return lax.all_to_all(value, "facet", 0, 0, axis_index_groups=columns, tiled=True)

    got3 = exchange(own3, 1, n)
    got1 = exchange(own1, 1, n)
    got2 = exchange(plus(own2, got3), 2, n)
    got = spread(plus(own0, got1, got2))

    residual, coefficients = pl.pallas_call(
        subgrid_kernel,
        out_shape=[pltpu.HBM(observed.shape, BF), held((far_n, 2, M, M))],
        in_specs=[SMEM] * 2 + [VMEM] * 9,
        out_specs=[ANY, VMEM],
        scratch_shapes=[
            pltpu.VMEM((2 * SG, SG), BF),
            pltpu.VMEM((8, 2 * SG, TV), F32),
            pltpu.VMEM((2 * SG, slots * TV), BF),
            pltpu.VMEM(observed.shape, BF),
            pltpu.SemaphoreType.DMA((slots // 4,)),
        ],
        compiler_params=params(24),
        name="subgrid",
    )(
        tile_count,
        tile_corners,
        near(got),
        near(observed),
        near(jnp.asarray(pad_np)),
        near(jnp.asarray(pad_np.transpose(0, 2, 1))),
        near(jnp.asarray(kern_np)),
        near(screen),
        near(kvt),
        near(kv),
        near(kut),
    )

    all0 = spread(coefficients)
    all2 = exchange(all0, 2, n)
    all1 = exchange(all0, 1, n)
    all3 = exchange(all2, 1, n)
    grid_shape = (2, F // M + 1, F + M, M)
    grid = pl.pallas_call(
        functools.partial(first_grid_kernel, quarter[:1]),
        out_shape=held(grid_shape, F32),
        in_specs=[SMEM] * 3 + [VMEM],
        out_specs=VMEM,
        compiler_params=params(8),
        name="grid_first",
    )(me, facet_offsets, corners, near(all0))
    grid = pl.pallas_call(
        functools.partial(next_grid_kernel, quarter[1:3]),
        out_shape=held(grid_shape, F32),
        in_specs=[SMEM] * 3 + [VMEM] * 3,
        out_specs=VMEM,
        compiler_params=params(8),
        name="grid_next",
    )(me, facet_offsets, corners, near(all1), near(all2), near(grid))
    update = pl.pallas_call(
        functools.partial(backward_kernel, quarter[3:]),
        out_shape=[pltpu.HBM(facets.shape, BF), held(grid_shape, F32)],
        in_specs=[SMEM] * 3 + [VMEM] * 3,
        out_specs=[ANY, VMEM],
        input_output_aliases={5: 1},
        scratch_shapes=[
            pltpu.VMEM((2, F, F), BF),
            pltpu.SemaphoreType.DMA((4,)),
        ],
        compiler_params=params(16),
        name="backward",
    )(me, facet_offsets, corners, near(basis), near(all3), near(grid))[0]
    return (residual, update)


def solution(mesh):
    placed = (
        P(("groups", "facet"), None, None, None),
        P(("groups", "facet"), None),
        P("groups", None),
        P(("groups", "facet")),
        P(("groups", "facet")),
        P(("groups", "facet"), None),
        P(("groups", "facet"), None, None, None),
    )
    return jax.shard_map(
        per_device,
        mesh=mesh,
        in_specs=placed,
        out_specs=(
            P(("groups", "facet"), None, None, None),
            P(("groups", "facet"), None, None, None),
        ),
        check_vma=False,
    )
```

```python
import functools
import math

import jax
import jax.numpy as jnp
import ml_dtypes
import numpy as np
from jax import lax
from jax.experimental import pallas as pl
from jax.experimental.pallas import tpu as pltpu
from jax.sharding import PartitionSpec as P

F = 512
M = 128
SG = 512
TV = 128
BF = jnp.bfloat16
F32 = jnp.float32
TWO_PI = 2.0 * math.pi


def basis_tables():
    index = np.arange(F, dtype=np.int64)
    angle = -TWO_PI * ((index[:, None] * index[None, :]) % F) / F
    table = np.stack([np.cos(angle), np.sin(angle)]) / math.sqrt(F)
    return table.astype(ml_dtypes.bfloat16)


def padding_tables(facet_count):
    product = (np.arange(SG)[:, None] * np.arange(M)[None, :]) % SG
    angle = TWO_PI * product / SG
    scale = (M * math.sqrt(facet_count)) ** (-0.5)
    table = np.stack([np.cos(angle), np.sin(angle)]) * scale
    return table.astype(ml_dtypes.bfloat16)


def kernel_table():
    rows = np.arange(TV, dtype=np.float64)[:, None]
    columns = np.arange(2 * TV, dtype=np.float64)[None, :]
    distance = columns - 2.0 * rows - 1.0
    value = 0.75 * np.exp(-((distance / 1.5) ** 2))
    return np.where(np.abs(distance) <= 4.0, value, 0.0).astype(ml_dtypes.bfloat16)


def taper_square():
    position = np.arange(M, dtype=np.float64)
    taper = 0.6 + 0.4 * np.sin(math.pi * (position + 0.5) / M)
    return (taper[:, None] * taper[None, :]).astype(np.float32)


def turn_polynomials():
    nodes = 0.5 * np.cos(math.pi * (np.arange(400) + 0.5) / 800)
    square = nodes * nodes
    powers = np.stack([square**k for k in range(8)], axis=1)
    cos_c = np.linalg.lstsq(powers, np.cos(TWO_PI * nodes), rcond=None)[0]
    sin_c = np.linalg.lstsq(powers, np.sin(TWO_PI * nodes) / nodes, rcond=None)[0]
    return [float(c) for c in cos_c], [float(c) for c in sin_c]


COS_C, SIN_C = turn_polynomials()


def cos_sin_turns(turns):
    rest = turns - jnp.floor(turns + 0.5)
    square = rest * rest
    cos_v = jnp.full_like(square, COS_C[7])
    sin_v = jnp.full_like(square, SIN_C[7])
    for k in range(6, -1, -1):
        cos_v = cos_v * square + COS_C[k]
        sin_v = sin_v * square + SIN_C[k]
    return cos_v, sin_v * rest


def dot(left, right):
    return jnp.dot(left, right, preferred_element_type=F32)


def mul_left(left_r, left_i, right_r, right_i):
    left = jnp.concatenate([left_r, left_i], axis=1)
    real = dot(left, jnp.concatenate([right_r, -right_i], axis=0))
    imag = dot(left, jnp.concatenate([right_i, right_r], axis=0))
    return real, imag


def mul_right(left_r, left_i, right_r, right_i):
    right = jnp.concatenate([right_r, right_i], axis=0)
    real = dot(jnp.concatenate([left_r, -left_i], axis=1), right)
    imag = dot(jnp.concatenate([left_i, left_r], axis=1), right)
    return real, imag


def phase_taper(fo_ref):
    rows = lax.broadcasted_iota(jnp.int32, (M, M), 0)
    columns = lax.broadcasted_iota(jnp.int32, (M, M), 1)
    total = (rows * fo_ref[0, 0] + columns * fo_ref[0, 1]) & (F - 1)
    cos_v, sin_v = cos_sin_turns(total.astype(F32) * (1.0 / F))
    row = lax.broadcasted_iota(jnp.int32, (M, 1), 0).astype(F32)
    column = lax.broadcasted_iota(jnp.int32, (1, M), 1).astype(F32)
    _, row_sin = cos_sin_turns((row + 0.5) * (0.5 / M))
    _, column_sin = cos_sin_turns((column + 0.5) * (0.5 / M))
    taper2 = (0.6 + 0.4 * row_sin) * (0.6 + 0.4 * column_sin)
    return cos_v * taper2, sin_v * taper2


def forward_kernel(js, me_ref, fo_ref, so_ref, facet_ref, basis_ref, out_ref, spec_ref, *rest):
    facet_buf, basis_buf, sems = rest
    copies = []
    for k in range(2):
        copies.append(pltpu.make_async_copy(basis_ref.at[k], basis_buf.at[k], sems.at[2 * k]))
        copies.append(pltpu.make_async_copy(facet_ref.at[0, k], facet_buf.at[k], sems.at[2 * k + 1]))
    for copy in copies:
        copy.start()
    for copy in copies:
        copy.wait()
    br, bi = basis_buf[0], basis_buf[1]
    hr, hi = mul_left(facet_buf[0], facet_buf[1], br, bi)
    spectrum = mul_right(br, bi, hr.astype(BF), hi.astype(BF))
    columns = F // M
    for plane in range(2):
        for c in range(columns):
            part = spectrum[plane][:, c * M : (c + 1) * M]
            spec_ref[plane, c, :F] = part
            spec_ref[plane, c, F:] = part[:M]
            if c == 0:
                spec_ref[plane, columns, :F] = part
                spec_ref[plane, columns, F:] = part[:M]
    extract([js], [out_ref], me_ref, fo_ref, so_ref, spec_ref)


def extract_kernel(sends, me_ref, fo_ref, so_ref, spec_ref, *outs):
    extract(sends, outs, me_ref, fo_ref, so_ref, spec_ref)


def extract(sends, outs, me_ref, fo_ref, so_ref, spec_ref):
    pc, ps = phase_taper(fo_ref)
    me = me_ref[0]

    def block(out_ref, item, j):
        owner = j ^ me
        sx, sy = so_ref[0, owner], so_ref[1, owner]
        lane = sy // M
        shift = (2 * M - (sy & (M - 1))) & (2 * M - 1)
        parts = []
        for plane in range(2):
            left = spec_ref[plane, lane, pl.ds(sx, M), :]
            right = spec_ref[plane, lane + 1, pl.ds(sx, M), :]
            wide = jnp.concatenate([left, right], axis=1)
            parts.append(pltpu.roll(wide, shift, 1)[:, :M])
        wr, wi = parts
        out_ref[item, 0] = (pc * wr - ps * wi).astype(BF)
        out_ref[item, 1] = (pc * wi + ps * wr).astype(BF)

    for out_ref, js in zip(outs, sends):
        for_blocks(block, out_ref, js)


def for_blocks(block, ref, js):
    step = js[1] - js[0] if len(js) > 1 else 1
    if len(js) > 1 and js == list(range(js[0], js[0] + step * len(js), step)):

        def body(item, carry):
            block(ref, item, item * step + js[0])
            return carry

        lax.fori_loop(0, len(js), body, 0)
    else:
        for item, j in enumerate(js):
            block(ref, item, j)


def prepare_kernel(w_ref, to_ref, _, *rest):
    loads = (len(rest) - 6) // 2
    sources, (screen_ref, kvt_ref, kv_ref, kut_ref) = rest[:loads], rest[loads : loads + 4]
    targets, zero_ref, sems = rest[loads + 4 : -2], rest[-2], rest[-1]
    zero_ref[...] = jnp.zeros_like(zero_ref)
    kt_ref, kwide_ref = targets[-2:]
    copies = []
    for k in range(loads - 1, -1, -1):
        copies.append(pltpu.make_async_copy(sources[k], targets[k], sems.at[k]))
        copies[-1].start()
    slots = kut_ref.shape[0]
    w = w_ref[0, 0]
    row = lax.broadcasted_iota(jnp.int32, (SG, 1), 0).astype(F32) - SG / 2.0
    column = lax.broadcasted_iota(jnp.int32, (1, SG), 1).astype(F32) - SG / 2.0
    row2 = row * row * (1.0 / (SG * SG)) + 1.0
    column2 = column * column * (1.0 / (SG * SG))
    cos_v, sin_v = cos_sin_turns((jnp.sqrt(row2 + column2) - 1.0) * w)
    screen_ref[0] = cos_v
    screen_ref[1] = sin_v
    for copy in copies:
        copy.wait()
    for t in range(slots):
        ou, ov = to_ref[0, t], to_ref[1, t]
        kut_ref[t] = kt_ref[pl.ds(2 * TV - ou, SG), :].astype(BF)
        kvt_ref[:, t * TV : (t + 1) * TV] = kt_ref[pl.ds(2 * TV - ov, SG), :].astype(BF)
        kv_ref[t * TV : (t + 1) * TV] = pltpu.roll(kwide_ref[...], ov, 1).astype(BF)


def subgrid_kernel(picks, tc_ref, to_ref, *rest):
    parts = len(picks)
    sums = rest[:parts]
    (obs_ref, pad_ref, padt_ref, kern_ref, screen_ref, kvt_ref, kv_ref, kut_ref) = rest[parts : parts + 8]
    (out_ref, coef_ref, model_ref, rows_ref, z_ref, res_ref, sems) = rest[parts + 8 :]
    slots = obs_ref.shape[0]
    count = tc_ref[0, 0]

    def total(plane):
        value = sums[0][picks[0], plane].astype(F32)
        for ref, item in zip(sums[1:], picks[1:]):
            value = value + ref[item, plane].astype(F32)
        return value.astype(BF)

    pr, pi = pad_ref[0], pad_ref[1]
    inner_r, inner_i = mul_right(pr, pi, total(0), total(1))
    tr, ti = padt_ref[0], padt_ref[1]
    image_r, image_i = mul_left(inner_r.astype(BF), inner_i.astype(BF), tr, ti)
    sc, ss = screen_ref[0], screen_ref[1]
    model_ref[:SG] = (sc * image_r - ss * image_i).astype(BF)
    model_ref[SG:] = (sc * image_i + ss * image_r).astype(BF)

    model = model_ref[...]
    kern = kern_ref[...]
    copies = []
    for t0 in range(0, slots, 2):
        pair = dot(model, kvt_ref[:, t0 * TV : (t0 + 2) * TV])
        for t in (t0, t0 + 1):
            rows_ref[t % rows_ref.shape[0]] = pair[:, (t - t0) * TV : (t - t0 + 1) * TV]
        for t in (t0, t0 + 1):
            slot = t % rows_ref.shape[0]
            ou = to_ref[0, t]
            wr = rows_ref[slot, pl.ds(ou, 2 * TV), :]
            wi = rows_ref[slot, pl.ds(SG + ou, 2 * TV), :]
            window = jnp.concatenate([wr.astype(BF), wi.astype(BF)], axis=1)
            predicted = dot(kern, window)
            live = count > t
            res = []
            for plane in range(2):
                value = obs_ref[t, plane].astype(F32) - predicted[:, plane * TV : (plane + 1) * TV]
                res.append(jnp.where(live, value, 0.0).astype(BF))
                res_ref[t, plane] = res[plane]
            z = dot(kut_ref[t], jnp.concatenate(res, axis=1)).astype(BF)
            z_ref[:SG, t * TV : (t + 1) * TV] = z[:, :TV]
            z_ref[SG:, t * TV : (t + 1) * TV] = z[:, TV:]
        if t0 % 4 == 2:
            copies.append(
                pltpu.make_async_copy(
                    res_ref.at[pl.ds(t0 - 2, 4)], out_ref.at[pl.ds(t0 - 2, 4)], sems.at[t0 // 4]
                )
            )
            copies[-1].start()

    kv = kv_ref[...]
    ar = dot(z_ref[:SG], kv)
    ai = dot(z_ref[SG:], kv)
    screened_r = (sc * ar + ss * ai).astype(BF)
    screened_i = (sc * ai - ss * ar).astype(BF)
    reduced_r, reduced_i = mul_right(tr, -ti, screened_r, screened_i)
    coef_r, coef_i = mul_left(reduced_r.astype(BF), reduced_i.astype(BF), pr, -pi)
    coef_ref[0, 0] = coef_r.astype(BF)
    coef_ref[0, 1] = coef_i.astype(BF)
    for copy in copies:
        copy.wait()


def grid_blocks(pieces, refs, me_ref, fo_ref, so_ref, grid_ref):
    pc, ps = phase_taper(fo_ref)
    me = me_ref[0]
    blank = jnp.zeros((M, M), F32)

    def block(in_ref, item, j):
        owner = j ^ me
        sx, sy = so_ref[0, owner], so_ref[1, owner]
        lane = sy // M
        shift = sy & (M - 1)
        cr, ci = in_ref[item, 0].astype(F32), in_ref[item, 1].astype(F32)
        values = (pc * cr + ps * ci, pc * ci - ps * cr)
        for plane in range(2):
            wide = pltpu.roll(jnp.concatenate([values[plane], blank], axis=1), shift, 1)
            grid_ref[plane, lane, pl.ds(sx, M), :] += wide[:, :M]
            grid_ref[plane, lane + 1, pl.ds(sx, M), :] += wide[:, M:]

    for in_ref, js in zip(refs, pieces):
        for_blocks(block, in_ref, js)


def first_grid_kernel(pieces, me_ref, fo_ref, so_ref, *rest):
    grid_ref = rest[-1]
    grid_ref[...] = jnp.zeros_like(grid_ref)
    grid_blocks(pieces, rest[:-1], me_ref, fo_ref, so_ref, grid_ref)


def next_grid_kernel(pieces, me_ref, fo_ref, so_ref, *rest):
    rest[-1][...] = rest[-2][...]
    grid_blocks(pieces, rest[:-2], me_ref, fo_ref, so_ref, rest[-1])


def backward_kernel(pieces, me_ref, fo_ref, so_ref, basis_hbm, *rest):
    grid_ref, out_ref, _, basis_ref, out_buf, sems = rest[len(pieces) :]
    load = pltpu.make_async_copy(basis_hbm, basis_ref, sems.at[4])
    load.start()
    grid_blocks(pieces, rest[: len(pieces)], me_ref, fo_ref, so_ref, grid_ref)
    columns = F // M
    folded = []
    for plane in range(2):
        strips = []
        for c in range(columns):
            strip = grid_ref[plane, c]
            if c == 0:
                strip = strip + grid_ref[plane, columns]
            top = strip[:M] + strip[F:]
            strips.append(jnp.concatenate([top.astype(BF), strip[M:F].astype(BF)], axis=0))
        folded.append(jnp.concatenate(strips, axis=1))
    load.wait()
    br, bi = basis_ref[0], basis_ref[1]
    hr, hi = mul_right(br, -bi, *folded)
    hr, hi = hr.astype(BF), hi.astype(BF)
    half = F // 2
    copies = []
    for k in range(2):
        rows = slice(k * half, (k + 1) * half)
        real, imag = mul_left(hr[rows], hi[rows], br, -bi)
        for plane, value in enumerate((real, imag)):
            out_buf[plane, rows] = value.astype(BF)
            copy = pltpu.make_async_copy(
                out_buf.at[plane, pl.ds(k * half, half)],
                out_ref.at[0, plane, pl.ds(k * half, half)],
                sems.at[2 * k + plane],
            )
            copy.start()
            copies.append(copy)
    for copy in copies:
        copy.wait()


SMEM = pl.BlockSpec(memory_space=pltpu.SMEM)
VMEM = pl.BlockSpec(memory_space=pltpu.VMEM)
ANY = pl.BlockSpec(memory_space=pl.ANY)


def params(mib):
    return pltpu.CompilerParams(vmem_limit_bytes=mib * 1024 * 1024)


def near(value):
    return pltpu.with_memory_space_constraint(value, pltpu.VMEM)


def far(value):
    return pltpu.with_memory_space_constraint(value, pltpu.HBM)


def held(shape, dtype=BF):
    return pltpu.VMEM(shape, dtype)


def exchange(value, mask, n):
    return lax.ppermute(value, "facet", [(i, i ^ mask) for i in range(n)])


def digit_levels(n):
    levels, base = [], 1
    while base < n:
        radix = 2 if base < 4 or n // base < 4 else 4
        levels.append((base, radix))
        base *= radix
    return levels


def reduce_sends(n):
    levels = digit_levels(n)
    sends = []
    for k, (base, radix) in enumerate(levels):
        for g in range(1, radix):
            js = [j for j in range(0, n, base) if (j // base) % radix == g]
            if k + 1 < len(levels):
                after, width = levels[k + 1]
                groups = [[j for j in js if (j // after) % width], [j for j in js if not (j // after) % width]]
            else:
                groups = [js]
            sends += [(group, g * base) for group in groups if group]
    return sends


def pick(value, items):
    step = items[1] - items[0] if len(items) > 1 else 1
    if items == list(range(items[0], items[0] + step * len(items), step)):
        if len(items) == value.shape[0]:
            return value
        return lax.slice_in_dim(value, items[0], items[-1] + 1, step)
    return jnp.concatenate([value[i : i + 1] for i in items])


def join(pieces):
    return [j for js, _ in pieces for j in js], jnp.concatenate([value for _, value in pieces])


def per_device(facets, facet_offsets, subgrid_offsets, w_terms, tile_count, tile_offsets, observed):
    n = lax.axis_size("facet")
    slots = observed.shape[0]
    me = lax.axis_index("facet").astype(jnp.int32).reshape(1)
    corners = far(subgrid_offsets.T)
    tile_corners = far(tile_offsets.T)
    facet_offsets = far(facet_offsets)
    basis = far(jnp.asarray(basis_tables()))
    pad_np = padding_tables(n)
    kern_np = kernel_table()
    kt_np = np.zeros((6 * TV, TV), np.float32)
    kt_np[2 * TV : 4 * TV] = kern_np.astype(np.float32).T
    kwide_np = np.zeros((TV, SG), np.float32)
    kwide_np[:, : 2 * TV] = kern_np.astype(np.float32)
    grid_shape = (2, F // M + 1, F + M, M)

    sends = reduce_sends(n)
    first, spec = pl.pallas_call(
        functools.partial(forward_kernel, sends[0][0]),
        out_shape=[held((len(sends[0][0]), 2, M, M)), held(grid_shape, F32)],
        in_specs=[SMEM] * 3 + [ANY] * 2,
        out_specs=[VMEM] * 2,
        scratch_shapes=[
            pltpu.VMEM((2, F, F), BF),
            pltpu.VMEM((2, F, F), BF),
            pltpu.SemaphoreType.DMA((4,)),
        ],
        compiler_params=params(16),
        name="forward",
    )(me, facet_offsets, corners, far(facets), basis)
    lists = [js for js, _ in sends[1:]] + [[0]]
    own = pl.pallas_call(
        functools.partial(extract_kernel, lists),
        out_shape=[held((len(js), 2, M, M)) for js in lists],
        in_specs=[SMEM] * 3 + [VMEM],
        out_specs=[VMEM] * len(lists),
        compiler_params=params(8),
        name="extract",
    )(me, facet_offsets, corners, near(spec))

    arrived = []
    for (js, mask), value in zip(sends, [first] + list(own)):
        terms = []
        for got_js, got in arrived:
            if set(js) <= set(got_js):
                terms.append(pick(got, [got_js.index(j) for j in js]))
            else:
                assert not set(js) & set(got_js)
        if terms:
            total = value.astype(F32)
            if mask > 2:
                total = total + prepared[-1]
            for term in terms:
                total = total + term.astype(F32)
            value = total.astype(BF)
        if mask == 2 and len(js) > 1:
            loads = [observed, pad_np, pad_np.transpose(0, 2, 1), kern_np, kt_np, kwide_np]
            prepared = pl.pallas_call(
                prepare_kernel,
                out_shape=[
                    held((2, SG, SG), F32),
                    held((SG, slots * TV)),
                    held((slots * TV, SG)),
                    held((slots, SG, TV)),
                ]
                + [held(load.shape, load.dtype) for load in loads]
                + [held((1, M), F32)],
                in_specs=[SMEM] * 2 + [VMEM] + [ANY] * len(loads),
                out_specs=[VMEM] * (5 + len(loads)),
                scratch_shapes=[pltpu.SemaphoreType.DMA((len(loads),))],
                compiler_params=params(8),
                name="prepare",
            )(w_terms.reshape(1, 1), tile_corners, near(value), *[far(jnp.asarray(load)) for load in loads])
        got = exchange(value, mask, n)
        arrived.append(([j ^ mask for j in js], got))
    last = [(js, got) for js, got in arrived if 0 in js]
    screen, kvt, kv, kut, tiles, pad, padt, kern = prepared[:8]

    residual, coefficient = pl.pallas_call(
        functools.partial(subgrid_kernel, [0] + [js.index(0) for js, _ in last]),
        out_shape=[pltpu.HBM(observed.shape, BF), held((1, 2, M, M))],
        in_specs=[SMEM] * 2 + [VMEM] * (len(last) + 9),
        out_specs=[ANY, VMEM],
        scratch_shapes=[
            pltpu.VMEM((2 * SG, SG), BF),
            pltpu.VMEM((8, 2 * SG, TV), F32),
            pltpu.VMEM((2 * SG, slots * TV), BF),
            pltpu.VMEM(observed.shape, BF),
            pltpu.SemaphoreType.DMA((slots // 4,)),
        ],
        compiler_params=params(24),
        name="subgrid",
    )(
        tile_count.reshape(1, 1),
        tile_corners,
        near(own[-1]),
        *[near(got) for _, got in last],
        *[near(value) for value in (tiles, pad, padt, kern, screen, kvt, kv, kut)],
    )

    mine = ([0], coefficient)
    beside = ([2], exchange(coefficient, 2, n))
    along = []
    for base, radix in reversed(digit_levels(n)[2:]):
        js, value = join([mine] + along) if along else mine
        along.append(
            join([([j ^ (g * base) for j in js], exchange(value, g * base, n)) for g in range(1, radix)])
        )
    along = join(along) if len(along) > 1 else along[0]
    early = join([mine, along, beside])
    early_other = ([j ^ 1 for j in early[0]], exchange(early[1], 1, n))
    late_js, late_value = [j ^ 2 for j in along[0]], exchange(along[1], 2, n)
    grid = pl.pallas_call(
        functools.partial(first_grid_kernel, [early[0], early_other[0]]),
        out_shape=held(grid_shape, F32),
        in_specs=[SMEM] * 3 + [VMEM] * 2,
        out_specs=VMEM,
        compiler_params=params(8),
        name="grid_first",
    )(me, facet_offsets, corners, near(early[1]), near(early_other[1]))
    late_other = ([j ^ 1 for j in late_js], exchange(late_value, 1, n))
    grid = pl.pallas_call(
        functools.partial(next_grid_kernel, [late_js]),
        out_shape=held(grid_shape, F32),
        in_specs=[SMEM] * 3 + [VMEM] * 2,
        out_specs=VMEM,
        compiler_params=params(8),
        name="grid_next",
    )(me, facet_offsets, corners, near(late_value), near(grid))
    update = pl.pallas_call(
        functools.partial(backward_kernel, [late_other[0]]),
        out_shape=[pltpu.HBM(facets.shape, BF), held(grid_shape, F32)],
        in_specs=[SMEM] * 3 + [ANY] + [VMEM] * 2,
        out_specs=[ANY, VMEM],
        input_output_aliases={5: 1},
        scratch_shapes=[
            pltpu.VMEM((2, F, F), BF),
            pltpu.VMEM((2, F, F), BF),
            pltpu.SemaphoreType.DMA((5,)),
        ],
        compiler_params=params(16),
        name="backward",
    )(me, facet_offsets, corners, basis, near(late_other[1]), near(grid))[0]
    return (residual, update)


def solution(mesh):
    placed = (
        P(("groups", "facet"), None, None, None),
        P(("groups", "facet"), None),
        P("groups", None),
        P(("groups", "facet")),
        P(("groups", "facet")),
        P(("groups", "facet"), None),
        P(("groups", "facet"), None, None, None),
    )
    return jax.shard_map(
        per_device,
        mesh=mesh,
        in_specs=placed,
        out_specs=(
            P(("groups", "facet"), None, None, None),
            P(("groups", "facet"), None, None, None),
        ),
        check_vma=False,
    )
```

```python
import functools
import math

import jax
import jax.numpy as jnp
import ml_dtypes
import numpy as np
from jax import lax
from jax.experimental import pallas as pl
from jax.experimental.pallas import tpu as pltpu
from jax.sharding import PartitionSpec as P

F = 512
M = 128
SG = 512
TV = 128
BF = jnp.bfloat16
F32 = jnp.float32
TWO_PI = 2.0 * math.pi


def basis_tables():
    index = np.arange(F, dtype=np.int64)
    angle = -TWO_PI * ((index[:, None] * index[None, :]) % F) / F
    table = np.stack([np.cos(angle), np.sin(angle)]) / math.sqrt(F)
    return table.astype(ml_dtypes.bfloat16)


def padding_tables(facet_count):
    product = (np.arange(SG)[:, None] * np.arange(M)[None, :]) % SG
    angle = TWO_PI * product / SG
    scale = (M * math.sqrt(facet_count)) ** (-0.5)
    table = np.stack([np.cos(angle), np.sin(angle)]) * scale
    return table.astype(ml_dtypes.bfloat16)


def kernel_table():
    rows = np.arange(TV, dtype=np.float64)[:, None]
    columns = np.arange(2 * TV, dtype=np.float64)[None, :]
    distance = columns - 2.0 * rows - 1.0
    value = 0.75 * np.exp(-((distance / 1.5) ** 2))
    return np.where(np.abs(distance) <= 4.0, value, 0.0).astype(ml_dtypes.bfloat16)


def taper_square():
    position = np.arange(M, dtype=np.float64)
    taper = 0.6 + 0.4 * np.sin(math.pi * (position + 0.5) / M)
    return (taper[:, None] * taper[None, :]).astype(np.float32)


def turn_polynomials():
    nodes = 0.5 * np.cos(math.pi * (np.arange(400) + 0.5) / 800)
    square = nodes * nodes
    powers = np.stack([square**k for k in range(8)], axis=1)
    cos_c = np.linalg.lstsq(powers, np.cos(TWO_PI * nodes), rcond=None)[0]
    sin_c = np.linalg.lstsq(powers, np.sin(TWO_PI * nodes) / nodes, rcond=None)[0]
    return [float(c) for c in cos_c], [float(c) for c in sin_c]


COS_C, SIN_C = turn_polynomials()


def cos_sin_turns(turns):
    rest = turns - jnp.floor(turns + 0.5)
    square = rest * rest
    cos_v = jnp.full_like(square, COS_C[7])
    sin_v = jnp.full_like(square, SIN_C[7])
    for k in range(6, -1, -1):
        cos_v = cos_v * square + COS_C[k]
        sin_v = sin_v * square + SIN_C[k]
    return cos_v, sin_v * rest


def dot(left, right):
    return jnp.dot(left, right, preferred_element_type=F32)


def mul_left(left_r, left_i, right_r, right_i):
    left = jnp.concatenate([left_r, left_i], axis=1)
    real = dot(left, jnp.concatenate([right_r, -right_i], axis=0))
    imag = dot(left, jnp.concatenate([right_i, right_r], axis=0))
    return real, imag


def mul_right(left_r, left_i, right_r, right_i):
    right = jnp.concatenate([right_r, right_i], axis=0)
    real = dot(jnp.concatenate([left_r, -left_i], axis=1), right)
    imag = dot(jnp.concatenate([left_i, left_r], axis=1), right)
    return real, imag


def phase_taper(fo_ref):
    rows = lax.broadcasted_iota(jnp.int32, (M, M), 0)
    columns = lax.broadcasted_iota(jnp.int32, (M, M), 1)
    total = (rows * fo_ref[0, 0] + columns * fo_ref[0, 1]) & (F - 1)
    cos_v, sin_v = cos_sin_turns(total.astype(F32) * (1.0 / F))
    row = lax.broadcasted_iota(jnp.int32, (M, 1), 0).astype(F32)
    column = lax.broadcasted_iota(jnp.int32, (1, M), 1).astype(F32)
    _, row_sin = cos_sin_turns((row + 0.5) * (0.5 / M))
    _, column_sin = cos_sin_turns((column + 0.5) * (0.5 / M))
    taper2 = (0.6 + 0.4 * row_sin) * (0.6 + 0.4 * column_sin)
    return cos_v * taper2, sin_v * taper2


def step_mask(n, step, odd):
    last = 4 << step >= n
    return 2 << step if not odd else (2 if last else 4 << step)


def position_of(label, other, me, n):
    who = me ^ other
    top = n.bit_length() - 3
    even = label << 1
    odd = ((label << 2) & (n - 1)) | ((label >> top) << 1)
    return who ^ jnp.where((who & 1) == 1, odd, even)


def forward_kernel(n, labels, me_ref, fo_ref, so_ref, facet_ref, basis_ref, out_ref, spec_ref, *rest):
    facet_buf, basis_buf, sems = rest
    copies = []
    for k in range(2):
        copies.append(pltpu.make_async_copy(basis_ref.at[k], basis_buf.at[k], sems.at[2 * k]))
        copies.append(pltpu.make_async_copy(facet_ref.at[0, k], facet_buf.at[k], sems.at[2 * k + 1]))
    for copy in copies:
        copy.start()
    for copy in copies:
        copy.wait()
    br, bi = basis_buf[0], basis_buf[1]
    hr, hi = mul_left(facet_buf[0], facet_buf[1], br, bi)
    spectrum = mul_right(br, bi, hr.astype(BF), hi.astype(BF))
    columns = F // M
    for plane in range(2):
        for c in range(columns):
            part = spectrum[plane][:, c * M : (c + 1) * M]
            spec_ref[plane, c, :F] = part
            spec_ref[plane, c, F:] = part[:M]
            if c == 0:
                spec_ref[plane, columns, :F] = part
                spec_ref[plane, columns, F:] = part[:M]
    extract(n, [labels], [out_ref], me_ref, fo_ref, so_ref, spec_ref)


def extract_kernel(n, sends, me_ref, fo_ref, so_ref, spec_ref, *outs):
    extract(n, sends, outs, me_ref, fo_ref, so_ref, spec_ref)


def extract(n, sends, outs, me_ref, fo_ref, so_ref, spec_ref):
    pc, ps = phase_taper(fo_ref)
    me = me_ref[0]

    def block(out_ref, item, label, other):
        owner = position_of(label, other, me, n)
        sx, sy = so_ref[0, owner], so_ref[1, owner]
        lane = sy // M
        shift = (2 * M - (sy & (M - 1))) & (2 * M - 1)
        parts = []
        for plane in range(2):
            left = spec_ref[plane, lane, pl.ds(sx, M), :]
            right = spec_ref[plane, lane + 1, pl.ds(sx, M), :]
            wide = jnp.concatenate([left, right], axis=1)
            parts.append(pltpu.roll(wide, shift, 1)[:, :M])
        wr, wi = parts
        out_ref[item, 0] = (pc * wr - ps * wi).astype(BF)
        out_ref[item, 1] = (pc * wi + ps * wr).astype(BF)

    for out_ref, labels in zip(outs, sends):
        for_blocks(block, out_ref, labels)


def for_blocks(block, ref, labels):
    js, other = labels
    step = js[1] - js[0] if len(js) > 1 else 1
    if len(js) > 1 and js == list(range(js[0], js[0] + step * len(js), step)):

        def body(item, carry):
            block(ref, item, item * step + js[0], other)
            return carry

        lax.fori_loop(0, len(js), body, 0)
    else:
        for item, j in enumerate(js):
            block(ref, item, j, other)


def band_kernel(to_ref, _, kt_hbm, kwide_hbm, kvt_ref, kv_ref, kut_ref, zero_ref, kt_ref, kwide_ref, sems):
    slots = kut_ref.shape[0]
    copies = [
        pltpu.make_async_copy(kt_hbm, kt_ref, sems.at[0]),
        pltpu.make_async_copy(kwide_hbm, kwide_ref, sems.at[1]),
    ]
    for copy in copies:
        copy.start()
    zero_ref[...] = jnp.zeros_like(zero_ref)
    for copy in copies:
        copy.wait()
    for t in range(slots):
        ou, ov = to_ref[0, t], to_ref[1, t]
        kut_ref[t] = kt_ref[pl.ds(2 * TV - ou, SG), :].astype(BF)
        kvt_ref[:, t * TV : (t + 1) * TV] = kt_ref[pl.ds(2 * TV - ov, SG), :].astype(BF)
        kv_ref[t * TV : (t + 1) * TV] = pltpu.roll(kwide_ref[...], ov, 1).astype(BF)


def screen_kernel(w_ref, _, *rest):
    loads = (len(rest) - 3) // 2
    sources, screen_ref = rest[:loads], rest[loads]
    targets, zero_ref, sems = rest[loads + 1 : -2], rest[-2], rest[-1]
    copies = [pltpu.make_async_copy(sources[k], targets[k], sems.at[k]) for k in range(loads)]
    for copy in copies:
        copy.start()
    zero_ref[...] = jnp.zeros_like(zero_ref)
    w = w_ref[0, 0]
    row = lax.broadcasted_iota(jnp.int32, (SG, 1), 0).astype(F32) - SG / 2.0
    column = lax.broadcasted_iota(jnp.int32, (1, SG), 1).astype(F32) - SG / 2.0
    row2 = row * row * (1.0 / (SG * SG)) + 1.0
    column2 = column * column * (1.0 / (SG * SG))
    cos_v, sin_v = cos_sin_turns((jnp.sqrt(row2 + column2) - 1.0) * w)
    screen_ref[0] = cos_v
    screen_ref[1] = sin_v
    for copy in copies:
        copy.wait()


def subgrid_kernel(picks, tc_ref, to_ref, *rest):
    parts = len(picks)
    sums = rest[:parts]
    (obs_ref, pad_ref, padt_ref, kern_ref, screen_ref, kvt_ref, kv_ref, kut_ref) = rest[parts : parts + 8]
    (out_ref, coef_ref, model_ref, rows_ref, z_ref, res_ref, sems) = rest[parts + 8 :]
    slots = obs_ref.shape[0]
    count = tc_ref[0, 0]

    def total(plane):
        value = sums[0][picks[0], plane].astype(F32)
        for ref, item in zip(sums[1:], picks[1:]):
            value = value + ref[item, plane].astype(F32)
        return value.astype(BF)

    pr, pi = pad_ref[0], pad_ref[1]
    inner_r, inner_i = mul_right(pr, pi, total(0), total(1))
    tr, ti = padt_ref[0], padt_ref[1]
    image_r, image_i = mul_left(inner_r.astype(BF), inner_i.astype(BF), tr, ti)
    sc, ss = screen_ref[0], screen_ref[1]
    model_ref[:SG] = (sc * image_r - ss * image_i).astype(BF)
    model_ref[SG:] = (sc * image_i + ss * image_r).astype(BF)

    model = model_ref[...]
    kern = kern_ref[...]
    copies = []
    for t0 in range(0, slots, 2):
        pair = dot(model, kvt_ref[:, t0 * TV : (t0 + 2) * TV])
        for t in (t0, t0 + 1):
            rows_ref[t % rows_ref.shape[0]] = pair[:, (t - t0) * TV : (t - t0 + 1) * TV]
        for t in (t0, t0 + 1):
            slot = t % rows_ref.shape[0]
            ou = to_ref[0, t]
            wr = rows_ref[slot, pl.ds(ou, 2 * TV), :]
            wi = rows_ref[slot, pl.ds(SG + ou, 2 * TV), :]
            window = jnp.concatenate([wr.astype(BF), wi.astype(BF)], axis=1)
            predicted = dot(kern, window)
            live = count > t
            res = []
            for plane in range(2):
                value = obs_ref[t, plane].astype(F32) - predicted[:, plane * TV : (plane + 1) * TV]
                res.append(jnp.where(live, value, 0.0).astype(BF))
                res_ref[t, plane] = res[plane]
            z = dot(kut_ref[t], jnp.concatenate(res, axis=1)).astype(BF)
            z_ref[:SG, t * TV : (t + 1) * TV] = z[:, :TV]
            z_ref[SG:, t * TV : (t + 1) * TV] = z[:, TV:]
        if t0 % 4 == 2:
            copies.append(
                pltpu.make_async_copy(
                    res_ref.at[pl.ds(t0 - 2, 4)], out_ref.at[pl.ds(t0 - 2, 4)], sems.at[t0 // 4]
                )
            )
            copies[-1].start()

    kv = kv_ref[...]
    ar = dot(z_ref[:SG], kv)
    ai = dot(z_ref[SG:], kv)
    screened_r = (sc * ar + ss * ai).astype(BF)
    screened_i = (sc * ai - ss * ar).astype(BF)
    reduced_r, reduced_i = mul_right(tr, -ti, screened_r, screened_i)
    coef_r, coef_i = mul_left(reduced_r.astype(BF), reduced_i.astype(BF), pr, -pi)
    coef_ref[0, 0] = coef_r.astype(BF)
    coef_ref[0, 1] = coef_i.astype(BF)
    for copy in copies:
        copy.wait()


def grid_blocks(n, pieces, refs, me_ref, fo_ref, so_ref, grid_ref):
    pc, ps = phase_taper(fo_ref)
    me = me_ref[0]
    blank = jnp.zeros((M, M), F32)

    def block(in_ref, item, label, other):
        owner = position_of(label, other, me, n)
        sx, sy = so_ref[0, owner], so_ref[1, owner]
        lane = sy // M
        shift = sy & (M - 1)
        cr, ci = in_ref[item, 0].astype(F32), in_ref[item, 1].astype(F32)
        values = (pc * cr + ps * ci, pc * ci - ps * cr)
        for plane in range(2):
            wide = pltpu.roll(jnp.concatenate([values[plane], blank], axis=1), shift, 1)
            grid_ref[plane, lane, pl.ds(sx, M), :] += wide[:, :M]
            grid_ref[plane, lane + 1, pl.ds(sx, M), :] += wide[:, M:]

    for in_ref, labels in zip(refs, pieces):
        for_blocks(block, in_ref, labels)


def first_grid_kernel(n, pieces, me_ref, fo_ref, so_ref, *rest):
    grid_ref, zero_ref = rest[-2:]
    zero_ref[...] = jnp.zeros_like(zero_ref)
    grid_ref[...] = jnp.zeros_like(grid_ref)
    grid_blocks(n, pieces, rest[:-2], me_ref, fo_ref, so_ref, grid_ref)


def next_grid_kernel(n, pieces, me_ref, fo_ref, so_ref, *rest):
    rest[-1][...] = rest[-2][...]
    grid_blocks(n, pieces, rest[:-2], me_ref, fo_ref, so_ref, rest[-1])


def backward_kernel(n, pieces, me_ref, fo_ref, so_ref, basis_hbm, *rest):
    grid_ref, out_ref, _, basis_ref, out_buf, sems = rest[len(pieces) :]
    load = pltpu.make_async_copy(basis_hbm, basis_ref, sems.at[4])
    load.start()
    grid_blocks(n, pieces, rest[: len(pieces)], me_ref, fo_ref, so_ref, grid_ref)
    columns = F // M
    folded = []
    for plane in range(2):
        strips = []
        for c in range(columns):
            strip = grid_ref[plane, c]
            if c == 0:
                strip = strip + grid_ref[plane, columns]
            top = strip[:M] + strip[F:]
            strips.append(jnp.concatenate([top.astype(BF), strip[M:F].astype(BF)], axis=0))
        folded.append(jnp.concatenate(strips, axis=1))
    load.wait()
    br, bi = basis_ref[0], basis_ref[1]
    hr, hi = mul_right(br, -bi, *folded)
    hr, hi = hr.astype(BF), hi.astype(BF)
    half = F // 2
    copies = []
    for k in range(2):
        rows = slice(k * half, (k + 1) * half)
        real, imag = mul_left(hr[rows], hi[rows], br, -bi)
        for plane, value in enumerate((real, imag)):
            out_buf[plane, rows] = value.astype(BF)
            copy = pltpu.make_async_copy(
                out_buf.at[plane, pl.ds(k * half, half)],
                out_ref.at[0, plane, pl.ds(k * half, half)],
                sems.at[2 * k + plane],
            )
            copy.start()
            copies.append(copy)
    for copy in copies:
        copy.wait()


SMEM = pl.BlockSpec(memory_space=pltpu.SMEM)
VMEM = pl.BlockSpec(memory_space=pltpu.VMEM)
ANY = pl.BlockSpec(memory_space=pl.ANY)


def params(mib):
    return pltpu.CompilerParams(vmem_limit_bytes=mib * 1024 * 1024)


def near(value):
    return pltpu.with_memory_space_constraint(value, pltpu.VMEM)


def far(value):
    return pltpu.with_memory_space_constraint(value, pltpu.HBM)


def held(shape, dtype=BF):
    return pltpu.VMEM(shape, dtype)


def exchange(value, step, n):
    masks = [1, 1] if step < 0 else [step_mask(n, step, odd) for odd in (0, 1)]
    return lax.ppermute(value, "facet", [(i, i ^ masks[i & 1]) for i in range(n)])


def pick(value, items):
    step = items[1] - items[0] if len(items) > 1 else 1
    if items == list(range(items[0], items[0] + step * len(items), step)):
        if len(items) == value.shape[0]:
            return value
        return lax.slice_in_dim(value, items[0], items[-1] + 1, step)
    return jnp.concatenate([value[i : i + 1] for i in items])


def join(pieces):
    return [j for js, _ in pieces for j in js], jnp.concatenate([value for _, value in pieces])


def per_device(facets, facet_offsets, subgrid_offsets, w_terms, tile_count, tile_offsets, observed):
    n = lax.axis_size("facet")
    slots = observed.shape[0]
    me = lax.axis_index("facet").astype(jnp.int32).reshape(1)
    corners = far(subgrid_offsets.T)
    tile_corners = far(tile_offsets.T)
    facet_offsets = far(facet_offsets)
    basis = far(jnp.asarray(basis_tables()))
    pad_np = padding_tables(n)
    kern_np = kernel_table()
    kt_np = np.zeros((6 * TV, TV), np.float32)
    kt_np[2 * TV : 4 * TV] = kern_np.astype(np.float32).T
    kwide_np = np.zeros((TV, SG), np.float32)
    kwide_np[:, : 2 * TV] = kern_np.astype(np.float32)
    grid_shape = (2, F // M + 1, F + M, M)

    steps = n.bit_length() - 2
    labels = list(range(n // 2))
    sends = [(-1, labels[1::2], 1), (-1, labels[::2], 1)]
    sends += [(k, labels[1 << k :: 2 << k], 0) for k in range(steps)]
    first, spec = pl.pallas_call(
        functools.partial(forward_kernel, n, sends[0][1:]),
        out_shape=[held((len(sends[0][1]), 2, M, M)), held(grid_shape, F32)],
        in_specs=[SMEM] * 3 + [ANY] * 2,
        out_specs=[VMEM] * 2,
        scratch_shapes=[
            pltpu.VMEM((2, F, F), BF),
            pltpu.VMEM((2, F, F), BF),
            pltpu.SemaphoreType.DMA((4,)),
        ],
        compiler_params=params(16),
        name="forward",
    )(me, facet_offsets, corners, far(facets), basis)
    lists = [send[1:] for send in sends[1:]] + [([0], 0)]
    own = pl.pallas_call(
        functools.partial(extract_kernel, n, lists),
        out_shape=[held((len(js), 2, M, M)) for js, _ in lists],
        in_specs=[SMEM] * 3 + [VMEM],
        out_specs=[VMEM] * len(lists),
        compiler_params=params(8),
        name="extract",
    )(me, facet_offsets, corners, near(spec))

    def make_bands(after):
        return pl.pallas_call(
            band_kernel,
            out_shape=[
                held((SG, slots * TV)),
                held((slots * TV, SG)),
                held((slots, SG, TV)),
                held((1, M), F32),
            ],
            in_specs=[SMEM, VMEM] + [ANY] * 2,
            out_specs=[VMEM] * 4,
            scratch_shapes=[
                pltpu.VMEM(kt_np.shape, F32),
                pltpu.VMEM(kwide_np.shape, F32),
                pltpu.SemaphoreType.DMA((2,)),
            ],
            compiler_params=params(8),
            name="bands",
        )(tile_corners, near(after), far(jnp.asarray(kt_np)), far(jnp.asarray(kwide_np)))

    def make_screen(after):
        loads = [observed, pad_np, pad_np.transpose(0, 2, 1), kern_np]
        return pl.pallas_call(
            screen_kernel,
            out_shape=[held((2, SG, SG), F32)]
            + [held(load.shape, load.dtype) for load in loads]
            + [held((1, M), F32)],
            in_specs=[SMEM, VMEM] + [ANY] * len(loads),
            out_specs=[VMEM] * (2 + len(loads)),
            scratch_shapes=[pltpu.SemaphoreType.DMA((len(loads),))],
            compiler_params=params(8),
            name="screen",
        )(w_terms.reshape(1, 1), near(after), *[far(jnp.asarray(load)) for load in loads])

    arrived = []
    token = None
    for (step, js, _), value in zip(sends, [first] + list(own)):
        if step >= 0:
            total = value.astype(F32)
            for got_js, got in arrived:
                if set(js) <= set(got_js):
                    total = total + pick(got, [got_js.index(j) for j in js]).astype(F32)
                else:
                    assert not set(js) & set(got_js)
            if token is not None:
                total = total + token
            value = total.astype(BF)
        got = exchange(value, step, n)
        if step == 0:
            kvt, kv, kut, token = make_bands(value)
        if step == 1:
            screen, tiles, pad, padt, kern, token = make_screen(value)
        arrived.append((js if step < 0 else [j ^ (1 << step) for j in js], got))
    last = [(js, got) for js, got in arrived if 0 in js]

    residual, coefficient = pl.pallas_call(
        functools.partial(subgrid_kernel, [0] + [js.index(0) for js, _ in last]),
        out_shape=[pltpu.HBM(observed.shape, BF), held((1, 2, M, M))],
        in_specs=[SMEM] * 2 + [VMEM] * (len(last) + 9),
        out_specs=[ANY, VMEM],
        scratch_shapes=[
            pltpu.VMEM((2 * SG, SG), BF),
            pltpu.VMEM((8, 2 * SG, TV), F32),
            pltpu.VMEM((2 * SG, slots * TV), BF),
            pltpu.VMEM(observed.shape, BF),
            pltpu.SemaphoreType.DMA((slots // 4,)),
        ],
        compiler_params=params(24),
        name="subgrid",
    )(
        tile_count.reshape(1, 1),
        tile_corners,
        near(own[-1]),
        *[near(got) for _, got in last],
        *[near(value) for value in (tiles, pad, padt, kern, screen, kvt, kv, kut)],
    )

    js, value = [0], coefficient
    for step in range(steps - 1, 0, -1):
        got = exchange(value, step, n)
        js, value = js + [j | (1 << step) for j in js], jnp.concatenate([value, got])
    late_js, late = [j | 1 for j in js], exchange(value, 0, n)
    other = exchange(value, -1, n)
    grid, token = pl.pallas_call(
        functools.partial(first_grid_kernel, n, [(js, 0)]),
        out_shape=[held(grid_shape, F32), held((1, M), F32)],
        in_specs=[SMEM] * 3 + [VMEM],
        out_specs=[VMEM] * 2,
        compiler_params=params(8),
        name="grid_first",
    )(me, facet_offsets, corners, near(value))
    late = (late.astype(F32) + token).astype(BF)
    late_other = exchange(late, -1, n)
    grid = pl.pallas_call(
        functools.partial(next_grid_kernel, n, [(js, 1), (late_js, 0)]),
        out_shape=held(grid_shape, F32),
        in_specs=[SMEM] * 3 + [VMEM] * 3,
        out_specs=VMEM,
        compiler_params=params(8),
        name="grid_next",
    )(me, facet_offsets, corners, near(other), near(late), near(grid))
    update = pl.pallas_call(
        functools.partial(backward_kernel, n, [(late_js, 1)]),
        out_shape=[pltpu.HBM(facets.shape, BF), held(grid_shape, F32)],
        in_specs=[SMEM] * 3 + [ANY] + [VMEM] * 2,
        out_specs=[ANY, VMEM],
        input_output_aliases={5: 1},
        scratch_shapes=[
            pltpu.VMEM((2, F, F), BF),
            pltpu.VMEM((2, F, F), BF),
            pltpu.SemaphoreType.DMA((5,)),
        ],
        compiler_params=params(16),
        name="backward",
    )(me, facet_offsets, corners, basis, near(late_other), near(grid))[0]
    return (residual, update)


def solution(mesh):
    placed = (
        P(("groups", "facet"), None, None, None),
        P(("groups", "facet"), None),
        P("groups", None),
        P(("groups", "facet")),
        P(("groups", "facet")),
        P(("groups", "facet"), None),
        P(("groups", "facet"), None, None, None),
    )
    return jax.shard_map(
        per_device,
        mesh=mesh,
        in_specs=placed,
        out_specs=(
            P(("groups", "facet"), None, None, None),
            P(("groups", "facet"), None, None, None),
        ),
        check_vma=False,
    )
```

```python
import functools
import math

import jax
import jax.numpy as jnp
import ml_dtypes
import numpy as np
from jax import lax
from jax.experimental import pallas as pl
from jax.experimental.pallas import tpu as pltpu
from jax.sharding import PartitionSpec as P

F = 512
M = 128
SG = 512
TV = 128
BF = jnp.bfloat16
F32 = jnp.float32
TWO_PI = 2.0 * math.pi
OUT_CHUNKS = 4


def basis_tables():
    index = np.arange(F, dtype=np.int64)
    angle = -TWO_PI * ((index[:, None] * index[None, :]) % F) / F
    table = np.stack([np.cos(angle), np.sin(angle)]) / math.sqrt(F)
    return table.astype(ml_dtypes.bfloat16)


def padding_tables(facet_count):
    product = (np.arange(SG)[:, None] * np.arange(M)[None, :]) % SG
    angle = TWO_PI * product / SG
    scale = (M * math.sqrt(facet_count)) ** (-0.5)
    table = np.stack([np.cos(angle), np.sin(angle)]) * scale
    return table.astype(ml_dtypes.bfloat16)


def kernel_table():
    rows = np.arange(TV, dtype=np.float64)[:, None]
    columns = np.arange(2 * TV, dtype=np.float64)[None, :]
    distance = columns - 2.0 * rows - 1.0
    value = 0.75 * np.exp(-((distance / 1.5) ** 2))
    return np.where(np.abs(distance) <= 4.0, value, 0.0).astype(ml_dtypes.bfloat16)


def taper_square():
    position = np.arange(M, dtype=np.float64)
    taper = 0.6 + 0.4 * np.sin(math.pi * (position + 0.5) / M)
    return (taper[:, None] * taper[None, :]).astype(np.float32)


def turn_polynomials():
    nodes = 0.5 * np.cos(math.pi * (np.arange(400) + 0.5) / 800)
    square = nodes * nodes
    powers = np.stack([square**k for k in range(8)], axis=1)
    cos_c = np.linalg.lstsq(powers, np.cos(TWO_PI * nodes), rcond=None)[0]
    sin_c = np.linalg.lstsq(powers, np.sin(TWO_PI * nodes) / nodes, rcond=None)[0]
    return [float(c) for c in cos_c], [float(c) for c in sin_c]


COS_C, SIN_C = turn_polynomials()


def cos_sin_turns(turns):
    rest = turns - jnp.floor(turns + 0.5)
    square = rest * rest
    cos_v = jnp.full_like(square, COS_C[7])
    sin_v = jnp.full_like(square, SIN_C[7])
    for k in range(6, -1, -1):
        cos_v = cos_v * square + COS_C[k]
        sin_v = sin_v * square + SIN_C[k]
    return cos_v, sin_v * rest


def dot(left, right):
    return jnp.dot(left, right, preferred_element_type=F32)


def mul_left(left_r, left_i, right_r, right_i):
    left = jnp.concatenate([left_r, left_i], axis=1)
    real = dot(left, jnp.concatenate([right_r, -right_i], axis=0))
    imag = dot(left, jnp.concatenate([right_i, right_r], axis=0))
    return real, imag


def mul_right(left_r, left_i, right_r, right_i):
    right = jnp.concatenate([right_r, right_i], axis=0)
    real = dot(jnp.concatenate([left_r, -left_i], axis=1), right)
    imag = dot(jnp.concatenate([left_i, left_r], axis=1), right)
    return real, imag


def phase_taper(fo_ref):
    rows = lax.broadcasted_iota(jnp.int32, (M, M), 0)
    columns = lax.broadcasted_iota(jnp.int32, (M, M), 1)
    total = (rows * fo_ref[0, 0] + columns * fo_ref[0, 1]) & (F - 1)
    cos_v, sin_v = cos_sin_turns(total.astype(F32) * (1.0 / F))
    row = lax.broadcasted_iota(jnp.int32, (M, 1), 0).astype(F32)
    column = lax.broadcasted_iota(jnp.int32, (1, M), 1).astype(F32)
    _, row_sin = cos_sin_turns((row + 0.5) * (0.5 / M))
    _, column_sin = cos_sin_turns((column + 0.5) * (0.5 / M))
    taper2 = (0.6 + 0.4 * row_sin) * (0.6 + 0.4 * column_sin)
    return cos_v * taper2, sin_v * taper2


def forward_kernel(js, me_ref, fo_ref, so_ref, facet_ref, basis_ref, out_ref, spec_ref, *rest):
    facet_buf, basis_buf, sems = rest
    copies = []
    for k in range(2):
        copies.append(pltpu.make_async_copy(basis_ref.at[k], basis_buf.at[k], sems.at[2 * k]))
        copies.append(pltpu.make_async_copy(facet_ref.at[0, k], facet_buf.at[k], sems.at[2 * k + 1]))
    for copy in copies:
        copy.start()
    for copy in copies:
        copy.wait()
    br, bi = basis_buf[0], basis_buf[1]
    hr, hi = mul_left(facet_buf[0], facet_buf[1], br, bi)
    spectrum = mul_right(br, bi, hr.astype(BF), hi.astype(BF))
    columns = F // M
    for plane in range(2):
        for c in range(columns):
            part = spectrum[plane][:, c * M : (c + 1) * M]
            spec_ref[plane, c, :F] = part
            spec_ref[plane, c, F:] = part[:M]
            if c == 0:
                spec_ref[plane, columns, :F] = part
                spec_ref[plane, columns, F:] = part[:M]
    extract([js], [out_ref], me_ref, fo_ref, so_ref, spec_ref)


def extract_kernel(sends, me_ref, fo_ref, so_ref, spec_ref, *outs):
    extract(sends, outs, me_ref, fo_ref, so_ref, spec_ref)


def extract(sends, outs, me_ref, fo_ref, so_ref, spec_ref):
    pc, ps = phase_taper(fo_ref)
    me = me_ref[0]

    def block(out_ref, item, j):
        owner = j ^ me
        sx, sy = so_ref[0, owner], so_ref[1, owner]
        lane = sy // M
        shift = (2 * M - (sy & (M - 1))) & (2 * M - 1)
        parts = []
        for plane in range(2):
            left = spec_ref[plane, lane, pl.ds(sx, M), :]
            right = spec_ref[plane, lane + 1, pl.ds(sx, M), :]
            wide = jnp.concatenate([left, right], axis=1)
            parts.append(pltpu.roll(wide, shift, 1)[:, :M])
        wr, wi = parts
        out_ref[item, 0] = (pc * wr - ps * wi).astype(BF)
        out_ref[item, 1] = (pc * wi + ps * wr).astype(BF)

    for out_ref, js in zip(outs, sends):
        for_blocks(block, out_ref, js)


def for_blocks(block, ref, js):
    step = js[1] - js[0] if len(js) > 1 else 1
    if len(js) > 1 and js == list(range(js[0], js[0] + step * len(js), step)):

        def body(item, carry):
            block(ref, item, item * step + js[0])
            return carry

        lax.fori_loop(0, len(js), body, 0)
    else:
        for item, j in enumerate(js):
            block(ref, item, j)


def prepare_kernel(w_ref, to_ref, _, *rest):
    loads = (len(rest) - 6) // 2
    sources, (screen_ref, kvt_ref, kv_ref, kut_ref) = rest[:loads], rest[loads : loads + 4]
    targets = rest[loads + 4 : 2 * loads + 2] + rest[-3:-1]
    zero_ref, sems = rest[2 * loads + 2], rest[-1]
    zero_ref[...] = jnp.zeros_like(zero_ref)
    kt_ref, kwide_ref = targets[-2:]
    copies = []
    for k in range(loads - 1, -1, -1):
        copies.append(pltpu.make_async_copy(sources[k], targets[k], sems.at[k]))
        copies[-1].start()
    slots = kut_ref.shape[0]
    w = w_ref[0, 0]
    row = lax.broadcasted_iota(jnp.int32, (SG, 1), 0).astype(F32) - SG / 2.0
    column = lax.broadcasted_iota(jnp.int32, (1, SG), 1).astype(F32) - SG / 2.0
    row2 = row * row * (1.0 / (SG * SG)) + 1.0
    column2 = column * column * (1.0 / (SG * SG))
    cos_v, sin_v = cos_sin_turns((jnp.sqrt(row2 + column2) - 1.0) * w)
    screen_ref[0] = cos_v
    screen_ref[1] = sin_v
    for copy in copies:
        copy.wait()
    for t in range(slots):
        ou, ov = to_ref[0, t], to_ref[1, t]
        kut_ref[t] = kt_ref[pl.ds(2 * TV - ou, SG), :].astype(BF)
        kvt_ref[:, t * TV : (t + 1) * TV] = kt_ref[pl.ds(2 * TV - ov, SG), :].astype(BF)
        kv_ref[t * TV : (t + 1) * TV] = pltpu.roll(kwide_ref[...], ov, 1).astype(BF)


def subgrid_kernel(picks, tc_ref, to_ref, *rest):
    parts = len(picks)
    sums = rest[:parts]
    (obs_ref, pad_ref, padt_ref, kern_ref, screen_ref, kvt_ref, kv_ref, kut_ref) = rest[parts : parts + 8]
    (out_ref, coef_ref, model_ref, z_ref, res_ref, sems, *rows_refs) = rest[parts + 8 :]
    slots = obs_ref.shape[0]
    count = tc_ref[0, 0]

    def total(plane):
        value = sums[0][picks[0], plane].astype(F32)
        for ref, item in zip(sums[1:], picks[1:]):
            value = value + ref[item, plane].astype(F32)
        return value.astype(BF)

    pr, pi = pad_ref[0], pad_ref[1]
    inner_r, inner_i = mul_right(pr, pi, total(0), total(1))
    tr, ti = padt_ref[0], padt_ref[1]
    image_r, image_i = mul_left(inner_r.astype(BF), inner_i.astype(BF), tr, ti)
    sc, ss = screen_ref[0], screen_ref[1]
    model_ref[:SG] = (sc * image_r - ss * image_i).astype(BF)
    model_ref[SG:] = (sc * image_i + ss * image_r).astype(BF)

    model = model_ref[...]
    kern = kern_ref[...]
    copies = []
    for t0 in range(0, slots, 2):
        pair = dot(model, kvt_ref[:, t0 * TV : (t0 + 2) * TV])
        for t in (t0, t0 + 1):
            rows_refs[t % len(rows_refs)][...] = pair[:, (t - t0) * TV : (t - t0 + 1) * TV]
        for t in (t0, t0 + 1):
            rows_ref = rows_refs[t % len(rows_refs)]
            ou = to_ref[0, t]
            wr = rows_ref[pl.ds(ou, 2 * TV), :]
            wi = rows_ref[pl.ds(SG + ou, 2 * TV), :]
            window = jnp.concatenate([wr.astype(BF), wi.astype(BF)], axis=1)
            predicted = dot(kern, window)
            live = count > t
            res = []
            for plane in range(2):
                value = obs_ref[t, plane].astype(F32) - predicted[:, plane * TV : (plane + 1) * TV]
                res.append(jnp.where(live, value, 0.0).astype(BF))
                res_ref[t, plane] = res[plane]
            z = dot(kut_ref[t], jnp.concatenate(res, axis=1)).astype(BF)
            z_ref[:SG, t * TV : (t + 1) * TV] = z[:, :TV]
            z_ref[SG:, t * TV : (t + 1) * TV] = z[:, TV:]
        if t0 % 4 == 2:
            copies.append(
                pltpu.make_async_copy(
                    res_ref.at[pl.ds(t0 - 2, 4)], out_ref.at[pl.ds(t0 - 2, 4)], sems.at[t0 // 4]
                )
            )
            copies[-1].start()

    kv = kv_ref[...]
    ar = dot(z_ref[:SG], kv)
    ai = dot(z_ref[SG:], kv)
    screened_r = (sc * ar + ss * ai).astype(BF)
    screened_i = (sc * ai - ss * ar).astype(BF)
    reduced_r, reduced_i = mul_right(tr, -ti, screened_r, screened_i)
    coef_r, coef_i = mul_left(reduced_r.astype(BF), reduced_i.astype(BF), pr, -pi)
    coef_ref[0, 0] = coef_r.astype(BF)
    coef_ref[0, 1] = coef_i.astype(BF)
    for copy in copies:
        copy.wait()


def grid_blocks(pieces, refs, me_ref, fo_ref, so_ref, grid_ref):
    pc, ps = phase_taper(fo_ref)
    me = me_ref[0]
    blank = jnp.zeros((M, M), F32)

    def block(in_ref, item, j):
        owner = j ^ me
        sx, sy = so_ref[0, owner], so_ref[1, owner]
        lane = sy // M
        shift = sy & (M - 1)
        cr, ci = in_ref[item, 0].astype(F32), in_ref[item, 1].astype(F32)
        values = (pc * cr + ps * ci, pc * ci - ps * cr)
        for plane in range(2):
            wide = pltpu.roll(jnp.concatenate([values[plane], blank], axis=1), shift, 1)
            grid_ref[plane, lane, pl.ds(sx, M), :] += wide[:, :M]
            grid_ref[plane, lane + 1, pl.ds(sx, M), :] += wide[:, M:]

    for in_ref, js in zip(refs, pieces):
        for_blocks(block, in_ref, js)


def first_grid_kernel(pieces, me_ref, fo_ref, so_ref, *rest):
    grid_ref, zero_ref = rest[-2:]
    zero_ref[...] = jnp.zeros_like(zero_ref)
    grid_ref[...] = jnp.zeros_like(grid_ref)
    grid_blocks(pieces, rest[:-2], me_ref, fo_ref, so_ref, grid_ref)


def next_grid_kernel(pieces, me_ref, fo_ref, so_ref, *rest):
    grid_blocks(pieces, rest[:-2], me_ref, fo_ref, so_ref, rest[-2])


def backward_kernel(pieces, me_ref, fo_ref, so_ref, basis_hbm, *rest):
    grid_ref, out_ref, _, basis_ref, out_buf, sems = rest[len(pieces) :]
    load = pltpu.make_async_copy(basis_hbm, basis_ref, sems.at[2 * OUT_CHUNKS])
    load.start()
    grid_blocks(pieces, rest[: len(pieces)], me_ref, fo_ref, so_ref, grid_ref)
    columns = F // M
    folded = []
    for plane in range(2):
        strips = []
        for c in range(columns):
            strip = grid_ref[plane, c]
            if c == 0:
                strip = strip + grid_ref[plane, columns]
            top = strip[:M] + strip[F:]
            strips.append(jnp.concatenate([top.astype(BF), strip[M:F].astype(BF)], axis=0))
        folded.append(jnp.concatenate(strips, axis=1))
    load.wait()
    br, bi = basis_ref[0], basis_ref[1]
    hr, hi = mul_right(br, -bi, *folded)
    hr, hi = hr.astype(BF), hi.astype(BF)
    size = F // OUT_CHUNKS
    copies = []
    for k in range(OUT_CHUNKS):
        rows = slice(k * size, (k + 1) * size)
        real, imag = mul_left(hr[rows], hi[rows], br, -bi)
        for plane, value in enumerate((real, imag)):
            out_buf[plane, rows] = value.astype(BF)
            copy = pltpu.make_async_copy(
                out_buf.at[plane, pl.ds(k * size, size)],
                out_ref.at[0, plane, pl.ds(k * size, size)],
                sems.at[2 * k + plane],
            )
            copy.start()
            copies.append(copy)
    for copy in copies:
        copy.wait()


SMEM = pl.BlockSpec(memory_space=pltpu.SMEM)
VMEM = pl.BlockSpec(memory_space=pltpu.VMEM)
ANY = pl.BlockSpec(memory_space=pl.ANY)


def params(mib):
    return pltpu.CompilerParams(vmem_limit_bytes=mib * 1024 * 1024)


def near(value):
    return pltpu.with_memory_space_constraint(value, pltpu.VMEM)


def far(value):
    return pltpu.with_memory_space_constraint(value, pltpu.HBM)


def held(shape, dtype=BF):
    return pltpu.VMEM(shape, dtype)


def exchange(value, mask, n):
    return lax.ppermute(value, "facet", [(i, i ^ mask) for i in range(n)])


def digit_levels(n):
    levels, base = [], 1
    while base < n:
        radix = 2 if base < 4 or n // base < 4 else 4
        levels.append((base, radix))
        base *= radix
    return levels


def reduce_sends(n):
    levels = digit_levels(n)
    sends = []
    for k, (base, radix) in enumerate(levels):
        for g in range(1, radix):
            js = [j for j in range(0, n, base) if (j // base) % radix == g]
            if k + 1 < len(levels):
                after, width = levels[k + 1]
                groups = [[j for j in js if (j // after) % width], [j for j in js if not (j // after) % width]]
            else:
                groups = [js]
            sends += [(group, g * base) for group in groups if group]
    return sends


def pick(value, items):
    step = items[1] - items[0] if len(items) > 1 else 1
    if items == list(range(items[0], items[0] + step * len(items), step)):
        if len(items) == value.shape[0]:
            return value
        return lax.slice_in_dim(value, items[0], items[-1] + 1, step)
    return jnp.concatenate([value[i : i + 1] for i in items])


def join(pieces):
    return [j for js, _ in pieces for j in js], jnp.concatenate([value for _, value in pieces])


def per_device(facets, facet_offsets, subgrid_offsets, w_terms, tile_count, tile_offsets, observed):
    n = lax.axis_size("facet")
    slots = observed.shape[0]
    me = lax.axis_index("facet").astype(jnp.int32).reshape(1)
    corners = far(subgrid_offsets.T)
    tile_corners = far(tile_offsets.T)
    facet_offsets = far(facet_offsets)
    basis = far(jnp.asarray(basis_tables()))
    pad_np = padding_tables(n)
    kern_np = kernel_table()
    kt_np = np.zeros((6 * TV, TV), np.float32)
    kt_np[2 * TV : 4 * TV] = kern_np.astype(np.float32).T
    kwide_np = np.zeros((TV, SG), np.float32)
    kwide_np[:, : 2 * TV] = kern_np.astype(np.float32)
    grid_shape = (2, F // M + 1, F + M, M)

    sends = reduce_sends(n)
    first, spec = pl.pallas_call(
        functools.partial(forward_kernel, sends[0][0]),
        out_shape=[held((len(sends[0][0]), 2, M, M)), held(grid_shape, F32)],
        in_specs=[SMEM] * 3 + [ANY] * 2,
        out_specs=[VMEM] * 2,
        scratch_shapes=[
            pltpu.VMEM((2, F, F), BF),
            pltpu.VMEM((2, F, F), BF),
            pltpu.SemaphoreType.DMA((4,)),
        ],
        compiler_params=params(16),
        name="forward",
    )(me, facet_offsets, corners, far(facets), basis)
    lists = [js for js, _ in sends[1:]] + [[0]]
    own = pl.pallas_call(
        functools.partial(extract_kernel, lists),
        out_shape=[held((len(js), 2, M, M)) for js in lists],
        in_specs=[SMEM] * 3 + [VMEM],
        out_specs=[VMEM] * len(lists),
        compiler_params=params(8),
        name="extract",
    )(me, facet_offsets, corners, near(spec))

    arrived = []
    for (js, mask), value in zip(sends, [first] + list(own)):
        terms = []
        for got_js, got in arrived:
            if set(js) <= set(got_js):
                terms.append(pick(got, [got_js.index(j) for j in js]))
            else:
                assert not set(js) & set(got_js)
        if terms:
            total = value.astype(F32)
            if mask > 2:
                total = total + prepared[-1]
            for term in terms:
                total = total + term.astype(F32)
            value = total.astype(BF)
        if mask == 2 and len(js) > 1:
            loads = [observed, pad_np, pad_np.transpose(0, 2, 1), kern_np]
            loads += [tile_offsets.T, subgrid_offsets.T, facet_offsets, kt_np, kwide_np]
            prepared = pl.pallas_call(
                prepare_kernel,
                out_shape=[
                    held((2, SG, SG), F32),
                    held((SG, slots * TV)),
                    held((slots * TV, SG)),
                    held((slots, SG, TV)),
                ]
                + [held(load.shape, load.dtype) for load in loads[:-2]]
                + [held((1, M), F32)],
                in_specs=[SMEM] * 2 + [VMEM] + [ANY] * len(loads),
                out_specs=[VMEM] * (3 + len(loads)),
                scratch_shapes=[
                    pltpu.VMEM(kt_np.shape, F32),
                    pltpu.VMEM(kwide_np.shape, F32),
                    pltpu.SemaphoreType.DMA((len(loads),)),
                ],
                compiler_params=params(8),
                name="prepare",
            )(w_terms.reshape(1, 1), tile_corners, near(value), *[far(jnp.asarray(load)) for load in loads])
        got = exchange(value, mask, n)
        arrived.append(([j ^ mask for j in js], got))
    last = [(js, got) for js, got in arrived if 0 in js]
    screen, kvt, kv, kut, tiles, pad, padt, kern = prepared[:8]
    tile_corners, corners, facet_offsets = [near(value) for value in prepared[8:11]]

    residual, coefficient = pl.pallas_call(
        functools.partial(subgrid_kernel, [0] + [js.index(0) for js, _ in last]),
        out_shape=[pltpu.HBM(observed.shape, BF), held((1, 2, M, M))],
        in_specs=[SMEM] * 2 + [VMEM] * (len(last) + 9),
        out_specs=[ANY, VMEM],
        scratch_shapes=[
            pltpu.VMEM((2 * SG, SG), BF),
            pltpu.VMEM((2 * SG, slots * TV), BF),
            pltpu.VMEM(observed.shape, BF),
            pltpu.SemaphoreType.DMA((slots // 4,)),
        ]
        + [pltpu.VMEM((2 * SG, TV), F32)] * 8,
        compiler_params=params(24),
        name="subgrid",
    )(
        tile_count.reshape(1, 1),
        tile_corners,
        near(own[-1]),
        *[near(got) for _, got in last],
        *[near(value) for value in (tiles, pad, padt, kern, screen, kvt, kv, kut)],
    )

    early = ([0], coefficient)
    for base, radix in reversed(digit_levels(n)[2:]):
        js, value = early
        more = [([j ^ (g * base) for j in js], exchange(value, g * base, n)) for g in range(1, radix)]
        early = join([early] + more)
    js, value = early
    late_js, late = [j ^ 2 for j in js], exchange(value, 2, n)
    other_js, other = [j ^ 1 for j in js], exchange(value, 1, n)
    grid, token = pl.pallas_call(
        functools.partial(first_grid_kernel, [js]),
        out_shape=[held(grid_shape, F32), held((1, M), F32)],
        in_specs=[SMEM] * 3 + [VMEM],
        out_specs=[VMEM] * 2,
        compiler_params=params(8),
        name="grid_first",
    )(me, facet_offsets, corners, near(value))
    late = (late.astype(F32) + token).astype(BF)
    late_other = ([j ^ 1 for j in late_js], exchange(late, 1, n))
    grid = pl.pallas_call(
        functools.partial(next_grid_kernel, [other_js, late_js]),
        out_shape=held(grid_shape, F32),
        in_specs=[SMEM] * 3 + [VMEM] * 3,
        out_specs=VMEM,
        input_output_aliases={5: 0},
        compiler_params=params(8),
        name="grid_next",
    )(me, facet_offsets, corners, near(other), near(late), near(grid))
    update = pl.pallas_call(
        functools.partial(backward_kernel, [late_other[0]]),
        out_shape=[pltpu.HBM(facets.shape, BF), held(grid_shape, F32)],
        in_specs=[SMEM] * 3 + [ANY] + [VMEM] * 2,
        out_specs=[ANY, VMEM],
        input_output_aliases={5: 1},
        scratch_shapes=[
            pltpu.VMEM((2, F, F), BF),
            pltpu.VMEM((2, F, F), BF),
            pltpu.SemaphoreType.DMA((2 * OUT_CHUNKS + 1,)),
        ],
        compiler_params=params(16),
        name="backward",
    )(me, facet_offsets, corners, basis, near(late_other[1]), near(grid))[0]
    return (residual, update)


def solution(mesh):
    placed = (
        P(("groups", "facet"), None, None, None),
        P(("groups", "facet"), None),
        P("groups", None),
        P(("groups", "facet")),
        P(("groups", "facet")),
        P(("groups", "facet"), None),
        P(("groups", "facet"), None, None, None),
    )
    return jax.shard_map(
        per_device,
        mesh=mesh,
        in_specs=placed,
        out_specs=(
            P(("groups", "facet"), None, None, None),
            P(("groups", "facet"), None, None, None),
        ),
        check_vma=False,
    )
```

```python
import functools
import math

import jax
import jax.numpy as jnp
import ml_dtypes
import numpy as np
from jax import lax
from jax.experimental import pallas as pl
from jax.experimental.pallas import tpu as pltpu
from jax.sharding import PartitionSpec as P

F = 512
M = 128
SG = 512
TV = 128
BF = jnp.bfloat16
F32 = jnp.float32
TWO_PI = 2.0 * math.pi
OUT_CHUNKS = 4


def basis_tables():
    index = np.arange(F, dtype=np.int64)
    angle = -TWO_PI * ((index[:, None] * index[None, :]) % F) / F
    table = np.stack([np.cos(angle), np.sin(angle)]) / math.sqrt(F)
    return table.astype(ml_dtypes.bfloat16)


def padding_tables(facet_count):
    product = (np.arange(SG)[:, None] * np.arange(M)[None, :]) % SG
    angle = TWO_PI * product / SG
    scale = (M * math.sqrt(facet_count)) ** (-0.5)
    table = np.stack([np.cos(angle), np.sin(angle)]) * scale
    return table.astype(ml_dtypes.bfloat16)


def kernel_table():
    rows = np.arange(TV, dtype=np.float64)[:, None]
    columns = np.arange(2 * TV, dtype=np.float64)[None, :]
    distance = columns - 2.0 * rows - 1.0
    value = 0.75 * np.exp(-((distance / 1.5) ** 2))
    return np.where(np.abs(distance) <= 4.0, value, 0.0).astype(ml_dtypes.bfloat16)


def taper_square():
    position = np.arange(M, dtype=np.float64)
    taper = 0.6 + 0.4 * np.sin(math.pi * (position + 0.5) / M)
    return (taper[:, None] * taper[None, :]).astype(np.float32)


def turn_polynomials():
    nodes = 0.5 * np.cos(math.pi * (np.arange(400) + 0.5) / 800)
    square = nodes * nodes
    powers = np.stack([square**k for k in range(8)], axis=1)
    cos_c = np.linalg.lstsq(powers, np.cos(TWO_PI * nodes), rcond=None)[0]
    sin_c = np.linalg.lstsq(powers, np.sin(TWO_PI * nodes) / nodes, rcond=None)[0]
    return [float(c) for c in cos_c], [float(c) for c in sin_c]


COS_C, SIN_C = turn_polynomials()


def cos_sin_turns(turns):
    rest = turns - jnp.floor(turns + 0.5)
    square = rest * rest
    cos_v = jnp.full_like(square, COS_C[7])
    sin_v = jnp.full_like(square, SIN_C[7])
    for k in range(6, -1, -1):
        cos_v = cos_v * square + COS_C[k]
        sin_v = sin_v * square + SIN_C[k]
    return cos_v, sin_v * rest


def dot(left, right):
    return jnp.dot(left, right, preferred_element_type=F32)


def mul_left(left_r, left_i, right_r, right_i):
    left = jnp.concatenate([left_r, left_i], axis=1)
    real = dot(left, jnp.concatenate([right_r, -right_i], axis=0))
    imag = dot(left, jnp.concatenate([right_i, right_r], axis=0))
    return real, imag


def mul_right(left_r, left_i, right_r, right_i):
    right = jnp.concatenate([right_r, right_i], axis=0)
    real = dot(jnp.concatenate([left_r, -left_i], axis=1), right)
    imag = dot(jnp.concatenate([left_i, left_r], axis=1), right)
    return real, imag


def phase_taper(fo_ref):
    rows = lax.broadcasted_iota(jnp.int32, (M, M), 0)
    columns = lax.broadcasted_iota(jnp.int32, (M, M), 1)
    total = (rows * fo_ref[0, 0] + columns * fo_ref[0, 1]) & (F - 1)
    cos_v, sin_v = cos_sin_turns(total.astype(F32) * (1.0 / F))
    row = lax.broadcasted_iota(jnp.int32, (M, 1), 0).astype(F32)
    column = lax.broadcasted_iota(jnp.int32, (1, M), 1).astype(F32)
    _, row_sin = cos_sin_turns((row + 0.5) * (0.5 / M))
    _, column_sin = cos_sin_turns((column + 0.5) * (0.5 / M))
    taper2 = (0.6 + 0.4 * row_sin) * (0.6 + 0.4 * column_sin)
    return cos_v * taper2, sin_v * taper2


def forward_kernel(js, me_ref, fo_hbm, so_hbm, facet_ref, basis_ref, out_ref, spec_ref, *rest):
    facet_buf, basis_buf, fo_ref, so_ref, sems = rest
    copies = [
        pltpu.make_async_copy(fo_hbm, fo_ref, sems.at[4]),
        pltpu.make_async_copy(so_hbm, so_ref, sems.at[5]),
    ]
    for k in range(2):
        copies.append(pltpu.make_async_copy(basis_ref.at[k], basis_buf.at[k], sems.at[2 * k]))
        copies.append(pltpu.make_async_copy(facet_ref.at[0, k], facet_buf.at[k], sems.at[2 * k + 1]))
    for copy in copies:
        copy.start()
    for copy in copies:
        copy.wait()
    br, bi = basis_buf[0], basis_buf[1]
    hr, hi = mul_left(facet_buf[0], facet_buf[1], br, bi)
    spectrum = mul_right(br, bi, hr.astype(BF), hi.astype(BF))
    columns = F // M
    for plane in range(2):
        for c in range(columns):
            part = spectrum[plane][:, c * M : (c + 1) * M]
            spec_ref[plane, c, :F] = part
            spec_ref[plane, c, F:] = part[:M]
            if c == 0:
                spec_ref[plane, columns, :F] = part
                spec_ref[plane, columns, F:] = part[:M]
    extract([js], [out_ref], me_ref, fo_ref, so_ref, spec_ref)


def extract_kernel(sends, me_ref, fo_ref, so_ref, spec_ref, *outs):
    extract(sends, outs, me_ref, fo_ref, so_ref, spec_ref)


def extract(sends, outs, me_ref, fo_ref, so_ref, spec_ref):
    pc, ps = phase_taper(fo_ref)
    me = me_ref[0]

    def block(out_ref, item, j):
        owner = j ^ me
        sx, sy = so_ref[0, owner], so_ref[1, owner]
        lane = sy // M
        shift = (2 * M - (sy & (M - 1))) & (2 * M - 1)
        parts = []
        for plane in range(2):
            left = spec_ref[plane, lane, pl.ds(sx, M), :]
            right = spec_ref[plane, lane + 1, pl.ds(sx, M), :]
            wide = jnp.concatenate([left, right], axis=1)
            parts.append(pltpu.roll(wide, shift, 1)[:, :M])
        wr, wi = parts
        out_ref[item, 0] = (pc * wr - ps * wi).astype(BF)
        out_ref[item, 1] = (pc * wi + ps * wr).astype(BF)

    for out_ref, js in zip(outs, sends):
        for_blocks(block, out_ref, js)


def for_blocks(block, ref, js):
    step = js[1] - js[0] if len(js) > 1 else 1
    if len(js) > 1 and js == list(range(js[0], js[0] + step * len(js), step)):

        def body(item, carry):
            block(ref, item, item * step + js[0])
            return carry

        lax.fori_loop(0, len(js), body, 0)
    else:
        for item, j in enumerate(js):
            block(ref, item, j)


def band_kernel(to_ref, _, kt_hbm, kwide_hbm, kvt_ref, kv_ref, kut_ref, ku_ref, zero_ref, kt_ref, kwide_ref, sems):
    slots = kut_ref.shape[0]
    copies = [
        pltpu.make_async_copy(kt_hbm, kt_ref, sems.at[0]),
        pltpu.make_async_copy(kwide_hbm, kwide_ref, sems.at[1]),
    ]
    for copy in copies:
        copy.start()
    zero_ref[...] = jnp.zeros_like(zero_ref)
    for copy in copies:
        copy.wait()
    for t in range(slots):
        ou, ov = to_ref[0, t], to_ref[1, t]
        rows = slice(t * TV, (t + 1) * TV)
        kut_ref[t] = kt_ref[pl.ds(2 * TV - ou, SG), :].astype(BF)
        kvt_ref[:, rows] = kt_ref[pl.ds(2 * TV - ov, SG), :].astype(BF)
        ku_ref[rows] = pltpu.roll(kwide_ref[...], ou, 1).astype(BF)
        kv_ref[rows] = pltpu.roll(kwide_ref[...], ov, 1).astype(BF)


def screen_kernel(w_ref, _, *rest):
    loads = (len(rest) - 2) // 2
    sources, screen_ref = rest[:loads], rest[loads]
    targets, sems = rest[loads + 1 : -1], rest[-1]
    copies = [pltpu.make_async_copy(sources[k], targets[k], sems.at[k]) for k in range(loads)]
    for copy in copies:
        copy.start()
    w = w_ref[0, 0]
    row = lax.broadcasted_iota(jnp.int32, (SG, 1), 0).astype(F32) - SG / 2.0
    column = lax.broadcasted_iota(jnp.int32, (1, SG), 1).astype(F32) - SG / 2.0
    row2 = row * row * (1.0 / (SG * SG)) + 1.0
    column2 = column * column * (1.0 / (SG * SG))
    cos_v, sin_v = cos_sin_turns((jnp.sqrt(row2 + column2) - 1.0) * w)
    screen_ref[0] = cos_v
    screen_ref[1] = sin_v
    for copy in copies:
        copy.wait()


def subgrid_kernel(picks, tc_ref, *rest):
    parts = len(picks)
    sums = rest[:parts]
    (obs_ref, pad_ref, padt_ref, screen_ref, kvt_ref, kv_ref, kut_ref, ku_ref) = rest[parts : parts + 8]
    (out_ref, coef_ref, model_ref, rows_ref, z_ref, res_ref, sems) = rest[parts + 8 :]
    slots = obs_ref.shape[0]
    count = tc_ref[0, 0]

    def total(plane):
        value = sums[0][picks[0], plane].astype(F32)
        for ref, item in zip(sums[1:], picks[1:]):
            value = value + ref[item, plane].astype(F32)
        return value.astype(BF)

    pr, pi = pad_ref[0], pad_ref[1]
    inner_r, inner_i = mul_right(pr, pi, total(0), total(1))
    tr, ti = padt_ref[0], padt_ref[1]
    image_r, image_i = mul_left(inner_r.astype(BF), inner_i.astype(BF), tr, ti)
    sc, ss = screen_ref[0], screen_ref[1]
    model_ref[:SG] = (sc * image_r - ss * image_i).astype(BF)
    model_ref[SG:] = (sc * image_i + ss * image_r).astype(BF)

    model = model_ref[...]
    for t0 in range(0, slots, 2):
        pair = dot(model, kvt_ref[:, t0 * TV : (t0 + 2) * TV]).astype(BF)
        for t in (t0, t0 + 1):
            lanes = slice((t - t0) * TV, (t - t0 + 1) * TV)
            rows_ref[:, 2 * t * TV : (2 * t + 1) * TV] = pair[:SG, lanes]
            rows_ref[:, (2 * t + 1) * TV : (2 * t + 2) * TV] = pair[SG:, lanes]
    copies = []
    for t in range(slots):
        predicted = dot(ku_ref[t * TV : (t + 1) * TV], rows_ref[:, 2 * t * TV : (2 * t + 2) * TV])
        live = count > t
        for plane in range(2):
            value = obs_ref[t, plane].astype(F32) - predicted[:, plane * TV : (plane + 1) * TV]
            res_ref[t, plane] = jnp.where(live, value, 0.0).astype(BF)
        if t % 4 == 3:
            copies.append(
                pltpu.make_async_copy(
                    res_ref.at[pl.ds(t - 3, 4)], out_ref.at[pl.ds(t - 3, 4)], sems.at[t // 4]
                )
            )
            copies[-1].start()
    for t in range(slots):
        z = dot(kut_ref[t], jnp.concatenate([res_ref[t, 0], res_ref[t, 1]], axis=1)).astype(BF)
        z_ref[:SG, t * TV : (t + 1) * TV] = z[:, :TV]
        z_ref[SG:, t * TV : (t + 1) * TV] = z[:, TV:]

    kv = kv_ref[...]
    ar = dot(z_ref[:SG], kv)
    ai = dot(z_ref[SG:], kv)
    screened_r = (sc * ar + ss * ai).astype(BF)
    screened_i = (sc * ai - ss * ar).astype(BF)
    reduced_r, reduced_i = mul_right(tr, -ti, screened_r, screened_i)
    coef_r, coef_i = mul_left(reduced_r.astype(BF), reduced_i.astype(BF), pr, -pi)
    coef_ref[0, 0] = coef_r.astype(BF)
    coef_ref[0, 1] = coef_i.astype(BF)
    for copy in copies:
        copy.wait()


def grid_blocks(pieces, refs, me_ref, fo_ref, so_ref, grid_ref):
    pc, ps = phase_taper(fo_ref)
    me = me_ref[0]
    blank = jnp.zeros((M, M), F32)

    def block(in_ref, item, j):
        owner = j ^ me
        sx, sy = so_ref[0, owner], so_ref[1, owner]
        lane = sy // M
        shift = sy & (M - 1)
        cr, ci = in_ref[item, 0].astype(F32), in_ref[item, 1].astype(F32)
        values = (pc * cr + ps * ci, pc * ci - ps * cr)
        for plane in range(2):
            wide = pltpu.roll(jnp.concatenate([values[plane], blank], axis=1), shift, 1)
            grid_ref[plane, lane, pl.ds(sx, M), :] += wide[:, :M]
            grid_ref[plane, lane + 1, pl.ds(sx, M), :] += wide[:, M:]

    for in_ref, js in zip(refs, pieces):
        for_blocks(block, in_ref, js)


def first_grid_kernel(pieces, me_ref, fo_ref, so_ref, *rest):
    grid_ref, zero_ref = rest[-2:]
    zero_ref[...] = jnp.zeros_like(zero_ref)
    grid_ref[...] = jnp.zeros_like(grid_ref)
    grid_blocks(pieces, rest[:-2], me_ref, fo_ref, so_ref, grid_ref)


def next_grid_kernel(pieces, me_ref, fo_ref, so_ref, *rest):
    grid_blocks(pieces, rest[:-2], me_ref, fo_ref, so_ref, rest[-2])


def backward_kernel(pieces, me_ref, fo_ref, so_ref, basis_hbm, *rest):
    grid_ref, out_ref, _, basis_ref, out_buf, sems = rest[len(pieces) :]
    load = pltpu.make_async_copy(basis_hbm, basis_ref, sems.at[2 * OUT_CHUNKS])
    load.start()
    grid_blocks(pieces, rest[: len(pieces)], me_ref, fo_ref, so_ref, grid_ref)
    columns = F // M
    folded = []
    for plane in range(2):
        strips = []
        for c in range(columns):
            strip = grid_ref[plane, c]
            if c == 0:
                strip = strip + grid_ref[plane, columns]
            top = strip[:M] + strip[F:]
            strips.append(jnp.concatenate([top.astype(BF), strip[M:F].astype(BF)], axis=0))
        folded.append(jnp.concatenate(strips, axis=1))
    load.wait()
    br, bi = basis_ref[0], basis_ref[1]
    hr, hi = mul_right(br, -bi, *folded)
    hr, hi = hr.astype(BF), hi.astype(BF)
    size = F // OUT_CHUNKS
    copies = []
    for k in range(OUT_CHUNKS):
        rows = slice(k * size, (k + 1) * size)
        real, imag = mul_left(hr[rows], hi[rows], br, -bi)
        for plane, value in enumerate((real, imag)):
            out_buf[plane, rows] = value.astype(BF)
            copy = pltpu.make_async_copy(
                out_buf.at[plane, pl.ds(k * size, size)],
                out_ref.at[0, plane, pl.ds(k * size, size)],
                sems.at[2 * k + plane],
            )
            copy.start()
            copies.append(copy)
    for copy in copies:
        copy.wait()


SMEM = pl.BlockSpec(memory_space=pltpu.SMEM)
VMEM = pl.BlockSpec(memory_space=pltpu.VMEM)
ANY = pl.BlockSpec(memory_space=pl.ANY)


def params(mib):
    return pltpu.CompilerParams(vmem_limit_bytes=mib * 1024 * 1024)


def near(value):
    return pltpu.with_memory_space_constraint(value, pltpu.VMEM)


def far(value):
    return pltpu.with_memory_space_constraint(value, pltpu.HBM)


def held(shape, dtype=BF):
    return pltpu.VMEM(shape, dtype)


def exchange(value, mask, n):
    return lax.ppermute(value, "facet", [(i, i ^ mask) for i in range(n)])


def digit_levels(n):
    levels, base = [], 1
    while base < n:
        radix = 2 if base < 4 or n // base < 4 else 4
        levels.append((base, radix))
        base *= radix
    return levels


def reduce_sends(n):
    levels = digit_levels(n)
    sends = []
    for k, (base, radix) in enumerate(levels):
        for g in range(1, radix):
            js = [j for j in range(0, n, base) if (j // base) % radix == g]
            if k + 1 < len(levels):
                after, width = levels[k + 1]
                groups = [[j for j in js if (j // after) % width], [j for j in js if not (j // after) % width]]
            else:
                groups = [js]
            sends += [(group, g * base) for group in groups if group]
    return sends


def pick(value, items):
    step = items[1] - items[0] if len(items) > 1 else 1
    if items == list(range(items[0], items[0] + step * len(items), step)):
        if len(items) == value.shape[0]:
            return value
        return lax.slice_in_dim(value, items[0], items[-1] + 1, step)
    return jnp.concatenate([value[i : i + 1] for i in items])


def join(pieces):
    return [j for js, _ in pieces for j in js], jnp.concatenate([value for _, value in pieces])


def per_device(facets, facet_offsets, subgrid_offsets, w_terms, tile_count, tile_offsets, observed):
    n = lax.axis_size("facet")
    slots = observed.shape[0]
    me = lax.axis_index("facet").astype(jnp.int32).reshape(1)
    corners = far(subgrid_offsets.T)
    tile_corners = far(tile_offsets.T)
    facet_offsets = far(facet_offsets)
    basis = far(jnp.asarray(basis_tables()))
    pad_np = padding_tables(n)
    kern_np = kernel_table()
    kt_np = np.zeros((6 * TV, TV), np.float32)
    kt_np[2 * TV : 4 * TV] = kern_np.astype(np.float32).T
    kwide_np = np.zeros((TV, SG), np.float32)
    kwide_np[:, : 2 * TV] = kern_np.astype(np.float32)
    grid_shape = (2, F // M + 1, F + M, M)

    sends = reduce_sends(n)
    first, spec = pl.pallas_call(
        functools.partial(forward_kernel, sends[0][0]),
        out_shape=[held((len(sends[0][0]), 2, M, M)), held(grid_shape, F32)],
        in_specs=[SMEM] + [ANY] * 4,
        out_specs=[VMEM] * 2,
        scratch_shapes=[
            pltpu.VMEM((2, F, F), BF),
            pltpu.VMEM((2, F, F), BF),
            pltpu.SMEM(facet_offsets.shape, jnp.int32),
            pltpu.SMEM(corners.shape, jnp.int32),
            pltpu.SemaphoreType.DMA((6,)),
        ],
        compiler_params=params(16),
        name="forward",
    )(me, facet_offsets, corners, far(facets), basis)
    lists = [js for js, _ in sends[1:]] + [[0]]
    own = pl.pallas_call(
        functools.partial(extract_kernel, lists),
        out_shape=[held((len(js), 2, M, M)) for js in lists],
        in_specs=[SMEM] * 3 + [VMEM],
        out_specs=[VMEM] * len(lists),
        compiler_params=params(8),
        name="extract",
    )(me, facet_offsets, corners, near(spec))

    def make_bands(after):
        big = held((slots * TV, SG))
        return pl.pallas_call(
            band_kernel,
            out_shape=[held((SG, slots * TV)), big, held((slots, SG, TV)), big, held((1, M), F32)],
            in_specs=[SMEM, VMEM] + [ANY] * 2,
            out_specs=[VMEM] * 5,
            scratch_shapes=[
                pltpu.VMEM(kt_np.shape, F32),
                pltpu.VMEM(kwide_np.shape, F32),
                pltpu.SemaphoreType.DMA((2,)),
            ],
            compiler_params=params(8),
            name="bands",
        )(tile_corners, near(after), far(jnp.asarray(kt_np)), far(jnp.asarray(kwide_np)))

    def make_screen(after):
        loads = [observed, pad_np, pad_np.transpose(0, 2, 1), subgrid_offsets.T, facet_offsets]
        return pl.pallas_call(
            screen_kernel,
            out_shape=[held((2, SG, SG), F32)] + [held(load.shape, load.dtype) for load in loads],
            in_specs=[SMEM, VMEM] + [ANY] * len(loads),
            out_specs=[VMEM] * (1 + len(loads)),
            scratch_shapes=[pltpu.SemaphoreType.DMA((len(loads),))],
            compiler_params=params(8),
            name="screen",
        )(w_terms.reshape(1, 1), near(after), *[far(jnp.asarray(load)) for load in loads])

    arrived = []
    token = None
    for (js, mask), value in zip(sends, [first] + list(own)):
        terms = []
        for got_js, got in arrived:
            if set(js) <= set(got_js):
                terms.append(pick(got, [got_js.index(j) for j in js]))
            else:
                assert not set(js) & set(got_js)
        if terms:
            total = value.astype(F32)
            if token is not None:
                total = total + token
            for term in terms:
                total = total + term.astype(F32)
            value = total.astype(BF)
        arrived.append(([j ^ mask for j in js], exchange(value, mask, n)))
        if mask == 2 and token is None:
            kvt, kv, kut, ku, token = make_bands(value)
    screen, tiles, pad, padt, corners, facet_offsets = make_screen(value)
    corners, facet_offsets = near(corners), near(facet_offsets)
    last = [(js, got) for js, got in arrived if 0 in js]

    residual, coefficient = pl.pallas_call(
        functools.partial(subgrid_kernel, [0] + [js.index(0) for js, _ in last]),
        out_shape=[pltpu.HBM(observed.shape, BF), held((1, 2, M, M))],
        in_specs=[SMEM] + [VMEM] * (len(last) + 9),
        out_specs=[ANY, VMEM],
        scratch_shapes=[
            pltpu.VMEM((2 * SG, SG), BF),
            pltpu.VMEM((SG, 2 * slots * TV), BF),
            pltpu.VMEM((2 * SG, slots * TV), BF),
            pltpu.VMEM(observed.shape, BF),
            pltpu.SemaphoreType.DMA((slots // 4,)),
        ],
        compiler_params=params(24),
        name="subgrid",
    )(
        tile_count.reshape(1, 1),
        near(own[-1]),
        *[near(got) for _, got in last],
        *[near(value) for value in (tiles, pad, padt, screen, kvt, kv, kut, ku)],
    )

    early = ([0], coefficient)
    for base, radix in reversed(digit_levels(n)[2:]):
        js, value = early
        more = [([j ^ (g * base) for j in js], exchange(value, g * base, n)) for g in range(1, radix)]
        early = join([early] + more)
    js, value = early
    late_js, late = [j ^ 2 for j in js], exchange(value, 2, n)
    other_js, other = [j ^ 1 for j in js], exchange(value, 1, n)
    grid, token = pl.pallas_call(
        functools.partial(first_grid_kernel, [js]),
        out_shape=[held(grid_shape, F32), held((1, M), F32)],
        in_specs=[SMEM] * 3 + [VMEM],
        out_specs=[VMEM] * 2,
        compiler_params=params(8),
        name="grid_first",
    )(me, facet_offsets, corners, near(value))
    late = (late.astype(F32) + token).astype(BF)
    late_other = ([j ^ 1 for j in late_js], exchange(late, 1, n))
    grid = pl.pallas_call(
        functools.partial(next_grid_kernel, [other_js, late_js]),
        out_shape=held(grid_shape, F32),
        in_specs=[SMEM] * 3 + [VMEM] * 3,
        out_specs=VMEM,
        input_output_aliases={5: 0},
        compiler_params=params(8),
        name="grid_next",
    )(me, facet_offsets, corners, near(other), near(late), near(grid))
    update = pl.pallas_call(
        functools.partial(backward_kernel, [late_other[0]]),
        out_shape=[pltpu.HBM(facets.shape, BF), held(grid_shape, F32)],
        in_specs=[SMEM] * 3 + [ANY] + [VMEM] * 2,
        out_specs=[ANY, VMEM],
        input_output_aliases={5: 1},
        scratch_shapes=[
            pltpu.VMEM((2, F, F), BF),
            pltpu.VMEM((2, F, F), BF),
            pltpu.SemaphoreType.DMA((2 * OUT_CHUNKS + 1,)),
        ],
        compiler_params=params(16),
        name="backward",
    )(me, facet_offsets, corners, basis, near(late_other[1]), near(grid))[0]
    return (residual, update)


def solution(mesh):
    placed = (
        P(("groups", "facet"), None, None, None),
        P(("groups", "facet"), None),
        P("groups", None),
        P(("groups", "facet")),
        P(("groups", "facet")),
        P(("groups", "facet"), None),
        P(("groups", "facet"), None, None, None),
    )
    return jax.shard_map(
        per_device,
        mesh=mesh,
        in_specs=placed,
        out_specs=(
            P(("groups", "facet"), None, None, None),
            P(("groups", "facet"), None, None, None),
        ),
        check_vma=False,
    )
```

```python
import functools
import math

import jax
import jax.numpy as jnp
import ml_dtypes
import numpy as np
from jax import lax
from jax.experimental import pallas as pl
from jax.experimental.pallas import tpu as pltpu
from jax.sharding import PartitionSpec as P

F = 512
M = 128
SG = 512
TV = 128
BF = jnp.bfloat16
F32 = jnp.float32
TWO_PI = 2.0 * math.pi
OUT_CHUNKS = 4


def basis_tables():
    index = np.arange(F, dtype=np.int64)
    angle = -TWO_PI * ((index[:, None] * index[None, :]) % F) / F
    table = np.stack([np.cos(angle), np.sin(angle)]) / math.sqrt(F)
    return table.astype(ml_dtypes.bfloat16)


def padding_tables(facet_count):
    product = (np.arange(SG)[:, None] * np.arange(M)[None, :]) % SG
    angle = TWO_PI * product / SG
    scale = (M * math.sqrt(facet_count)) ** (-0.5)
    table = np.stack([np.cos(angle), np.sin(angle)]) * scale
    return table.astype(ml_dtypes.bfloat16)


def kernel_table():
    rows = np.arange(TV, dtype=np.float64)[:, None]
    columns = np.arange(2 * TV, dtype=np.float64)[None, :]
    distance = columns - 2.0 * rows - 1.0
    value = 0.75 * np.exp(-((distance / 1.5) ** 2))
    return np.where(np.abs(distance) <= 4.0, value, 0.0).astype(ml_dtypes.bfloat16)


def taper_square():
    position = np.arange(M, dtype=np.float64)
    taper = 0.6 + 0.4 * np.sin(math.pi * (position + 0.5) / M)
    return (taper[:, None] * taper[None, :]).astype(np.float32)


def turn_polynomials():
    nodes = 0.5 * np.cos(math.pi * (np.arange(400) + 0.5) / 800)
    square = nodes * nodes
    powers = np.stack([square**k for k in range(8)], axis=1)
    cos_c = np.linalg.lstsq(powers, np.cos(TWO_PI * nodes), rcond=None)[0]
    sin_c = np.linalg.lstsq(powers, np.sin(TWO_PI * nodes) / nodes, rcond=None)[0]
    return [float(c) for c in cos_c], [float(c) for c in sin_c]


COS_C, SIN_C = turn_polynomials()


def cos_sin_turns(turns):
    rest = turns - jnp.floor(turns + 0.5)
    square = rest * rest
    cos_v = jnp.full_like(square, COS_C[7])
    sin_v = jnp.full_like(square, SIN_C[7])
    for k in range(6, -1, -1):
        cos_v = cos_v * square + COS_C[k]
        sin_v = sin_v * square + SIN_C[k]
    return cos_v, sin_v * rest


def dot(left, right):
    return jnp.dot(left, right, preferred_element_type=F32)


def mul_left(left_r, left_i, right_r, right_i):
    left = jnp.concatenate([left_r, left_i], axis=1)
    real = dot(left, jnp.concatenate([right_r, -right_i], axis=0))
    imag = dot(left, jnp.concatenate([right_i, right_r], axis=0))
    return real, imag


def mul_right(left_r, left_i, right_r, right_i):
    right = jnp.concatenate([right_r, right_i], axis=0)
    real = dot(jnp.concatenate([left_r, -left_i], axis=1), right)
    imag = dot(jnp.concatenate([left_i, left_r], axis=1), right)
    return real, imag


def phase_taper(fo_ref):
    rows = lax.broadcasted_iota(jnp.int32, (M, M), 0)
    columns = lax.broadcasted_iota(jnp.int32, (M, M), 1)
    total = (rows * fo_ref[0, 0] + columns * fo_ref[0, 1]) & (F - 1)
    cos_v, sin_v = cos_sin_turns(total.astype(F32) * (1.0 / F))
    row = lax.broadcasted_iota(jnp.int32, (M, 1), 0).astype(F32)
    column = lax.broadcasted_iota(jnp.int32, (1, M), 1).astype(F32)
    _, row_sin = cos_sin_turns((row + 0.5) * (0.5 / M))
    _, column_sin = cos_sin_turns((column + 0.5) * (0.5 / M))
    taper2 = (0.6 + 0.4 * row_sin) * (0.6 + 0.4 * column_sin)
    return cos_v * taper2, sin_v * taper2


def forward_kernel(js, me_ref, fo_hbm, so_hbm, facet_ref, basis_ref, out_ref, spec_ref, *rest):
    facet_buf, basis_buf, fo_ref, so_ref, sems = rest
    copies = [
        pltpu.make_async_copy(fo_hbm, fo_ref, sems.at[4]),
        pltpu.make_async_copy(so_hbm, so_ref, sems.at[5]),
    ]
    for k in range(2):
        copies.append(pltpu.make_async_copy(basis_ref.at[k], basis_buf.at[k], sems.at[2 * k]))
        copies.append(pltpu.make_async_copy(facet_ref.at[0, k], facet_buf.at[k], sems.at[2 * k + 1]))
    for copy in copies:
        copy.start()
    for copy in copies:
        copy.wait()
    br, bi = basis_buf[0], basis_buf[1]
    hr, hi = mul_left(facet_buf[0], facet_buf[1], br, bi)
    spectrum = mul_right(br, bi, hr.astype(BF), hi.astype(BF))
    columns = F // M
    for plane in range(2):
        for c in range(columns):
            part = spectrum[plane][:, c * M : (c + 1) * M]
            spec_ref[plane, c, :F] = part
            spec_ref[plane, c, F:] = part[:M]
            if c == 0:
                spec_ref[plane, columns, :F] = part
                spec_ref[plane, columns, F:] = part[:M]
    extract([js], [out_ref], me_ref, fo_ref, so_ref, spec_ref)


def extract_kernel(sends, me_ref, fo_ref, so_ref, spec_ref, *outs):
    outs = outs[-len(sends) :]
    extract(sends, outs, me_ref, fo_ref, so_ref, spec_ref)


def extract(sends, outs, me_ref, fo_ref, so_ref, spec_ref):
    pc, ps = phase_taper(fo_ref)
    me = me_ref[0]

    def block(out_ref, item, j):
        owner = j ^ me
        sx, sy = so_ref[0, owner], so_ref[1, owner]
        lane = sy // M
        shift = (2 * M - (sy & (M - 1))) & (2 * M - 1)
        parts = []
        for plane in range(2):
            left = spec_ref[plane, lane, pl.ds(sx, M), :]
            right = spec_ref[plane, lane + 1, pl.ds(sx, M), :]
            wide = jnp.concatenate([left, right], axis=1)
            parts.append(pltpu.roll(wide, shift, 1)[:, :M])
        wr, wi = parts
        out_ref[item, 0] = (pc * wr - ps * wi).astype(BF)
        out_ref[item, 1] = (pc * wi + ps * wr).astype(BF)

    for out_ref, js in zip(outs, sends):
        for_blocks(block, out_ref, js)


def for_blocks(block, ref, js):
    step = js[1] - js[0] if len(js) > 1 else 1
    if len(js) > 1 and js == list(range(js[0], js[0] + step * len(js), step)):

        def body(item, carry):
            block(ref, item, item * step + js[0])
            return carry

        lax.fori_loop(0, len(js), body, 0)
    else:
        for item, j in enumerate(js):
            block(ref, item, j)


def band_kernel(to_ref, _, kt_hbm, kwide_hbm, kvt_ref, kv_ref, kut_ref, ku_ref, zero_ref, kt_ref, kwide_ref, sems):
    slots = kut_ref.shape[0]
    copies = [
        pltpu.make_async_copy(kt_hbm, kt_ref, sems.at[0]),
        pltpu.make_async_copy(kwide_hbm, kwide_ref, sems.at[1]),
    ]
    for copy in copies:
        copy.start()
    zero_ref[...] = jnp.zeros_like(zero_ref)
    for copy in copies:
        copy.wait()
    for t in range(slots):
        ou, ov = to_ref[0, t], to_ref[1, t]
        rows = slice(t * TV, (t + 1) * TV)
        kut_ref[t] = kt_ref[pl.ds(2 * TV - ou, SG), :].astype(BF)
        kvt_ref[:, rows] = kt_ref[pl.ds(2 * TV - ov, SG), :].astype(BF)
        ku_ref[rows] = pltpu.roll(kwide_ref[...], ou, 1).astype(BF)
        kv_ref[rows] = pltpu.roll(kwide_ref[...], ov, 1).astype(BF)


def screen_kernel(w_ref, _, *rest):
    loads = (len(rest) - 2) // 2
    sources, screen_ref = rest[:loads], rest[loads]
    targets, sems = rest[loads + 1 : -1], rest[-1]
    copies = [pltpu.make_async_copy(sources[k], targets[k], sems.at[k]) for k in range(loads)]
    for copy in copies:
        copy.start()
    w = w_ref[0, 0]
    row = lax.broadcasted_iota(jnp.int32, (SG, 1), 0).astype(F32) - SG / 2.0
    column = lax.broadcasted_iota(jnp.int32, (1, SG), 1).astype(F32) - SG / 2.0
    row2 = row * row * (1.0 / (SG * SG)) + 1.0
    column2 = column * column * (1.0 / (SG * SG))
    cos_v, sin_v = cos_sin_turns((jnp.sqrt(row2 + column2) - 1.0) * w)
    screen_ref[0] = cos_v
    screen_ref[1] = sin_v
    for copy in copies:
        copy.wait()


def subgrid_kernel(picks, tc_ref, *rest):
    parts = len(picks)
    sums = rest[:parts]
    (obs_ref, pad_ref, padt_ref, screen_ref, kvt_ref, kv_ref, kut_ref, ku_ref) = rest[parts : parts + 8]
    (out_ref, coef_ref, model_ref, rows_ref, z_ref, res_ref, sems) = rest[parts + 8 :]
    slots = obs_ref.shape[0]
    count = tc_ref[0, 0]

    def total(plane):
        value = sums[0][picks[0], plane].astype(F32)
        for ref, item in zip(sums[1:], picks[1:]):
            value = value + ref[item, plane].astype(F32)
        return value.astype(BF)

    pr, pi = pad_ref[0], pad_ref[1]
    inner_r, inner_i = mul_right(pr, pi, total(0), total(1))
    tr, ti = padt_ref[0], padt_ref[1]
    image_r, image_i = mul_left(inner_r.astype(BF), inner_i.astype(BF), tr, ti)
    sc, ss = screen_ref[0], screen_ref[1]
    model_ref[:SG] = (sc * image_r - ss * image_i).astype(BF)
    model_ref[SG:] = (sc * image_i + ss * image_r).astype(BF)

    model = model_ref[...]
    for t0 in range(0, slots, 2):
        pair = dot(model, kvt_ref[:, t0 * TV : (t0 + 2) * TV]).astype(BF)
        for t in (t0, t0 + 1):
            lanes = slice((t - t0) * TV, (t - t0 + 1) * TV)
            rows_ref[:, 2 * t * TV : (2 * t + 1) * TV] = pair[:SG, lanes]
            rows_ref[:, (2 * t + 1) * TV : (2 * t + 2) * TV] = pair[SG:, lanes]
    copies = []
    for t in range(slots):
        predicted = dot(ku_ref[t * TV : (t + 1) * TV], rows_ref[:, 2 * t * TV : (2 * t + 2) * TV])
        live = count > t
        for plane in range(2):
            value = obs_ref[t, plane].astype(F32) - predicted[:, plane * TV : (plane + 1) * TV]
            res_ref[t, plane] = jnp.where(live, value, 0.0).astype(BF)
        if t % 4 == 3:
            copies.append(
                pltpu.make_async_copy(
                    res_ref.at[pl.ds(t - 3, 4)], out_ref.at[pl.ds(t - 3, 4)], sems.at[t // 4]
                )
            )
            copies[-1].start()
    for t in range(slots):
        z = dot(kut_ref[t], jnp.concatenate([res_ref[t, 0], res_ref[t, 1]], axis=1)).astype(BF)
        z_ref[:SG, t * TV : (t + 1) * TV] = z[:, :TV]
        z_ref[SG:, t * TV : (t + 1) * TV] = z[:, TV:]

    kv = kv_ref[...]
    ar = dot(z_ref[:SG], kv)
    ai = dot(z_ref[SG:], kv)
    screened_r = (sc * ar + ss * ai).astype(BF)
    screened_i = (sc * ai - ss * ar).astype(BF)
    reduced_r, reduced_i = mul_right(tr, -ti, screened_r, screened_i)
    coef_r, coef_i = mul_left(reduced_r.astype(BF), reduced_i.astype(BF), pr, -pi)
    coef_ref[0, 0] = coef_r.astype(BF)
    coef_ref[0, 1] = coef_i.astype(BF)
    for copy in copies:
        copy.wait()


def grid_blocks(pieces, refs, me_ref, fo_ref, so_ref, grid_ref):
    pc, ps = phase_taper(fo_ref)
    me = me_ref[0]
    blank = jnp.zeros((M, M), F32)

    def block(in_ref, item, j):
        owner = j ^ me
        sx, sy = so_ref[0, owner], so_ref[1, owner]
        lane = sy // M
        shift = sy & (M - 1)
        cr, ci = in_ref[item, 0].astype(F32), in_ref[item, 1].astype(F32)
        values = (pc * cr + ps * ci, pc * ci - ps * cr)
        for plane in range(2):
            wide = pltpu.roll(jnp.concatenate([values[plane], blank], axis=1), shift, 1)
            grid_ref[plane, lane, pl.ds(sx, M), :] += wide[:, :M]
            grid_ref[plane, lane + 1, pl.ds(sx, M), :] += wide[:, M:]

    for in_ref, js in zip(refs, pieces):
        for_blocks(block, in_ref, js)


def first_grid_kernel(pieces, me_ref, fo_ref, so_ref, basis_hbm, *rest):
    grid_ref, zero_ref, basis_ref, sem = rest[-4:]
    load = pltpu.make_async_copy(basis_hbm, basis_ref, sem)
    load.start()
    zero_ref[...] = jnp.zeros_like(zero_ref)
    grid_ref[...] = jnp.zeros_like(grid_ref)
    grid_blocks(pieces, rest[:-4], me_ref, fo_ref, so_ref, grid_ref)
    load.wait()


def next_grid_kernel(pieces, me_ref, fo_ref, so_ref, *rest):
    grid_blocks(pieces, rest[:-2], me_ref, fo_ref, so_ref, rest[-2])


def backward_kernel(pieces, me_ref, fo_ref, so_ref, basis_ref, *rest):
    grid_ref, out_ref, _, out_buf, sems = rest[len(pieces) :]
    grid_blocks(pieces, rest[: len(pieces)], me_ref, fo_ref, so_ref, grid_ref)
    columns = F // M
    folded = []
    for plane in range(2):
        strips = []
        for c in range(columns):
            strip = grid_ref[plane, c]
            if c == 0:
                strip = strip + grid_ref[plane, columns]
            top = strip[:M] + strip[F:]
            strips.append(jnp.concatenate([top.astype(BF), strip[M:F].astype(BF)], axis=0))
        folded.append(jnp.concatenate(strips, axis=1))
    br, bi = basis_ref[0], basis_ref[1]
    hr, hi = mul_right(br, -bi, *folded)
    hr, hi = hr.astype(BF), hi.astype(BF)
    size = F // OUT_CHUNKS
    copies = []
    for k in range(OUT_CHUNKS):
        rows = slice(k * size, (k + 1) * size)
        real, imag = mul_left(hr[rows], hi[rows], br, -bi)
        for plane, value in enumerate((real, imag)):
            out_buf[plane, rows] = value.astype(BF)
            copy = pltpu.make_async_copy(
                out_buf.at[plane, pl.ds(k * size, size)],
                out_ref.at[0, plane, pl.ds(k * size, size)],
                sems.at[2 * k + plane],
            )
            copy.start()
            copies.append(copy)
    for copy in copies:
        copy.wait()


SMEM = pl.BlockSpec(memory_space=pltpu.SMEM)
VMEM = pl.BlockSpec(memory_space=pltpu.VMEM)
ANY = pl.BlockSpec(memory_space=pl.ANY)


def params(mib):
    return pltpu.CompilerParams(vmem_limit_bytes=mib * 1024 * 1024)


def near(value):
    return pltpu.with_memory_space_constraint(value, pltpu.VMEM)


def far(value):
    return pltpu.with_memory_space_constraint(value, pltpu.HBM)


def held(shape, dtype=BF):
    return pltpu.VMEM(shape, dtype)


def exchange(value, mask, n):
    return lax.ppermute(value, "facet", [(i, i ^ mask) for i in range(n)])


def digit_levels(n):
    levels, base = [], 1
    while base < n:
        radix = 2 if base < 4 or n // base < 4 else 4
        levels.append((base, radix))
        base *= radix
    return levels


def reduce_sends(n):
    sends = []
    for base, radix in digit_levels(n):
        for g in range(1, radix):
            js = [j for j in range(0, n, base) if (j // base) % radix == g]
            groups = [js[1::2], js[::2]] if base == 1 else [js]
            sends += [(group, g * base) for group in groups]
    return sends


def pick(value, items):
    step = items[1] - items[0] if len(items) > 1 else 1
    if items == list(range(items[0], items[0] + step * len(items), step)):
        if len(items) == value.shape[0]:
            return value
        return lax.slice_in_dim(value, items[0], items[-1] + 1, step)
    return jnp.concatenate([value[i : i + 1] for i in items])


def join(pieces):
    return [j for js, _ in pieces for j in js], jnp.concatenate([value for _, value in pieces])


def per_device(facets, facet_offsets, subgrid_offsets, w_terms, tile_count, tile_offsets, observed):
    n = lax.axis_size("facet")
    slots = observed.shape[0]
    me = lax.axis_index("facet").astype(jnp.int32).reshape(1)
    corners = far(subgrid_offsets.T)
    tile_corners = far(tile_offsets.T)
    facet_offsets = far(facet_offsets)
    basis = far(jnp.asarray(basis_tables()))
    pad_np = padding_tables(n)
    kern_np = kernel_table()
    kt_np = np.zeros((6 * TV, TV), np.float32)
    kt_np[2 * TV : 4 * TV] = kern_np.astype(np.float32).T
    kwide_np = np.zeros((TV, SG), np.float32)
    kwide_np[:, : 2 * TV] = kern_np.astype(np.float32)
    grid_shape = (2, F // M + 1, F + M, M)

    sends = reduce_sends(n)
    first, spec = pl.pallas_call(
        functools.partial(forward_kernel, sends[0][0]),
        out_shape=[held((len(sends[0][0]), 2, M, M)), held(grid_shape, F32)],
        in_specs=[SMEM] + [ANY] * 4,
        out_specs=[VMEM] * 2,
        scratch_shapes=[
            pltpu.VMEM((2, F, F), BF),
            pltpu.VMEM((2, F, F), BF),
            pltpu.SMEM(facet_offsets.shape, jnp.int32),
            pltpu.SMEM(corners.shape, jnp.int32),
            pltpu.SemaphoreType.DMA((6,)),
        ],
        compiler_params=params(16),
        name="forward",
    )(me, facet_offsets, corners, far(facets), basis)
    def make_blocks(lists, after):
        return pl.pallas_call(
            functools.partial(extract_kernel, lists),
            out_shape=[held((len(js), 2, M, M)) for js in lists],
            in_specs=[SMEM] * 3 + [VMEM] * (1 + len(after)),
            out_specs=[VMEM] * len(lists),
            compiler_params=params(8),
            name="extract",
        )(me, facet_offsets, corners, near(spec), *[near(value) for value in after])

    def make_bands(after):
        big = held((slots * TV, SG))
        return pl.pallas_call(
            band_kernel,
            out_shape=[held((SG, slots * TV)), big, held((slots, SG, TV)), big, held((1, M), F32)],
            in_specs=[SMEM, VMEM] + [ANY] * 2,
            out_specs=[VMEM] * 5,
            scratch_shapes=[
                pltpu.VMEM(kt_np.shape, F32),
                pltpu.VMEM(kwide_np.shape, F32),
                pltpu.SemaphoreType.DMA((2,)),
            ],
            compiler_params=params(8),
            name="bands",
        )(tile_corners, near(after), far(jnp.asarray(kt_np)), far(jnp.asarray(kwide_np)))

    def make_screen(after):
        loads = [observed, pad_np, pad_np.transpose(0, 2, 1), subgrid_offsets.T, facet_offsets]
        return pl.pallas_call(
            screen_kernel,
            out_shape=[held((2, SG, SG), F32)] + [held(load.shape, load.dtype) for load in loads],
            in_specs=[SMEM, VMEM] + [ANY] * len(loads),
            out_specs=[VMEM] * (1 + len(loads)),
            scratch_shapes=[pltpu.SemaphoreType.DMA((len(loads),))],
            compiler_params=params(8),
            name="screen",
        )(w_terms.reshape(1, 1), near(after), *[far(jnp.asarray(load)) for load in loads])

    arrived = []

    def send(js, mask, value, token=None):
        total = value.astype(F32)
        if token is not None:
            total = total + token
        for got_js, got in arrived:
            if set(js) <= set(got_js):
                total = total + pick(got, [got_js.index(j) for j in js]).astype(F32)
            else:
                assert not set(js) & set(got_js)
        value = total.astype(BF)
        arrived.append(([j ^ mask for j in js], exchange(value, mask, n)))
        return value

    (urgent, _), (lazy, _), (beside, _) = sends[:3]
    send(urgent, 1, first)
    beside_own, lazy_own = make_blocks([beside, lazy], [])
    value = send(beside, 2, beside_own)
    send(lazy, 1, lazy_own)
    own = make_blocks([js for js, _ in sends[3:]] + [[0]], [value])
    kvt, kv, kut, ku, token = make_bands(value)
    for (js, mask), value in zip(sends[3:], own):
        value = send(js, mask, value, token)
    screen, tiles, pad, padt, corners, facet_offsets = make_screen(value)
    corners, facet_offsets = near(corners), near(facet_offsets)
    last = [(js, got) for js, got in arrived if 0 in js]

    residual, coefficient = pl.pallas_call(
        functools.partial(subgrid_kernel, [0] + [js.index(0) for js, _ in last]),
        out_shape=[pltpu.HBM(observed.shape, BF), held((1, 2, M, M))],
        in_specs=[SMEM] + [VMEM] * (len(last) + 9),
        out_specs=[ANY, VMEM],
        scratch_shapes=[
            pltpu.VMEM((2 * SG, SG), BF),
            pltpu.VMEM((SG, 2 * slots * TV), BF),
            pltpu.VMEM((2 * SG, slots * TV), BF),
            pltpu.VMEM(observed.shape, BF),
            pltpu.SemaphoreType.DMA((slots // 4,)),
        ],
        compiler_params=params(24),
        name="subgrid",
    )(
        tile_count.reshape(1, 1),
        near(own[-1]),
        *[near(got) for _, got in last],
        *[near(value) for value in (tiles, pad, padt, screen, kvt, kv, kut, ku)],
    )

    early = ([0], coefficient)
    for base, radix in reversed(digit_levels(n)[2:]):
        js, value = early
        more = [([j ^ (g * base) for j in js], exchange(value, g * base, n)) for g in range(1, radix)]
        early_parts = [join([early, more[0]]), join(more[1:])]
        early = join(early_parts)

    def hop(part, mask):
        return [j ^ mask for j in part[0]], exchange(part[1], mask, n)

    a, b = early_parts
    late_a, late_b = hop(a, 2), hop(b, 2)
    ready = [a, b, hop(a, 1), hop(b, 1)]
    grid, token, basis_near = pl.pallas_call(
        functools.partial(first_grid_kernel, [js for js, _ in ready]),
        out_shape=[held(grid_shape, F32), held((1, M), F32), held(basis.shape)],
        in_specs=[SMEM] * 3 + [ANY] + [VMEM] * len(ready),
        out_specs=[VMEM] * 3,
        scratch_shapes=[pltpu.SemaphoreType.DMA(())],
        compiler_params=params(8),
        name="grid_first",
    )(me, facet_offsets, corners, basis, *[near(value) for _, value in ready])
    late_a_other = hop(late_a, 1)
    late_b = (late_b[0], (late_b[1].astype(F32) + token).astype(BF))
    late_b_other = hop(late_b, 1)
    ready = [late_a, late_a_other, late_b]
    grid = pl.pallas_call(
        functools.partial(next_grid_kernel, [js for js, _ in ready]),
        out_shape=held(grid_shape, F32),
        in_specs=[SMEM] * 3 + [VMEM] * (len(ready) + 1),
        out_specs=VMEM,
        input_output_aliases={3 + len(ready): 0},
        compiler_params=params(8),
        name="grid_next",
    )(me, facet_offsets, corners, *[near(value) for _, value in ready], near(grid))
    update = pl.pallas_call(
        functools.partial(backward_kernel, [late_b_other[0]]),
        out_shape=[pltpu.HBM(facets.shape, BF), held(grid_shape, F32)],
        in_specs=[SMEM] * 3 + [VMEM] * 3,
        out_specs=[ANY, VMEM],
        input_output_aliases={5: 1},
        scratch_shapes=[
            pltpu.VMEM((2, F, F), BF),
            pltpu.SemaphoreType.DMA((2 * OUT_CHUNKS,)),
        ],
        compiler_params=params(16),
        name="backward",
    )(me, facet_offsets, corners, near(basis_near), near(late_b_other[1]), near(grid))[0]
    return (residual, update)


def solution(mesh):
    placed = (
        P(("groups", "facet"), None, None, None),
        P(("groups", "facet"), None),
        P("groups", None),
        P(("groups", "facet")),
        P(("groups", "facet")),
        P(("groups", "facet"), None),
        P(("groups", "facet"), None, None, None),
    )
    return jax.shard_map(
        per_device,
        mesh=mesh,
        in_specs=placed,
        out_specs=(
            P(("groups", "facet"), None, None, None),
            P(("groups", "facet"), None, None, None),
        ),
        check_vma=False,
    )
```

```python
import functools
import math

import jax
import jax.numpy as jnp
import ml_dtypes
import numpy as np
from jax import lax
from jax.experimental import pallas as pl
from jax.experimental.pallas import tpu as pltpu
from jax.sharding import PartitionSpec as P

F = 512
M = 128
SG = 512
TV = 128
BF = jnp.bfloat16
F32 = jnp.float32
TWO_PI = 2.0 * math.pi
OUT_CHUNKS = 4


def basis_tables():
    index = np.arange(F, dtype=np.int64)
    angle = -TWO_PI * ((index[:, None] * index[None, :]) % F) / F
    table = np.stack([np.cos(angle), np.sin(angle)]) / math.sqrt(F)
    return table.astype(ml_dtypes.bfloat16)


def padding_tables(facet_count):
    product = (np.arange(SG)[:, None] * np.arange(M)[None, :]) % SG
    angle = TWO_PI * product / SG
    scale = (M * math.sqrt(facet_count)) ** (-0.5)
    table = np.stack([np.cos(angle), np.sin(angle)]) * scale
    return table.astype(ml_dtypes.bfloat16)


def kernel_table():
    rows = np.arange(TV, dtype=np.float64)[:, None]
    columns = np.arange(2 * TV, dtype=np.float64)[None, :]
    distance = columns - 2.0 * rows - 1.0
    value = 0.75 * np.exp(-((distance / 1.5) ** 2))
    return np.where(np.abs(distance) <= 4.0, value, 0.0).astype(ml_dtypes.bfloat16)


def taper_square():
    position = np.arange(M, dtype=np.float64)
    taper = 0.6 + 0.4 * np.sin(math.pi * (position + 0.5) / M)
    return (taper[:, None] * taper[None, :]).astype(np.float32)


def turn_polynomials():
    nodes = 0.5 * np.cos(math.pi * (np.arange(400) + 0.5) / 800)
    square = nodes * nodes
    powers = np.stack([square**k for k in range(8)], axis=1)
    cos_c = np.linalg.lstsq(powers, np.cos(TWO_PI * nodes), rcond=None)[0]
    sin_c = np.linalg.lstsq(powers, np.sin(TWO_PI * nodes) / nodes, rcond=None)[0]
    return [float(c) for c in cos_c], [float(c) for c in sin_c]


COS_C, SIN_C = turn_polynomials()


def cos_sin_turns(turns):
    rest = turns - jnp.floor(turns + 0.5)
    square = rest * rest
    cos_v = jnp.full_like(square, COS_C[7])
    sin_v = jnp.full_like(square, SIN_C[7])
    for k in range(6, -1, -1):
        cos_v = cos_v * square + COS_C[k]
        sin_v = sin_v * square + SIN_C[k]
    return cos_v, sin_v * rest


def dot(left, right):
    return jnp.dot(left, right, preferred_element_type=F32)


def dot_nt(left, right):
    return lax.dot_general(left, right, (((1,), (1,)), ((), ())), preferred_element_type=F32)


def mul_left(left_r, left_i, right_r, right_i):
    left = jnp.concatenate([left_r, left_i], axis=1)
    real = dot(left, jnp.concatenate([right_r, -right_i], axis=0))
    imag = dot(left, jnp.concatenate([right_i, right_r], axis=0))
    return real, imag


def mul_right(left_r, left_i, right_r, right_i):
    right = jnp.concatenate([right_r, right_i], axis=0)
    real = dot(jnp.concatenate([left_r, -left_i], axis=1), right)
    imag = dot(jnp.concatenate([left_i, left_r], axis=1), right)
    return real, imag


def phase_taper(fo_ref):
    rows = lax.broadcasted_iota(jnp.int32, (M, M), 0)
    columns = lax.broadcasted_iota(jnp.int32, (M, M), 1)
    total = (rows * fo_ref[0, 0] + columns * fo_ref[0, 1]) & (F - 1)
    cos_v, sin_v = cos_sin_turns(total.astype(F32) * (1.0 / F))
    row = lax.broadcasted_iota(jnp.int32, (M, 1), 0).astype(F32)
    column = lax.broadcasted_iota(jnp.int32, (1, M), 1).astype(F32)
    _, row_sin = cos_sin_turns((row + 0.5) * (0.5 / M))
    _, column_sin = cos_sin_turns((column + 0.5) * (0.5 / M))
    taper2 = (0.6 + 0.4 * row_sin) * (0.6 + 0.4 * column_sin)
    return cos_v * taper2, sin_v * taper2


def forward_kernel(js, me_ref, fo_hbm, so_hbm, facet_ref, basis_ref, out_ref, spec_ref, *rest):
    facet_buf, basis_buf, fo_ref, so_ref, sems = rest
    copies = [
        pltpu.make_async_copy(fo_hbm, fo_ref, sems.at[4]),
        pltpu.make_async_copy(so_hbm, so_ref, sems.at[5]),
    ]
    for k in range(2):
        copies.append(pltpu.make_async_copy(basis_ref.at[k], basis_buf.at[k], sems.at[2 * k]))
        copies.append(pltpu.make_async_copy(facet_ref.at[0, k], facet_buf.at[k], sems.at[2 * k + 1]))
    for copy in copies:
        copy.start()
    for copy in copies[:2]:
        copy.wait()
    phase = phase_taper(fo_ref)
    for copy in copies[2:]:
        copy.wait()
    br, bi = basis_buf[0], basis_buf[1]
    hr, hi = mul_left(facet_buf[0], facet_buf[1], br, bi)
    spectrum = mul_right(br, bi, hr.astype(BF), hi.astype(BF))
    columns = F // M
    for plane in range(2):
        for c in range(columns):
            part = spectrum[plane][:, c * M : (c + 1) * M]
            spec_ref[plane, c, :F] = part
            spec_ref[plane, c, F:] = part[:M]
            if c == 0:
                spec_ref[plane, columns, :F] = part
                spec_ref[plane, columns, F:] = part[:M]
    extract([js], [out_ref], me_ref, phase, so_ref, spec_ref)


def extract_kernel(sends, me_ref, fo_ref, so_ref, spec_ref, *outs):
    outs = outs[-len(sends) :]
    extract(sends, outs, me_ref, phase_taper(fo_ref), so_ref, spec_ref)


def extract(sends, outs, me_ref, phase, so_ref, spec_ref):
    pc, ps = phase
    me = me_ref[0]

    def block(out_ref, item, j):
        owner = j ^ me
        sx, sy = so_ref[0, owner], so_ref[1, owner]
        lane = sy // M
        shift = (2 * M - (sy & (M - 1))) & (2 * M - 1)
        parts = []
        for plane in range(2):
            left = spec_ref[plane, lane, pl.ds(sx, M), :]
            right = spec_ref[plane, lane + 1, pl.ds(sx, M), :]
            wide = jnp.concatenate([left, right], axis=1)
            parts.append(pltpu.roll(wide, shift, 1)[:, :M])
        wr, wi = parts
        out_ref[item, 0] = (pc * wr - ps * wi).astype(BF)
        out_ref[item, 1] = (pc * wi + ps * wr).astype(BF)

    for out_ref, js in zip(outs, sends):
        for_blocks(block, out_ref, js)


def for_blocks(block, ref, js):
    step = js[1] - js[0] if len(js) > 1 else 1
    if len(js) > 1 and js == list(range(js[0], js[0] + step * len(js), step)):

        def body(item, carry):
            block(ref, item, item * step + js[0])
            return carry

        lax.fori_loop(0, len(js), body, 0)
    else:
        for item, j in enumerate(js):
            block(ref, item, j)


def band_kernel(to_ref, _, kt_hbm, kwide_hbm, kvt_ref, kut_ref, ku_ref, zero_ref, kt_ref, kwide_ref, sems):
    slots = kut_ref.shape[0]
    copies = [
        pltpu.make_async_copy(kt_hbm, kt_ref, sems.at[0]),
        pltpu.make_async_copy(kwide_hbm, kwide_ref, sems.at[1]),
    ]
    for copy in copies:
        copy.start()
    zero_ref[...] = jnp.zeros_like(zero_ref)
    for copy in copies:
        copy.wait()
    for t in range(slots):
        ou, ov = to_ref[0, t], to_ref[1, t]
        rows = slice(t * TV, (t + 1) * TV)
        kut_ref[t] = kt_ref[pl.ds(2 * TV - ou, SG), :].astype(BF)
        kvt_ref[:, rows] = kt_ref[pl.ds(2 * TV - ov, SG), :].astype(BF)
        ku_ref[rows] = pltpu.roll(kwide_ref[...], ou, 1).astype(BF)


def screen_kernel(w_ref, _, *rest):
    loads = (len(rest) - 3) // 2
    sources, screen_ref = rest[:loads], rest[loads]
    targets, zero_ref, sems = rest[loads + 1 : -2], rest[-2], rest[-1]
    zero_ref[...] = jnp.zeros_like(zero_ref)
    copies = [pltpu.make_async_copy(sources[k], targets[k], sems.at[k]) for k in range(loads)]
    for copy in copies:
        copy.start()
    w = w_ref[0, 0]
    row = lax.broadcasted_iota(jnp.int32, (SG, 1), 0).astype(F32) - SG / 2.0
    column = lax.broadcasted_iota(jnp.int32, (1, SG), 1).astype(F32) - SG / 2.0
    row2 = row * row * (1.0 / (SG * SG)) + 1.0
    column2 = column * column * (1.0 / (SG * SG))
    cos_v, sin_v = cos_sin_turns((jnp.sqrt(row2 + column2) - 1.0) * w)
    screen_ref[0] = cos_v
    screen_ref[1] = sin_v
    for copy in copies:
        copy.wait()


def subgrid_kernel(picks, tc_ref, *rest):
    parts = len(picks)
    sums = rest[:parts]
    (obs_ref, pad_ref, padt_ref, screen_ref, kvt_ref, kut_ref, ku_ref) = rest[parts : parts + 7]
    (out_ref, coef_ref, model_ref, rows_ref, z_ref, res_ref, sems) = rest[parts + 7 :]
    slots = obs_ref.shape[0]
    count = tc_ref[0, 0]

    def total(plane):
        value = sums[0][picks[0], plane].astype(F32)
        for ref, item in zip(sums[1:], picks[1:]):
            value = value + ref[item, plane].astype(F32)
        return value.astype(BF)

    pr, pi = pad_ref[0], pad_ref[1]
    inner_r, inner_i = mul_right(pr, pi, total(0), total(1))
    tr, ti = padt_ref[0], padt_ref[1]
    image_r, image_i = mul_left(inner_r.astype(BF), inner_i.astype(BF), tr, ti)
    sc, ss = screen_ref[0], screen_ref[1]
    model_ref[:SG] = (sc * image_r - ss * image_i).astype(BF)
    model_ref[SG:] = (sc * image_i + ss * image_r).astype(BF)

    model = model_ref[...]
    for t0 in range(0, slots, 2):
        pair = dot(model, kvt_ref[:, t0 * TV : (t0 + 2) * TV]).astype(BF)
        for t in (t0, t0 + 1):
            lanes = slice((t - t0) * TV, (t - t0 + 1) * TV)
            rows_ref[:, 2 * t * TV : (2 * t + 1) * TV] = pair[:SG, lanes]
            rows_ref[:, (2 * t + 1) * TV : (2 * t + 2) * TV] = pair[SG:, lanes]
    copies = []
    for t in range(slots):
        predicted = dot(ku_ref[t * TV : (t + 1) * TV], rows_ref[:, 2 * t * TV : (2 * t + 2) * TV])
        live = count > t
        for plane in range(2):
            value = obs_ref[t, plane].astype(F32) - predicted[:, plane * TV : (plane + 1) * TV]
            res_ref[t, plane] = jnp.where(live, value, 0.0).astype(BF)
        if t % 4 == 3:
            copies.append(
                pltpu.make_async_copy(
                    res_ref.at[pl.ds(t - 3, 4)], out_ref.at[pl.ds(t - 3, 4)], sems.at[t // 4]
                )
            )
            copies[-1].start()
    for t in range(slots):
        z = dot(kut_ref[t], jnp.concatenate([res_ref[t, 0], res_ref[t, 1]], axis=1)).astype(BF)
        z_ref[:SG, t * TV : (t + 1) * TV] = z[:, :TV]
        z_ref[SG:, t * TV : (t + 1) * TV] = z[:, TV:]

    kvt = kvt_ref[...]
    ar = dot_nt(z_ref[:SG], kvt)
    ai = dot_nt(z_ref[SG:], kvt)
    screened_r = (sc * ar + ss * ai).astype(BF)
    screened_i = (sc * ai - ss * ar).astype(BF)
    reduced_r, reduced_i = mul_right(tr, -ti, screened_r, screened_i)
    coef_r, coef_i = mul_left(reduced_r.astype(BF), reduced_i.astype(BF), pr, -pi)
    coef_ref[0, 0] = coef_r.astype(BF)
    coef_ref[0, 1] = coef_i.astype(BF)
    for copy in copies:
        copy.wait()


def grid_blocks(pieces, refs, me_ref, fo_ref, so_ref, grid_ref):
    pc, ps = phase_taper(fo_ref)
    me = me_ref[0]
    blank = jnp.zeros((M, M), F32)

    def block(in_ref, item, j):
        owner = j ^ me
        sx, sy = so_ref[0, owner], so_ref[1, owner]
        lane = sy // M
        shift = sy & (M - 1)
        cr, ci = in_ref[item, 0].astype(F32), in_ref[item, 1].astype(F32)
        values = (pc * cr + ps * ci, pc * ci - ps * cr)
        for plane in range(2):
            wide = pltpu.roll(jnp.concatenate([values[plane], blank], axis=1), shift, 1)
            grid_ref[plane, lane, pl.ds(sx, M), :] += wide[:, :M]
            grid_ref[plane, lane + 1, pl.ds(sx, M), :] += wide[:, M:]

    for in_ref, js in zip(refs, pieces):
        for_blocks(block, in_ref, js)


def first_grid_kernel(pieces, me_ref, fo_ref, so_ref, basis_hbm, *rest):
    grid_ref, zero_ref, basis_ref, sem = rest[-4:]
    load = pltpu.make_async_copy(basis_hbm, basis_ref, sem)
    load.start()
    zero_ref[...] = jnp.zeros_like(zero_ref)
    grid_ref[...] = jnp.zeros_like(grid_ref)
    grid_blocks(pieces, rest[:-4], me_ref, fo_ref, so_ref, grid_ref)
    load.wait()


def next_grid_kernel(pieces, me_ref, fo_ref, so_ref, *rest):
    grid_blocks(pieces, rest[:-2], me_ref, fo_ref, so_ref, rest[-2])


def backward_kernel(pieces, me_ref, fo_ref, so_ref, basis_ref, *rest):
    grid_ref, out_ref, _, out_buf, sems = rest[len(pieces) :]
    grid_blocks(pieces, rest[: len(pieces)], me_ref, fo_ref, so_ref, grid_ref)
    columns = F // M
    folded = []
    for plane in range(2):
        strips = []
        for c in range(columns):
            strip = grid_ref[plane, c]
            if c == 0:
                strip = strip + grid_ref[plane, columns]
            top = strip[:M] + strip[F:]
            strips.append(jnp.concatenate([top.astype(BF), strip[M:F].astype(BF)], axis=0))
        folded.append(jnp.concatenate(strips, axis=1))
    br, bi = basis_ref[0], basis_ref[1]
    hr, hi = mul_right(br, -bi, *folded)
    hr, hi = hr.astype(BF), hi.astype(BF)
    size = F // OUT_CHUNKS
    copies = []
    for k in range(OUT_CHUNKS):
        rows = slice(k * size, (k + 1) * size)
        real, imag = mul_left(hr[rows], hi[rows], br, -bi)
        for plane, value in enumerate((real, imag)):
            out_buf[plane, rows] = value.astype(BF)
            copy = pltpu.make_async_copy(
                out_buf.at[plane, pl.ds(k * size, size)],
                out_ref.at[0, plane, pl.ds(k * size, size)],
                sems.at[2 * k + plane],
            )
            copy.start()
            copies.append(copy)
    for copy in copies:
        copy.wait()


SMEM = pl.BlockSpec(memory_space=pltpu.SMEM)
VMEM = pl.BlockSpec(memory_space=pltpu.VMEM)
ANY = pl.BlockSpec(memory_space=pl.ANY)


def params(mib):
    return pltpu.CompilerParams(vmem_limit_bytes=mib * 1024 * 1024)


def near(value):
    return pltpu.with_memory_space_constraint(value, pltpu.VMEM)


def far(value):
    return pltpu.with_memory_space_constraint(value, pltpu.HBM)


def held(shape, dtype=BF):
    return pltpu.VMEM(shape, dtype)


def exchange(value, mask, n):
    return lax.ppermute(value, "facet", [(i, i ^ mask) for i in range(n)])


def digit_levels(n):
    levels, base = [], 1
    while base < n:
        radix = 2 if base < 4 or n // base < 4 else 4
        levels.append((base, radix))
        base *= radix
    return levels


def reduce_sends(n):
    sends = []
    for base, radix in digit_levels(n):
        for g in range(1, radix):
            js = [j for j in range(0, n, base) if (j // base) % radix == g]
            groups = [js[1::2], js[::2]] if base == 1 else [js]
            sends += [(group, g * base) for group in groups]
    return sends


def pick(value, items):
    step = items[1] - items[0] if len(items) > 1 else 1
    if items == list(range(items[0], items[0] + step * len(items), step)):
        if len(items) == value.shape[0]:
            return value
        return lax.slice_in_dim(value, items[0], items[-1] + 1, step)
    return jnp.concatenate([value[i : i + 1] for i in items])


def join(pieces):
    return [j for js, _ in pieces for j in js], jnp.concatenate([value for _, value in pieces])


def per_device(facets, facet_offsets, subgrid_offsets, w_terms, tile_count, tile_offsets, observed):
    n = lax.axis_size("facet")
    slots = observed.shape[0]
    me = lax.axis_index("facet").astype(jnp.int32).reshape(1)
    corners = far(subgrid_offsets.T)
    tile_corners = far(tile_offsets.T)
    facet_offsets = far(facet_offsets)
    basis = far(jnp.asarray(basis_tables()))
    pad_np = padding_tables(n)
    kern_np = kernel_table()
    kt_np = np.zeros((6 * TV, TV), np.float32)
    kt_np[2 * TV : 4 * TV] = kern_np.astype(np.float32).T
    kwide_np = np.zeros((TV, SG), np.float32)
    kwide_np[:, : 2 * TV] = kern_np.astype(np.float32)
    grid_shape = (2, F // M + 1, F + M, M)

    sends = reduce_sends(n)
    first, spec = pl.pallas_call(
        functools.partial(forward_kernel, sends[0][0]),
        out_shape=[held((len(sends[0][0]), 2, M, M)), held(grid_shape, F32)],
        in_specs=[SMEM] + [ANY] * 4,
        out_specs=[VMEM] * 2,
        scratch_shapes=[
            pltpu.VMEM((2, F, F), BF),
            pltpu.VMEM((2, F, F), BF),
            pltpu.SMEM(facet_offsets.shape, jnp.int32),
            pltpu.SMEM(corners.shape, jnp.int32),
            pltpu.SemaphoreType.DMA((6,)),
        ],
        compiler_params=params(16),
        name="forward",
    )(me, facet_offsets, corners, far(facets), basis)
    def make_blocks(lists, after):
        return pl.pallas_call(
            functools.partial(extract_kernel, lists),
            out_shape=[held((len(js), 2, M, M)) for js in lists],
            in_specs=[SMEM] * 3 + [VMEM] * (1 + len(after)),
            out_specs=[VMEM] * len(lists),
            compiler_params=params(8),
            name="extract",
        )(me, facet_offsets, corners, near(spec), *[near(value) for value in after])

    def make_bands(after):
        return pl.pallas_call(
            band_kernel,
            out_shape=[
                held((SG, slots * TV)),
                held((slots, SG, TV)),
                held((slots * TV, SG)),
                held((1, M), F32),
            ],
            in_specs=[SMEM, VMEM] + [ANY] * 2,
            out_specs=[VMEM] * 4,
            scratch_shapes=[
                pltpu.VMEM(kt_np.shape, F32),
                pltpu.VMEM(kwide_np.shape, F32),
                pltpu.SemaphoreType.DMA((2,)),
            ],
            compiler_params=params(8),
            name="bands",
        )(tile_corners, near(after), far(jnp.asarray(kt_np)), far(jnp.asarray(kwide_np)))

    def make_screen(after):
        loads = [observed, pad_np, pad_np.transpose(0, 2, 1), subgrid_offsets.T, facet_offsets]
        return pl.pallas_call(
            screen_kernel,
            out_shape=[held((2, SG, SG), F32)] + [held(load.shape, load.dtype) for load in loads] + [held((1, M), F32)],
            in_specs=[SMEM, VMEM] + [ANY] * len(loads),
            out_specs=[VMEM] * (2 + len(loads)),
            scratch_shapes=[pltpu.SemaphoreType.DMA((len(loads),))],
            compiler_params=params(8),
            name="screen",
        )(w_terms.reshape(1, 1), near(after), *[far(jnp.asarray(load)) for load in loads])

    arrived = []

    def send(js, mask, value, token=None):
        total = value.astype(F32)
        if token is not None:
            total = total + token
        for got_js, got in arrived:
            if set(js) <= set(got_js):
                total = total + pick(got, [got_js.index(j) for j in js]).astype(F32)
            else:
                assert not set(js) & set(got_js)
        value = total.astype(BF)
        arrived.append(([j ^ mask for j in js], exchange(value, mask, n)))
        return value

    (urgent, _), (lazy, _), (beside, _) = sends[:3]
    send(urgent, 1, first)
    beside_own, lazy_own = make_blocks([beside, lazy], [])
    value = send(beside, 2, beside_own)
    send(lazy, 1, lazy_own)
    own = make_blocks([js for js, _ in sends[3:]] + [[0]], [value])
    kvt, kut, ku, token = make_bands(value)
    screen, tiles, pad, padt, late_corners, late_facet_offsets, token = make_screen(token)
    for (js, mask), value in zip(sends[3:], own):
        value = send(js, mask, value, token)
    corners, facet_offsets = near(late_corners), near(late_facet_offsets)
    last = [(js, got) for js, got in arrived if 0 in js]

    residual, coefficient = pl.pallas_call(
        functools.partial(subgrid_kernel, [0] + [js.index(0) for js, _ in last]),
        out_shape=[pltpu.HBM(observed.shape, BF), held((1, 2, M, M))],
        in_specs=[SMEM] + [VMEM] * (len(last) + 8),
        out_specs=[ANY, VMEM],
        scratch_shapes=[
            pltpu.VMEM((2 * SG, SG), BF),
            pltpu.VMEM((SG, 2 * slots * TV), BF),
            pltpu.VMEM((2 * SG, slots * TV), BF),
            pltpu.VMEM(observed.shape, BF),
            pltpu.SemaphoreType.DMA((slots // 4,)),
        ],
        compiler_params=params(24),
        name="subgrid",
    )(
        tile_count.reshape(1, 1),
        near(own[-1]),
        *[near(got) for _, got in last],
        *[near(value) for value in (tiles, pad, padt, screen, kvt, kut, ku)],
    )

    early = ([0], coefficient)
    for base, radix in reversed(digit_levels(n)[2:]):
        js, value = early
        more = [([j ^ (g * base) for j in js], exchange(value, g * base, n)) for g in range(1, radix)]
        early = join([early] + more)

    def hop(part, mask):
        return [j ^ mask for j in part[0]], exchange(part[1], mask, n)

    late = hop(early, 2)
    ready = [early, hop(early, 1)]
    grid, token, basis_near = pl.pallas_call(
        functools.partial(first_grid_kernel, [js for js, _ in ready]),
        out_shape=[held(grid_shape, F32), held((1, M), F32), held(basis.shape)],
        in_specs=[SMEM] * 3 + [ANY] + [VMEM] * len(ready),
        out_specs=[VMEM] * 3,
        scratch_shapes=[pltpu.SemaphoreType.DMA(())],
        compiler_params=params(8),
        name="grid_first",
    )(me, facet_offsets, corners, basis, *[near(value) for _, value in ready])
    late = (late[0], (late[1].astype(F32) + token).astype(BF))
    late_other = hop(late, 1)
    ready = [late]
    grid = pl.pallas_call(
        functools.partial(next_grid_kernel, [js for js, _ in ready]),
        out_shape=held(grid_shape, F32),
        in_specs=[SMEM] * 3 + [VMEM] * (len(ready) + 1),
        out_specs=VMEM,
        input_output_aliases={3 + len(ready): 0},
        compiler_params=params(8),
        name="grid_next",
    )(me, facet_offsets, corners, *[near(value) for _, value in ready], near(grid))
    update = pl.pallas_call(
        functools.partial(backward_kernel, [late_other[0]]),
        out_shape=[pltpu.HBM(facets.shape, BF), held(grid_shape, F32)],
        in_specs=[SMEM] * 3 + [VMEM] * 3,
        out_specs=[ANY, VMEM],
        input_output_aliases={5: 1},
        scratch_shapes=[
            pltpu.VMEM((2, F, F), BF),
            pltpu.SemaphoreType.DMA((2 * OUT_CHUNKS,)),
        ],
        compiler_params=params(16),
        name="backward",
    )(me, facet_offsets, corners, near(basis_near), near(late_other[1]), near(grid))[0]
    return (residual, update)


def solution(mesh):
    placed = (
        P(("groups", "facet"), None, None, None),
        P(("groups", "facet"), None),
        P("groups", None),
        P(("groups", "facet")),
        P(("groups", "facet")),
        P(("groups", "facet"), None),
        P(("groups", "facet"), None, None, None),
    )
    return jax.shard_map(
        per_device,
        mesh=mesh,
        in_specs=placed,
        out_specs=(
            P(("groups", "facet"), None, None, None),
            P(("groups", "facet"), None, None, None),
        ),
        check_vma=False,
    )
```

```python
import functools
import math

import jax
import jax.numpy as jnp
import ml_dtypes
import numpy as np
from jax import lax
from jax.experimental import pallas as pl
from jax.experimental.pallas import tpu as pltpu
from jax.sharding import PartitionSpec as P

F = 512
M = 128
SG = 512
TV = 128
BF = jnp.bfloat16
F32 = jnp.float32
TWO_PI = 2.0 * math.pi
OUT_CHUNKS = 4


def basis_tables():
    index = np.arange(F, dtype=np.int64)
    angle = -TWO_PI * ((index[:, None] * index[None, :]) % F) / F
    table = np.stack([np.cos(angle), np.sin(angle)]) / math.sqrt(F)
    return table.astype(ml_dtypes.bfloat16)


def padding_tables(facet_count):
    product = (np.arange(SG)[:, None] * np.arange(M)[None, :]) % SG
    angle = TWO_PI * product / SG
    scale = (M * math.sqrt(facet_count)) ** (-0.5)
    table = np.stack([np.cos(angle), np.sin(angle)]) * scale
    return table.astype(ml_dtypes.bfloat16)


def kernel_table():
    rows = np.arange(TV, dtype=np.float64)[:, None]
    columns = np.arange(2 * TV, dtype=np.float64)[None, :]
    distance = columns - 2.0 * rows - 1.0
    value = 0.75 * np.exp(-((distance / 1.5) ** 2))
    return np.where(np.abs(distance) <= 4.0, value, 0.0).astype(ml_dtypes.bfloat16)


def taper_square():
    position = np.arange(M, dtype=np.float64)
    taper = 0.6 + 0.4 * np.sin(math.pi * (position + 0.5) / M)
    return (taper[:, None] * taper[None, :]).astype(np.float32)


def turn_polynomials():
    nodes = 0.5 * np.cos(math.pi * (np.arange(400) + 0.5) / 800)
    square = nodes * nodes
    powers = np.stack([square**k for k in range(8)], axis=1)
    cos_c = np.linalg.lstsq(powers, np.cos(TWO_PI * nodes), rcond=None)[0]
    sin_c = np.linalg.lstsq(powers, np.sin(TWO_PI * nodes) / nodes, rcond=None)[0]
    return [float(c) for c in cos_c], [float(c) for c in sin_c]


COS_C, SIN_C = turn_polynomials()


def cos_sin_turns(turns):
    rest = turns - jnp.floor(turns + 0.5)
    square = rest * rest
    cos_v = jnp.full_like(square, COS_C[7])
    sin_v = jnp.full_like(square, SIN_C[7])
    for k in range(6, -1, -1):
        cos_v = cos_v * square + COS_C[k]
        sin_v = sin_v * square + SIN_C[k]
    return cos_v, sin_v * rest


def dot(left, right):
    return jnp.dot(left, right, preferred_element_type=F32)


def dot_nt(left, right):
    return lax.dot_general(left, right, (((1,), (1,)), ((), ())), preferred_element_type=F32)


def mul_left(left_r, left_i, right_r, right_i):
    left = jnp.concatenate([left_r, left_i], axis=1)
    real = dot(left, jnp.concatenate([right_r, -right_i], axis=0))
    imag = dot(left, jnp.concatenate([right_i, right_r], axis=0))
    return real, imag


def mul_right(left_r, left_i, right_r, right_i):
    right = jnp.concatenate([right_r, right_i], axis=0)
    real = dot(jnp.concatenate([left_r, -left_i], axis=1), right)
    imag = dot(jnp.concatenate([left_i, left_r], axis=1), right)
    return real, imag


def phase_taper(fo_ref):
    rows = lax.broadcasted_iota(jnp.int32, (M, M), 0)
    columns = lax.broadcasted_iota(jnp.int32, (M, M), 1)
    total = (rows * fo_ref[0, 0] + columns * fo_ref[0, 1]) & (F - 1)
    cos_v, sin_v = cos_sin_turns(total.astype(F32) * (1.0 / F))
    row = lax.broadcasted_iota(jnp.int32, (M, 1), 0).astype(F32)
    column = lax.broadcasted_iota(jnp.int32, (1, M), 1).astype(F32)
    _, row_sin = cos_sin_turns((row + 0.5) * (0.5 / M))
    _, column_sin = cos_sin_turns((column + 0.5) * (0.5 / M))
    taper2 = (0.6 + 0.4 * row_sin) * (0.6 + 0.4 * column_sin)
    return cos_v * taper2, sin_v * taper2


def forward_kernel(js, me_ref, fo_hbm, so_hbm, facet_ref, basis_ref, out_ref, spec_ref, *rest):
    facet_buf, basis_buf, fo_ref, so_ref, sems = rest
    copies = [
        pltpu.make_async_copy(fo_hbm, fo_ref, sems.at[4]),
        pltpu.make_async_copy(so_hbm, so_ref, sems.at[5]),
    ]
    for k in range(2):
        copies.append(pltpu.make_async_copy(basis_ref.at[k], basis_buf.at[k], sems.at[2 * k]))
        copies.append(pltpu.make_async_copy(facet_ref.at[0, k], facet_buf.at[k], sems.at[2 * k + 1]))
    for copy in copies:
        copy.start()
    for copy in copies[:2]:
        copy.wait()
    phase = phase_taper(fo_ref)
    for copy in copies[2:]:
        copy.wait()
    br, bi = basis_buf[0], basis_buf[1]
    hr, hi = mul_left(facet_buf[0], facet_buf[1], br, bi)
    spectrum = mul_right(br, bi, hr.astype(BF), hi.astype(BF))
    columns = F // M
    for plane in range(2):
        for c in range(columns):
            part = spectrum[plane][:, c * M : (c + 1) * M]
            spec_ref[plane, c, :F] = part
            spec_ref[plane, c, F:] = part[:M]
            if c == 0:
                spec_ref[plane, columns, :F] = part
                spec_ref[plane, columns, F:] = part[:M]
    extract([js], [out_ref], me_ref, phase, so_ref, spec_ref)


def extract_kernel(sends, me_ref, fo_ref, so_ref, spec_ref, *outs):
    outs = outs[-len(sends) :]
    extract(sends, outs, me_ref, phase_taper(fo_ref), so_ref, spec_ref)


def extract(sends, outs, me_ref, phase, so_ref, spec_ref):
    pc, ps = phase
    me = me_ref[0]

    def block(out_ref, item, j):
        owner = j ^ me
        sx, sy = so_ref[0, owner], so_ref[1, owner]
        lane = sy // M
        shift = (2 * M - (sy & (M - 1))) & (2 * M - 1)
        parts = []
        for plane in range(2):
            left = spec_ref[plane, lane, pl.ds(sx, M), :]
            right = spec_ref[plane, lane + 1, pl.ds(sx, M), :]
            wide = jnp.concatenate([left, right], axis=1)
            parts.append(pltpu.roll(wide, shift, 1)[:, :M])
        wr, wi = parts
        out_ref[item, 0] = (pc * wr - ps * wi).astype(BF)
        out_ref[item, 1] = (pc * wi + ps * wr).astype(BF)

    for out_ref, js in zip(outs, sends):
        for_blocks(block, out_ref, js)


def for_blocks(block, ref, js):
    step = js[1] - js[0] if len(js) > 1 else 1
    if len(js) > 1 and js == list(range(js[0], js[0] + step * len(js), step)):

        def body(item, carry):
            block(ref, item, item * step + js[0])
            return carry

        lax.fori_loop(0, len(js), body, 0)
    else:
        for item, j in enumerate(js):
            block(ref, item, j)


def band_kernel(odd, me_ref, to_ref, kt_hbm, kwide_hbm, *rest):
    kvt_ref, kut_ref, ku_ref, zero_ref, kt_ref, kwide_ref, sems = rest[-7:]
    slots = kut_ref.shape[0]
    zero_ref[...] = jnp.zeros_like(zero_ref)

    @pl.when((me_ref[0] & 1) == odd)
    def _():
        copies = [
            pltpu.make_async_copy(kt_hbm, kt_ref, sems.at[0]),
            pltpu.make_async_copy(kwide_hbm, kwide_ref, sems.at[1]),
        ]
        for copy in copies:
            copy.start()
        for copy in copies:
            copy.wait()
        for t in range(slots):
            ou, ov = to_ref[0, t], to_ref[1, t]
            rows = slice(t * TV, (t + 1) * TV)
            kut_ref[t] = kt_ref[pl.ds(2 * TV - ou, SG), :].astype(BF)
            kvt_ref[:, rows] = kt_ref[pl.ds(2 * TV - ov, SG), :].astype(BF)
            ku_ref[rows] = pltpu.roll(kwide_ref[...], ou, 1).astype(BF)


def screen_kernel(w_ref, _, *rest):
    loads = (len(rest) - 3) // 2
    sources, screen_ref = rest[:loads], rest[loads]
    targets, zero_ref, sems = rest[loads + 1 : -2], rest[-2], rest[-1]
    zero_ref[...] = jnp.zeros_like(zero_ref)
    copies = [pltpu.make_async_copy(sources[k], targets[k], sems.at[k]) for k in range(loads)]
    for copy in copies:
        copy.start()
    w = w_ref[0, 0]
    row = lax.broadcasted_iota(jnp.int32, (SG, 1), 0).astype(F32) - SG / 2.0
    column = lax.broadcasted_iota(jnp.int32, (1, SG), 1).astype(F32) - SG / 2.0
    row2 = row * row * (1.0 / (SG * SG)) + 1.0
    column2 = column * column * (1.0 / (SG * SG))
    cos_v, sin_v = cos_sin_turns((jnp.sqrt(row2 + column2) - 1.0) * w)
    screen_ref[0] = cos_v
    screen_ref[1] = sin_v
    for copy in copies:
        copy.wait()


def subgrid_kernel(picks, tc_ref, *rest):
    parts = len(picks)
    sums = rest[:parts]
    (obs_ref, pad_ref, padt_ref, screen_ref, kvt_ref, kut_ref, ku_ref) = rest[parts : parts + 7]
    (out_ref, coef_ref, model_ref, rows_ref, z_ref, res_ref, sems) = rest[parts + 7 :]
    slots = obs_ref.shape[0]
    count = tc_ref[0, 0]

    def total(plane):
        value = sums[0][picks[0], plane].astype(F32)
        for ref, item in zip(sums[1:], picks[1:]):
            value = value + ref[item, plane].astype(F32)
        return value.astype(BF)

    pr, pi = pad_ref[0], pad_ref[1]
    inner_r, inner_i = mul_right(pr, pi, total(0), total(1))
    tr, ti = padt_ref[0], padt_ref[1]
    image_r, image_i = mul_left(inner_r.astype(BF), inner_i.astype(BF), tr, ti)
    sc, ss = screen_ref[0], screen_ref[1]
    model_ref[:SG] = (sc * image_r - ss * image_i).astype(BF)
    model_ref[SG:] = (sc * image_i + ss * image_r).astype(BF)

    model = model_ref[...]
    for t0 in range(0, slots, 2):
        pair = dot(model, kvt_ref[:, t0 * TV : (t0 + 2) * TV]).astype(BF)
        for t in (t0, t0 + 1):
            lanes = slice((t - t0) * TV, (t - t0 + 1) * TV)
            rows_ref[:, 2 * t * TV : (2 * t + 1) * TV] = pair[:SG, lanes]
            rows_ref[:, (2 * t + 1) * TV : (2 * t + 2) * TV] = pair[SG:, lanes]
    copies = []
    for t in range(slots):
        predicted = dot(ku_ref[t * TV : (t + 1) * TV], rows_ref[:, 2 * t * TV : (2 * t + 2) * TV])
        live = count > t
        for plane in range(2):
            value = obs_ref[t, plane].astype(F32) - predicted[:, plane * TV : (plane + 1) * TV]
            res_ref[t, plane] = jnp.where(live, value, 0.0).astype(BF)
        if t % 4 == 3:
            copies.append(
                pltpu.make_async_copy(
                    res_ref.at[pl.ds(t - 3, 4)], out_ref.at[pl.ds(t - 3, 4)], sems.at[t // 4]
                )
            )
            copies[-1].start()
    for t in range(slots):
        z = dot(kut_ref[t], jnp.concatenate([res_ref[t, 0], res_ref[t, 1]], axis=1)).astype(BF)
        z_ref[:SG, t * TV : (t + 1) * TV] = z[:, :TV]
        z_ref[SG:, t * TV : (t + 1) * TV] = z[:, TV:]

    kvt = kvt_ref[...]
    ar = dot_nt(z_ref[:SG], kvt)
    ai = dot_nt(z_ref[SG:], kvt)
    screened_r = (sc * ar + ss * ai).astype(BF)
    screened_i = (sc * ai - ss * ar).astype(BF)
    reduced_r, reduced_i = mul_right(tr, -ti, screened_r, screened_i)
    coef_r, coef_i = mul_left(reduced_r.astype(BF), reduced_i.astype(BF), pr, -pi)
    coef_ref[0, 0] = coef_r.astype(BF)
    coef_ref[0, 1] = coef_i.astype(BF)
    for copy in copies:
        copy.wait()


def grid_blocks(pieces, refs, me_ref, fo_ref, so_ref, grid_ref):
    pc, ps = phase_taper(fo_ref)
    me = me_ref[0]
    blank = jnp.zeros((M, M), F32)

    def block(in_ref, item, j):
        owner = j ^ me
        sx, sy = so_ref[0, owner], so_ref[1, owner]
        lane = sy // M
        shift = sy & (M - 1)
        cr, ci = in_ref[item, 0].astype(F32), in_ref[item, 1].astype(F32)
        values = (pc * cr + ps * ci, pc * ci - ps * cr)
        for plane in range(2):
            wide = pltpu.roll(jnp.concatenate([values[plane], blank], axis=1), shift, 1)
            grid_ref[plane, lane, pl.ds(sx, M), :] += wide[:, :M]
            grid_ref[plane, lane + 1, pl.ds(sx, M), :] += wide[:, M:]

    for in_ref, js in zip(refs, pieces):
        for_blocks(block, in_ref, js)


def first_grid_kernel(pieces, me_ref, fo_ref, so_ref, basis_hbm, *rest):
    grid_ref, zero_ref, basis_ref, sem = rest[-4:]
    load = pltpu.make_async_copy(basis_hbm, basis_ref, sem)
    load.start()
    zero_ref[...] = jnp.zeros_like(zero_ref)
    grid_ref[...] = jnp.zeros_like(grid_ref)
    grid_blocks(pieces, rest[:-4], me_ref, fo_ref, so_ref, grid_ref)
    load.wait()


def next_grid_kernel(pieces, me_ref, fo_ref, so_ref, *rest):
    grid_ref, _, zero_ref = rest[-3:]
    zero_ref[...] = jnp.zeros_like(zero_ref)
    grid_blocks(pieces, rest[:-3], me_ref, fo_ref, so_ref, grid_ref)


def backward_kernel(pieces, me_ref, fo_ref, so_ref, basis_ref, *rest):
    grid_ref, out_ref, _, out_buf, sems = rest[len(pieces) :]
    grid_blocks(pieces, rest[: len(pieces)], me_ref, fo_ref, so_ref, grid_ref)
    columns = F // M
    folded = []
    for plane in range(2):
        strips = []
        for c in range(columns):
            strip = grid_ref[plane, c]
            if c == 0:
                strip = strip + grid_ref[plane, columns]
            top = strip[:M] + strip[F:]
            strips.append(jnp.concatenate([top.astype(BF), strip[M:F].astype(BF)], axis=0))
        folded.append(jnp.concatenate(strips, axis=1))
    br, bi = basis_ref[0], basis_ref[1]
    hr, hi = mul_right(br, -bi, *folded)
    hr, hi = hr.astype(BF), hi.astype(BF)
    size = F // OUT_CHUNKS
    copies = []
    for k in range(OUT_CHUNKS):
        rows = slice(k * size, (k + 1) * size)
        real, imag = mul_left(hr[rows], hi[rows], br, -bi)
        for plane, value in enumerate((real, imag)):
            out_buf[plane, rows] = value.astype(BF)
            copy = pltpu.make_async_copy(
                out_buf.at[plane, pl.ds(k * size, size)],
                out_ref.at[0, plane, pl.ds(k * size, size)],
                sems.at[2 * k + plane],
            )
            copy.start()
            copies.append(copy)
    for copy in copies:
        copy.wait()


SMEM = pl.BlockSpec(memory_space=pltpu.SMEM)
VMEM = pl.BlockSpec(memory_space=pltpu.VMEM)
ANY = pl.BlockSpec(memory_space=pl.ANY)


def params(mib):
    return pltpu.CompilerParams(vmem_limit_bytes=mib * 1024 * 1024)


def near(value):
    return pltpu.with_memory_space_constraint(value, pltpu.VMEM)


def far(value):
    return pltpu.with_memory_space_constraint(value, pltpu.HBM)


def held(shape, dtype=BF):
    return pltpu.VMEM(shape, dtype)


def exchange(value, mask, n):
    return lax.ppermute(value, "facet", [(i, i ^ mask) for i in range(n)])


def digit_levels(n):
    levels, base = [], 1
    while base < n:
        radix = 2 if base < 4 or n // base < 4 else 4
        levels.append((base, radix))
        base *= radix
    return levels


def reduce_sends(n):
    sends = []
    for base, radix in digit_levels(n):
        for g in range(radix - 1, 0, -1):
            js = [j for j in range(0, n, base) if (j // base) % radix == g]
            groups = [js[1::2], js[::2]] if base == 1 else [js]
            sends += [(group, g * base) for group in groups]
    return sends


def pick(value, items):
    step = items[1] - items[0] if len(items) > 1 else 1
    if items == list(range(items[0], items[0] + step * len(items), step)):
        if len(items) == value.shape[0]:
            return value
        return lax.slice_in_dim(value, items[0], items[-1] + 1, step)
    return jnp.concatenate([value[i : i + 1] for i in items])


def join(pieces):
    return [j for js, _ in pieces for j in js], jnp.concatenate([value for _, value in pieces])


def per_device(facets, facet_offsets, subgrid_offsets, w_terms, tile_count, tile_offsets, observed):
    n = lax.axis_size("facet")
    slots = observed.shape[0]
    me = lax.axis_index("facet").astype(jnp.int32).reshape(1)
    corners = far(subgrid_offsets.T)
    tile_corners = far(tile_offsets.T)
    facet_offsets = far(facet_offsets)
    basis = far(jnp.asarray(basis_tables()))
    pad_np = padding_tables(n)
    kern_np = kernel_table()
    kt_np = np.zeros((6 * TV, TV), np.float32)
    kt_np[2 * TV : 4 * TV] = kern_np.astype(np.float32).T
    kwide_np = np.zeros((TV, SG), np.float32)
    kwide_np[:, : 2 * TV] = kern_np.astype(np.float32)
    grid_shape = (2, F // M + 1, F + M, M)

    sends = reduce_sends(n)
    first, spec = pl.pallas_call(
        functools.partial(forward_kernel, sends[0][0]),
        out_shape=[held((len(sends[0][0]), 2, M, M)), held(grid_shape, F32)],
        in_specs=[SMEM] + [ANY] * 4,
        out_specs=[VMEM] * 2,
        scratch_shapes=[
            pltpu.VMEM((2, F, F), BF),
            pltpu.VMEM((2, F, F), BF),
            pltpu.SMEM(facet_offsets.shape, jnp.int32),
            pltpu.SMEM(corners.shape, jnp.int32),
            pltpu.SemaphoreType.DMA((6,)),
        ],
        compiler_params=params(16),
        name="forward",
    )(me, facet_offsets, corners, far(facets), basis)
    def make_blocks(lists, after):
        return pl.pallas_call(
            functools.partial(extract_kernel, lists),
            out_shape=[held((len(js), 2, M, M)) for js in lists],
            in_specs=[SMEM] * 3 + [VMEM] * (1 + len(after)),
            out_specs=[VMEM] * len(lists),
            compiler_params=params(8),
            name="extract",
        )(me, facet_offsets, corners, near(spec), *[near(value) for value in after])

    def make_bands(odd, bands, after):
        shapes = [(SG, slots * TV), (slots, SG, TV), (slots * TV, SG)]
        return pl.pallas_call(
            functools.partial(band_kernel, odd),
            out_shape=[held(shape) for shape in shapes] + [held((1, M), F32)],
            in_specs=[SMEM] * 2 + [ANY] * 2 + [VMEM] * (len(bands) + len(after)),
            out_specs=[VMEM] * 4,
            scratch_shapes=[
                pltpu.VMEM(kt_np.shape, F32),
                pltpu.VMEM(kwide_np.shape, F32),
                pltpu.SemaphoreType.DMA((2,)),
            ],
            input_output_aliases={4 + k: k for k in range(len(bands))},
            compiler_params=params(8),
            name="bands",
        )(
            me,
            tile_corners,
            far(jnp.asarray(kt_np)),
            far(jnp.asarray(kwide_np)),
            *[near(value) for value in list(bands) + after],
        )

    def make_screen(after):
        loads = [observed, pad_np, pad_np.transpose(0, 2, 1), subgrid_offsets.T, facet_offsets]
        return pl.pallas_call(
            screen_kernel,
            out_shape=[held((2, SG, SG), F32)] + [held(load.shape, load.dtype) for load in loads] + [held((1, M), F32)],
            in_specs=[SMEM, VMEM] + [ANY] * len(loads),
            out_specs=[VMEM] * (2 + len(loads)),
            scratch_shapes=[pltpu.SemaphoreType.DMA((len(loads),))],
            compiler_params=params(8),
            name="screen",
        )(w_terms.reshape(1, 1), near(after), *[far(jnp.asarray(load)) for load in loads])

    arrived = []

    def send(js, mask, value, token=None):
        total = value.astype(F32)
        if token is not None:
            total = total + token
        for got_js, got in arrived:
            if set(js) <= set(got_js):
                total = total + pick(got, [got_js.index(j) for j in js]).astype(F32)
            else:
                assert not set(js) & set(got_js)
        value = total.astype(BF)
        arrived.append(([j ^ mask for j in js], exchange(value, mask, n)))
        return value

    (urgent, _), (lazy, _), (beside, _) = sends[:3]
    send(urgent, 1, first)
    beside_own, lazy_own = make_blocks([beside, lazy], [])
    *bands, token = make_bands(0, [], [beside_own])
    value = send(beside, 2, beside_own, token)
    send(lazy, 1, lazy_own)
    own = make_blocks([js for js, _ in sends[3:]] + [[0]], [value])
    screen, tiles, pad, padt, late_corners, late_facet_offsets, token = make_screen(value)
    for (js, mask), value in zip(sends[3:], own):
        value = send(js, mask, value, token)
    kvt, kut, ku, _ = make_bands(1, bands, [value])
    corners, facet_offsets = near(late_corners), near(late_facet_offsets)
    last = [(js, got) for js, got in arrived if 0 in js]

    residual, coefficient = pl.pallas_call(
        functools.partial(subgrid_kernel, [0] + [js.index(0) for js, _ in last]),
        out_shape=[pltpu.HBM(observed.shape, BF), held((1, 2, M, M))],
        in_specs=[SMEM] + [VMEM] * (len(last) + 8),
        out_specs=[ANY, VMEM],
        scratch_shapes=[
            pltpu.VMEM((2 * SG, SG), BF),
            pltpu.VMEM((SG, 2 * slots * TV), BF),
            pltpu.VMEM((2 * SG, slots * TV), BF),
            pltpu.VMEM(observed.shape, BF),
            pltpu.SemaphoreType.DMA((slots // 4,)),
        ],
        compiler_params=params(24),
        name="subgrid",
    )(
        tile_count.reshape(1, 1),
        near(own[-1]),
        *[near(got) for _, got in last],
        *[near(value) for value in (tiles, pad, padt, screen, kvt, kut, ku)],
    )

    early = ([0], coefficient)
    for base, radix in reversed(digit_levels(n)[2:]):
        js, value = early
        masks = [g * base for g in range(radix - 1, 0, -1)]
        more = [([j ^ mask for j in js], exchange(value, mask, n)) for mask in masks]
        early = join([early] + more)

    def hop(part, mask):
        return [j ^ mask for j in part[0]], exchange(part[1], mask, n)

    late = hop(early, 2)
    ready = [early]
    def next_grid(ready, grid):
        return pl.pallas_call(
            functools.partial(next_grid_kernel, [js for js, _ in ready]),
            out_shape=[held(grid_shape, F32), held((1, M), F32)],
            in_specs=[SMEM] * 3 + [VMEM] * (len(ready) + 1),
            out_specs=[VMEM] * 2,
            input_output_aliases={3 + len(ready): 0},
            compiler_params=params(8),
            name="grid_next",
        )(me, facet_offsets, corners, *[near(value) for _, value in ready], near(grid))

    grid, token, basis_near = pl.pallas_call(
        functools.partial(first_grid_kernel, [js for js, _ in ready]),
        out_shape=[held(grid_shape, F32), held((1, M), F32), held(basis.shape)],
        in_specs=[SMEM] * 3 + [ANY] + [VMEM] * len(ready),
        out_specs=[VMEM] * 3,
        scratch_shapes=[pltpu.SemaphoreType.DMA(())],
        compiler_params=params(8),
        name="grid_first",
    )(me, facet_offsets, corners, basis, *[near(value) for _, value in ready])
    other = hop(early, 1)
    late = (late[0], (late[1].astype(F32) + token).astype(BF))
    late_other = hop(late, 1)
    grid, _ = next_grid([other, late], grid)
    update = pl.pallas_call(
        functools.partial(backward_kernel, [late_other[0]]),
        out_shape=[pltpu.HBM(facets.shape, BF), held(grid_shape, F32)],
        in_specs=[SMEM] * 3 + [VMEM] * 3,
        out_specs=[ANY, VMEM],
        input_output_aliases={5: 1},
        scratch_shapes=[
            pltpu.VMEM((2, F, F), BF),
            pltpu.SemaphoreType.DMA((2 * OUT_CHUNKS,)),
        ],
        compiler_params=params(16),
        name="backward",
    )(me, facet_offsets, corners, near(basis_near), near(late_other[1]), near(grid))[0]
    return (residual, update)


def solution(mesh):
    placed = (
        P(("groups", "facet"), None, None, None),
        P(("groups", "facet"), None),
        P("groups", None),
        P(("groups", "facet")),
        P(("groups", "facet")),
        P(("groups", "facet"), None),
        P(("groups", "facet"), None, None, None),
    )
    return jax.shard_map(
        per_device,
        mesh=mesh,
        in_specs=placed,
        out_specs=(
            P(("groups", "facet"), None, None, None),
            P(("groups", "facet"), None, None, None),
        ),
        check_vma=False,
    )
```

```python
import functools
import math

import jax
import jax.numpy as jnp
import ml_dtypes
import numpy as np
from jax import lax
from jax.experimental import pallas as pl
from jax.experimental.pallas import tpu as pltpu
from jax.sharding import PartitionSpec as P

F = 512
M = 128
SG = 512
TV = 128
BF = jnp.bfloat16
F32 = jnp.float32
TWO_PI = 2.0 * math.pi
OUT_CHUNKS = 4


def basis_tables():
    index = np.arange(F, dtype=np.int64)
    angle = -TWO_PI * ((index[:, None] * index[None, :]) % F) / F
    table = np.stack([np.cos(angle), np.sin(angle)]) / math.sqrt(F)
    return table.astype(ml_dtypes.bfloat16)


def padding_tables(facet_count):
    product = (np.arange(SG)[:, None] * np.arange(M)[None, :]) % SG
    angle = TWO_PI * product / SG
    scale = (M * math.sqrt(facet_count)) ** (-0.5)
    table = np.stack([np.cos(angle), np.sin(angle)]) * scale
    return table.astype(ml_dtypes.bfloat16)


def kernel_table():
    rows = np.arange(TV, dtype=np.float64)[:, None]
    columns = np.arange(2 * TV, dtype=np.float64)[None, :]
    distance = columns - 2.0 * rows - 1.0
    value = 0.75 * np.exp(-((distance / 1.5) ** 2))
    return np.where(np.abs(distance) <= 4.0, value, 0.0).astype(ml_dtypes.bfloat16)


def taper_square():
    position = np.arange(M, dtype=np.float64)
    taper = 0.6 + 0.4 * np.sin(math.pi * (position + 0.5) / M)
    return (taper[:, None] * taper[None, :]).astype(np.float32)


def turn_polynomials():
    nodes = 0.5 * np.cos(math.pi * (np.arange(400) + 0.5) / 800)
    square = nodes * nodes
    powers = np.stack([square**k for k in range(8)], axis=1)
    cos_c = np.linalg.lstsq(powers, np.cos(TWO_PI * nodes), rcond=None)[0]
    sin_c = np.linalg.lstsq(powers, np.sin(TWO_PI * nodes) / nodes, rcond=None)[0]
    return [float(c) for c in cos_c], [float(c) for c in sin_c]


COS_C, SIN_C = turn_polynomials()


def cos_sin_turns(turns):
    rest = turns - jnp.floor(turns + 0.5)
    square = rest * rest
    cos_v = jnp.full_like(square, COS_C[7])
    sin_v = jnp.full_like(square, SIN_C[7])
    for k in range(6, -1, -1):
        cos_v = cos_v * square + COS_C[k]
        sin_v = sin_v * square + SIN_C[k]
    return cos_v, sin_v * rest


def dot(left, right):
    return jnp.dot(left, right, preferred_element_type=F32)


def dot_nt(left, right):
    return lax.dot_general(left, right, (((1,), (1,)), ((), ())), preferred_element_type=F32)


def mul_left(left_r, left_i, right_r, right_i):
    left = jnp.concatenate([left_r, left_i], axis=1)
    real = dot(left, jnp.concatenate([right_r, -right_i], axis=0))
    imag = dot(left, jnp.concatenate([right_i, right_r], axis=0))
    return real, imag


def mul_right(left_r, left_i, right_r, right_i):
    right = jnp.concatenate([right_r, right_i], axis=0)
    real = dot(jnp.concatenate([left_r, -left_i], axis=1), right)
    imag = dot(jnp.concatenate([left_i, left_r], axis=1), right)
    return real, imag


def phase_taper(fo_ref):
    rows = lax.broadcasted_iota(jnp.int32, (M, M), 0)
    columns = lax.broadcasted_iota(jnp.int32, (M, M), 1)
    total = (rows * fo_ref[0, 0] + columns * fo_ref[0, 1]) & (F - 1)
    cos_v, sin_v = cos_sin_turns(total.astype(F32) * (1.0 / F))
    row = lax.broadcasted_iota(jnp.int32, (M, 1), 0).astype(F32)
    column = lax.broadcasted_iota(jnp.int32, (1, M), 1).astype(F32)
    _, row_sin = cos_sin_turns((row + 0.5) * (0.5 / M))
    _, column_sin = cos_sin_turns((column + 0.5) * (0.5 / M))
    taper2 = (0.6 + 0.4 * row_sin) * (0.6 + 0.4 * column_sin)
    return cos_v * taper2, sin_v * taper2


def forward_kernel(js, me_ref, fo_hbm, so_hbm, facet_ref, basis_ref, out_ref, spec_ref, *rest):
    facet_buf, basis_buf, fo_ref, so_ref, sems = rest
    copies = [
        pltpu.make_async_copy(fo_hbm, fo_ref, sems.at[4]),
        pltpu.make_async_copy(so_hbm, so_ref, sems.at[5]),
    ]
    for k in range(2):
        copies.append(pltpu.make_async_copy(basis_ref.at[k], basis_buf.at[k], sems.at[2 * k]))
        copies.append(pltpu.make_async_copy(facet_ref.at[0, k], facet_buf.at[k], sems.at[2 * k + 1]))
    for copy in copies:
        copy.start()
    for copy in copies[:2]:
        copy.wait()
    phase = phase_taper(fo_ref)
    for copy in copies[2:]:
        copy.wait()
    br, bi = basis_buf[0], basis_buf[1]
    hr, hi = mul_left(facet_buf[0], facet_buf[1], br, bi)
    spectrum = mul_right(br, bi, hr.astype(BF), hi.astype(BF))
    columns = F // M
    for plane in range(2):
        for c in range(columns):
            part = spectrum[plane][:, c * M : (c + 1) * M]
            spec_ref[plane, c, :F] = part
            spec_ref[plane, c, F:] = part[:M]
            if c == 0:
                spec_ref[plane, columns, :F] = part
                spec_ref[plane, columns, F:] = part[:M]
    extract([js], [out_ref], me_ref, phase, so_ref, spec_ref)


def extract_kernel(sends, me_ref, fo_ref, so_ref, spec_ref, *outs):
    outs = outs[-len(sends) :]
    extract(sends, outs, me_ref, phase_taper(fo_ref), so_ref, spec_ref)


def extract(sends, outs, me_ref, phase, so_ref, spec_ref):
    pc, ps = phase
    me = me_ref[0]

    def block(out_ref, item, j):
        owner = j ^ me
        sx, sy = so_ref[0, owner], so_ref[1, owner]
        lane = sy // M
        shift = (2 * M - (sy & (M - 1))) & (2 * M - 1)
        parts = []
        for plane in range(2):
            left = spec_ref[plane, lane, pl.ds(sx, M), :]
            right = spec_ref[plane, lane + 1, pl.ds(sx, M), :]
            wide = jnp.concatenate([left, right], axis=1)
            parts.append(pltpu.roll(wide, shift, 1)[:, :M])
        wr, wi = parts
        out_ref[item, 0] = (pc * wr - ps * wi).astype(BF)
        out_ref[item, 1] = (pc * wi + ps * wr).astype(BF)

    for out_ref, js in zip(outs, sends):
        for_blocks(block, out_ref, js)


def for_blocks(block, ref, js):
    step = js[1] - js[0] if len(js) > 1 else 1
    if len(js) > 1 and js == list(range(js[0], js[0] + step * len(js), step)):

        def body(item, carry):
            block(ref, item, item * step + js[0])
            return carry

        lax.fori_loop(0, len(js), body, 0)
    else:
        for item, j in enumerate(js):
            block(ref, item, j)


def band_kernel(odds, tiles, me_ref, to_ref, kt_hbm, kwide_hbm, *rest):
    kvt_ref, kut_ref, ku_ref, zero_ref, kt_ref, kwide_ref, sems = rest[-7:]
    zero_ref[...] = jnp.zeros_like(zero_ref)

    def make():
        copies = [
            pltpu.make_async_copy(kt_hbm, kt_ref, sems.at[0]),
            pltpu.make_async_copy(kwide_hbm, kwide_ref, sems.at[1]),
        ]
        for copy in copies:
            copy.start()
        for copy in copies:
            copy.wait()
        for t in tiles:
            ou, ov = to_ref[0, t], to_ref[1, t]
            rows = slice(t * TV, (t + 1) * TV)
            kut_ref[t] = kt_ref[pl.ds(2 * TV - ou, SG), :].astype(BF)
            kvt_ref[:, rows] = kt_ref[pl.ds(2 * TV - ov, SG), :].astype(BF)
            ku_ref[rows] = pltpu.roll(kwide_ref[...], ou, 1).astype(BF)

    if len(odds) == 2:
        make()
    else:
        pl.when((me_ref[0] & 1) == odds[0])(make)


def screen_kernel(w_ref, _, *rest):
    loads = (len(rest) - 3) // 2
    sources, screen_ref = rest[:loads], rest[loads]
    targets, zero_ref, sems = rest[loads + 1 : -2], rest[-2], rest[-1]
    zero_ref[...] = jnp.zeros_like(zero_ref)
    copies = [pltpu.make_async_copy(sources[k], targets[k], sems.at[k]) for k in range(loads)]
    for copy in copies:
        copy.start()
    w = w_ref[0, 0]
    row = lax.broadcasted_iota(jnp.int32, (SG, 1), 0).astype(F32) - SG / 2.0
    column = lax.broadcasted_iota(jnp.int32, (1, SG), 1).astype(F32) - SG / 2.0
    row2 = row * row * (1.0 / (SG * SG)) + 1.0
    column2 = column * column * (1.0 / (SG * SG))
    cos_v, sin_v = cos_sin_turns((jnp.sqrt(row2 + column2) - 1.0) * w)
    screen_ref[0] = cos_v
    screen_ref[1] = sin_v
    for copy in copies:
        copy.wait()


def subgrid_kernel(picks, tc_ref, *rest):
    parts = len(picks)
    sums = rest[:parts]
    (obs_ref, pad_ref, padt_ref, screen_ref, kvt_ref, kut_ref, ku_ref) = rest[parts : parts + 7]
    (out_ref, coef_ref, model_ref, rows_ref, z_ref, res_ref, sems) = rest[parts + 7 :]
    slots = obs_ref.shape[0]
    count = tc_ref[0, 0]

    def total(plane):
        value = sums[0][picks[0], plane].astype(F32)
        for ref, item in zip(sums[1:], picks[1:]):
            value = value + ref[item, plane].astype(F32)
        return value.astype(BF)

    pr, pi = pad_ref[0], pad_ref[1]
    inner_r, inner_i = mul_right(pr, pi, total(0), total(1))
    tr, ti = padt_ref[0], padt_ref[1]
    image_r, image_i = mul_left(inner_r.astype(BF), inner_i.astype(BF), tr, ti)
    sc, ss = screen_ref[0], screen_ref[1]
    model_ref[:SG] = (sc * image_r - ss * image_i).astype(BF)
    model_ref[SG:] = (sc * image_i + ss * image_r).astype(BF)

    model = model_ref[...]
    for t0 in range(0, slots, 2):
        pair = dot(model, kvt_ref[:, t0 * TV : (t0 + 2) * TV]).astype(BF)
        for t in (t0, t0 + 1):
            lanes = slice((t - t0) * TV, (t - t0 + 1) * TV)
            rows_ref[:, 2 * t * TV : (2 * t + 1) * TV] = pair[:SG, lanes]
            rows_ref[:, (2 * t + 1) * TV : (2 * t + 2) * TV] = pair[SG:, lanes]
    copies = []
    for t in range(slots):
        predicted = dot(ku_ref[t * TV : (t + 1) * TV], rows_ref[:, 2 * t * TV : (2 * t + 2) * TV])
        live = count > t
        for plane in range(2):
            value = obs_ref[t, plane].astype(F32) - predicted[:, plane * TV : (plane + 1) * TV]
            res_ref[t, plane] = jnp.where(live, value, 0.0).astype(BF)
        if t % 4 == 3:
            copies.append(
                pltpu.make_async_copy(
                    res_ref.at[pl.ds(t - 3, 4)], out_ref.at[pl.ds(t - 3, 4)], sems.at[t // 4]
                )
            )
            copies[-1].start()
    for t in range(slots):
        z = dot(kut_ref[t], jnp.concatenate([res_ref[t, 0], res_ref[t, 1]], axis=1)).astype(BF)
        z_ref[:SG, t * TV : (t + 1) * TV] = z[:, :TV]
        z_ref[SG:, t * TV : (t + 1) * TV] = z[:, TV:]

    kvt = kvt_ref[...]
    ar = dot_nt(z_ref[:SG], kvt)
    ai = dot_nt(z_ref[SG:], kvt)
    screened_r = (sc * ar + ss * ai).astype(BF)
    screened_i = (sc * ai - ss * ar).astype(BF)
    reduced_r, reduced_i = mul_right(tr, -ti, screened_r, screened_i)
    coef_r, coef_i = mul_left(reduced_r.astype(BF), reduced_i.astype(BF), pr, -pi)
    coef_ref[0, 0] = coef_r.astype(BF)
    coef_ref[0, 1] = coef_i.astype(BF)
    for copy in copies:
        copy.wait()


def grid_blocks(pieces, refs, me_ref, fo_ref, so_ref, grid_ref):
    pc, ps = phase_taper(fo_ref)
    me = me_ref[0]
    blank = jnp.zeros((M, M), F32)

    def block(in_ref, item, j):
        owner = j ^ me
        sx, sy = so_ref[0, owner], so_ref[1, owner]
        lane = sy // M
        shift = sy & (M - 1)
        cr, ci = in_ref[item, 0].astype(F32), in_ref[item, 1].astype(F32)
        values = (pc * cr + ps * ci, pc * ci - ps * cr)
        for plane in range(2):
            wide = pltpu.roll(jnp.concatenate([values[plane], blank], axis=1), shift, 1)
            grid_ref[plane, lane, pl.ds(sx, M), :] += wide[:, :M]
            grid_ref[plane, lane + 1, pl.ds(sx, M), :] += wide[:, M:]

    for in_ref, js in zip(refs, pieces):
        for_blocks(block, in_ref, js)


def first_grid_kernel(pieces, me_ref, fo_ref, so_ref, basis_hbm, *rest):
    grid_ref, zero_ref, basis_ref, sem = rest[-4:]
    load = pltpu.make_async_copy(basis_hbm, basis_ref, sem)
    load.start()
    zero_ref[...] = jnp.zeros_like(zero_ref)
    grid_ref[...] = jnp.zeros_like(grid_ref)
    grid_blocks(pieces, rest[:-4], me_ref, fo_ref, so_ref, grid_ref)
    load.wait()


def next_grid_kernel(pieces, me_ref, fo_ref, so_ref, *rest):
    grid_ref, _, zero_ref = rest[-3:]
    zero_ref[...] = jnp.zeros_like(zero_ref)
    grid_blocks(pieces, rest[:-3], me_ref, fo_ref, so_ref, grid_ref)


def backward_kernel(pieces, me_ref, fo_ref, so_ref, basis_ref, *rest):
    grid_ref, out_ref, _, out_buf, sems = rest[len(pieces) :]
    grid_blocks(pieces, rest[: len(pieces)], me_ref, fo_ref, so_ref, grid_ref)
    columns = F // M
    folded = []
    for plane in range(2):
        strips = []
        for c in range(columns):
            strip = grid_ref[plane, c]
            if c == 0:
                strip = strip + grid_ref[plane, columns]
            top = strip[:M] + strip[F:]
            strips.append(jnp.concatenate([top.astype(BF), strip[M:F].astype(BF)], axis=0))
        folded.append(jnp.concatenate(strips, axis=1))
    br, bi = basis_ref[0], basis_ref[1]
    hr, hi = mul_right(br, -bi, *folded)
    hr, hi = hr.astype(BF), hi.astype(BF)
    size = F // OUT_CHUNKS
    copies = []
    for k in range(OUT_CHUNKS):
        rows = slice(k * size, (k + 1) * size)
        real, imag = mul_left(hr[rows], hi[rows], br, -bi)
        for plane, value in enumerate((real, imag)):
            out_buf[plane, rows] = value.astype(BF)
            copy = pltpu.make_async_copy(
                out_buf.at[plane, pl.ds(k * size, size)],
                out_ref.at[0, plane, pl.ds(k * size, size)],
                sems.at[2 * k + plane],
            )
            copy.start()
            copies.append(copy)
    for copy in copies:
        copy.wait()


SMEM = pl.BlockSpec(memory_space=pltpu.SMEM)
VMEM = pl.BlockSpec(memory_space=pltpu.VMEM)
ANY = pl.BlockSpec(memory_space=pl.ANY)


def params(mib):
    return pltpu.CompilerParams(vmem_limit_bytes=mib * 1024 * 1024)


def near(value):
    return pltpu.with_memory_space_constraint(value, pltpu.VMEM)


def far(value):
    return pltpu.with_memory_space_constraint(value, pltpu.HBM)


def held(shape, dtype=BF):
    return pltpu.VMEM(shape, dtype)


def exchange(value, mask, n):
    return lax.ppermute(value, "facet", [(i, i ^ mask) for i in range(n)])


def digit_levels(n):
    levels, base = [], 1
    while base < n:
        radix = 2 if base < 4 or n // base < 4 else 4
        levels.append((base, radix))
        base *= radix
    return levels


def reduce_sends(n):
    sends = []
    for base, radix in digit_levels(n):
        for g in range(radix - 1, 0, -1):
            js = [j for j in range(0, n, base) if (j // base) % radix == g]
            groups = [js[1::2], js[::2]] if base == 1 else [js]
            sends += [(group, g * base) for group in groups]
    return sends


def pick(value, items):
    step = items[1] - items[0] if len(items) > 1 else 1
    if items == list(range(items[0], items[0] + step * len(items), step)):
        if len(items) == value.shape[0]:
            return value
        return lax.slice_in_dim(value, items[0], items[-1] + 1, step)
    return jnp.concatenate([value[i : i + 1] for i in items])


def join(pieces):
    return [j for js, _ in pieces for j in js], jnp.concatenate([value for _, value in pieces])


def per_device(facets, facet_offsets, subgrid_offsets, w_terms, tile_count, tile_offsets, observed):
    n = lax.axis_size("facet")
    slots = observed.shape[0]
    me = lax.axis_index("facet").astype(jnp.int32).reshape(1)
    corners = far(subgrid_offsets.T)
    tile_corners = far(tile_offsets.T)
    facet_offsets = far(facet_offsets)
    basis = far(jnp.asarray(basis_tables()))
    pad_np = padding_tables(n)
    kern_np = kernel_table()
    kt_np = np.zeros((6 * TV, TV), np.float32)
    kt_np[2 * TV : 4 * TV] = kern_np.astype(np.float32).T
    kwide_np = np.zeros((TV, SG), np.float32)
    kwide_np[:, : 2 * TV] = kern_np.astype(np.float32)
    grid_shape = (2, F // M + 1, F + M, M)

    sends = reduce_sends(n)
    first, spec = pl.pallas_call(
        functools.partial(forward_kernel, sends[0][0]),
        out_shape=[held((len(sends[0][0]), 2, M, M)), held(grid_shape, F32)],
        in_specs=[SMEM] + [ANY] * 4,
        out_specs=[VMEM] * 2,
        scratch_shapes=[
            pltpu.VMEM((2, F, F), BF),
            pltpu.VMEM((2, F, F), BF),
            pltpu.SMEM(facet_offsets.shape, jnp.int32),
            pltpu.SMEM(corners.shape, jnp.int32),
            pltpu.SemaphoreType.DMA((6,)),
        ],
        compiler_params=params(16),
        name="forward",
    )(me, facet_offsets, corners, far(facets), basis)
    def make_blocks(lists, after):
        return pl.pallas_call(
            functools.partial(extract_kernel, lists),
            out_shape=[held((len(js), 2, M, M)) for js in lists],
            in_specs=[SMEM] * 3 + [VMEM] * (1 + len(after)),
            out_specs=[VMEM] * len(lists),
            compiler_params=params(8),
            name="extract",
        )(me, facet_offsets, corners, near(spec), *[near(value) for value in after])

    def make_bands(odds, tiles, bands, after):
        shapes = [(SG, slots * TV), (slots, SG, TV), (slots * TV, SG)]
        return pl.pallas_call(
            functools.partial(band_kernel, odds, tiles),
            out_shape=[held(shape) for shape in shapes] + [held((1, M), F32)],
            in_specs=[SMEM] * 2 + [ANY] * 2 + [VMEM] * (len(bands) + len(after)),
            out_specs=[VMEM] * 4,
            scratch_shapes=[
                pltpu.VMEM(kt_np.shape, F32),
                pltpu.VMEM(kwide_np.shape, F32),
                pltpu.SemaphoreType.DMA((2,)),
            ],
            input_output_aliases={4 + k: k for k in range(len(bands))},
            compiler_params=params(8),
            name="bands",
        )(
            me,
            tile_corners,
            far(jnp.asarray(kt_np)),
            far(jnp.asarray(kwide_np)),
            *[near(value) for value in list(bands) + after],
        )

    def make_screen(after):
        loads = [observed, pad_np, pad_np.transpose(0, 2, 1), subgrid_offsets.T, facet_offsets]
        return pl.pallas_call(
            screen_kernel,
            out_shape=[held((2, SG, SG), F32)] + [held(load.shape, load.dtype) for load in loads] + [held((1, M), F32)],
            in_specs=[SMEM, VMEM] + [ANY] * len(loads),
            out_specs=[VMEM] * (2 + len(loads)),
            scratch_shapes=[pltpu.SemaphoreType.DMA((len(loads),))],
            compiler_params=params(8),
            name="screen",
        )(w_terms.reshape(1, 1), near(after), *[far(jnp.asarray(load)) for load in loads])

    arrived = []

    def send(js, mask, value, token=None):
        total = value.astype(F32)
        if token is not None:
            total = total + token
        for got_js, got in arrived:
            if set(js) <= set(got_js):
                total = total + pick(got, [got_js.index(j) for j in js]).astype(F32)
            else:
                assert not set(js) & set(got_js)
        value = total.astype(BF)
        arrived.append(([j ^ mask for j in js], exchange(value, mask, n)))
        return value

    (urgent, _), (lazy, _), (beside, _) = sends[:3]
    send(urgent, 1, first)
    beside_own, lazy_own = make_blocks([beside, lazy], [])
    some, others = range(slots // 2), range(slots // 2, slots)
    *bands, token = make_bands([0], some, [], [beside_own])
    value = send(beside, 2, beside_own, token)
    send(lazy, 1, lazy_own)
    own = make_blocks([js for js, _ in sends[3:]] + [[0]], [value])
    screen, tiles, pad, padt, late_corners, late_facet_offsets, token = make_screen(value)
    *bands, band_token = make_bands([0, 1], others, bands, [value])
    for (js, mask), value in zip(sends[3:], own):
        value = send(js, mask, value, token + band_token)
    kvt, kut, ku, _ = make_bands([1], some, bands, [value])
    corners, facet_offsets = near(late_corners), near(late_facet_offsets)
    last = [(js, got) for js, got in arrived if 0 in js]

    residual, coefficient = pl.pallas_call(
        functools.partial(subgrid_kernel, [0] + [js.index(0) for js, _ in last]),
        out_shape=[pltpu.HBM(observed.shape, BF), held((1, 2, M, M))],
        in_specs=[SMEM] + [VMEM] * (len(last) + 8),
        out_specs=[ANY, VMEM],
        scratch_shapes=[
            pltpu.VMEM((2 * SG, SG), BF),
            pltpu.VMEM((SG, 2 * slots * TV), BF),
            pltpu.VMEM((2 * SG, slots * TV), BF),
            pltpu.VMEM(observed.shape, BF),
            pltpu.SemaphoreType.DMA((slots // 4,)),
        ],
        compiler_params=params(24),
        name="subgrid",
    )(
        tile_count.reshape(1, 1),
        near(own[-1]),
        *[near(got) for _, got in last],
        *[near(value) for value in (tiles, pad, padt, screen, kvt, kut, ku)],
    )

    early = ([0], coefficient)
    for base, radix in reversed(digit_levels(n)[2:]):
        js, value = early
        masks = [g * base for g in range(radix - 1, 0, -1)]
        more = [([j ^ mask for j in js], exchange(value, mask, n)) for mask in masks]
        early = join([early] + more)

    def hop(part, mask):
        return [j ^ mask for j in part[0]], exchange(part[1], mask, n)

    late = hop(early, 2)
    ready = [early]
    def next_grid(ready, grid):
        return pl.pallas_call(
            functools.partial(next_grid_kernel, [js for js, _ in ready]),
            out_shape=[held(grid_shape, F32), held((1, M), F32)],
            in_specs=[SMEM] * 3 + [VMEM] * (len(ready) + 1),
            out_specs=[VMEM] * 2,
            input_output_aliases={3 + len(ready): 0},
            compiler_params=params(8),
            name="grid_next",
        )(me, facet_offsets, corners, *[near(value) for _, value in ready], near(grid))

    grid, token, basis_near = pl.pallas_call(
        functools.partial(first_grid_kernel, [js for js, _ in ready]),
        out_shape=[held(grid_shape, F32), held((1, M), F32), held(basis.shape)],
        in_specs=[SMEM] * 3 + [ANY] + [VMEM] * len(ready),
        out_specs=[VMEM] * 3,
        scratch_shapes=[pltpu.SemaphoreType.DMA(())],
        compiler_params=params(8),
        name="grid_first",
    )(me, facet_offsets, corners, basis, *[near(value) for _, value in ready])
    other = hop(early, 1)
    late = (late[0], (late[1].astype(F32) + token).astype(BF))
    late_other = hop(late, 1)
    grid, _ = next_grid([other, late], grid)
    update = pl.pallas_call(
        functools.partial(backward_kernel, [late_other[0]]),
        out_shape=[pltpu.HBM(facets.shape, BF), held(grid_shape, F32)],
        in_specs=[SMEM] * 3 + [VMEM] * 3,
        out_specs=[ANY, VMEM],
        input_output_aliases={5: 1},
        scratch_shapes=[
            pltpu.VMEM((2, F, F), BF),
            pltpu.SemaphoreType.DMA((2 * OUT_CHUNKS,)),
        ],
        compiler_params=params(16),
        name="backward",
    )(me, facet_offsets, corners, near(basis_near), near(late_other[1]), near(grid))[0]
    return (residual, update)


def solution(mesh):
    placed = (
        P(("groups", "facet"), None, None, None),
        P(("groups", "facet"), None),
        P("groups", None),
        P(("groups", "facet")),
        P(("groups", "facet")),
        P(("groups", "facet"), None),
        P(("groups", "facet"), None, None, None),
    )
    return jax.shard_map(
        per_device,
        mesh=mesh,
        in_specs=placed,
        out_specs=(
            P(("groups", "facet"), None, None, None),
            P(("groups", "facet"), None, None, None),
        ),
        check_vma=False,
    )
```

```python
import functools
import math

import jax
import jax.numpy as jnp
import ml_dtypes
import numpy as np
from jax import lax
from jax.experimental import pallas as pl
from jax.experimental.pallas import tpu as pltpu
from jax.sharding import PartitionSpec as P

F = 512
M = 128
SG = 512
TV = 128
BF = jnp.bfloat16
F32 = jnp.float32
TWO_PI = 2.0 * math.pi
OUT_CHUNKS = 4


def basis_tables():
    index = np.arange(F, dtype=np.int64)
    angle = -TWO_PI * ((index[:, None] * index[None, :]) % F) / F
    table = np.stack([np.cos(angle), np.sin(angle)]) / math.sqrt(F)
    return table.astype(ml_dtypes.bfloat16)


def padding_tables(facet_count):
    product = (np.arange(SG)[:, None] * np.arange(M)[None, :]) % SG
    angle = TWO_PI * product / SG
    scale = (M * math.sqrt(facet_count)) ** (-0.5)
    table = np.stack([np.cos(angle), np.sin(angle)]) * scale
    return table.astype(ml_dtypes.bfloat16)


def kernel_table():
    rows = np.arange(TV, dtype=np.float64)[:, None]
    columns = np.arange(2 * TV, dtype=np.float64)[None, :]
    distance = columns - 2.0 * rows - 1.0
    value = 0.75 * np.exp(-((distance / 1.5) ** 2))
    return np.where(np.abs(distance) <= 4.0, value, 0.0).astype(ml_dtypes.bfloat16)


def taper_square():
    position = np.arange(M, dtype=np.float64)
    taper = 0.6 + 0.4 * np.sin(math.pi * (position + 0.5) / M)
    return (taper[:, None] * taper[None, :]).astype(np.float32)


def turn_polynomials():
    nodes = 0.5 * np.cos(math.pi * (np.arange(400) + 0.5) / 800)
    square = nodes * nodes
    powers = np.stack([square**k for k in range(8)], axis=1)
    cos_c = np.linalg.lstsq(powers, np.cos(TWO_PI * nodes), rcond=None)[0]
    sin_c = np.linalg.lstsq(powers, np.sin(TWO_PI * nodes) / nodes, rcond=None)[0]
    return [float(c) for c in cos_c], [float(c) for c in sin_c]


COS_C, SIN_C = turn_polynomials()


def cos_sin_turns(turns):
    rest = turns - jnp.floor(turns + 0.5)
    square = rest * rest
    cos_v = jnp.full_like(square, COS_C[7])
    sin_v = jnp.full_like(square, SIN_C[7])
    for k in range(6, -1, -1):
        cos_v = cos_v * square + COS_C[k]
        sin_v = sin_v * square + SIN_C[k]
    return cos_v, sin_v * rest


def dot(left, right):
    return jnp.dot(left, right, preferred_element_type=F32)


def dot_nt(left, right):
    return lax.dot_general(left, right, (((1,), (1,)), ((), ())), preferred_element_type=F32)


def mul_left(left_r, left_i, right_r, right_i):
    left = jnp.concatenate([left_r, left_i], axis=1)
    real = dot(left, jnp.concatenate([right_r, -right_i], axis=0))
    imag = dot(left, jnp.concatenate([right_i, right_r], axis=0))
    return real, imag


def mul_right(left_r, left_i, right_r, right_i):
    right = jnp.concatenate([right_r, right_i], axis=0)
    real = dot(jnp.concatenate([left_r, -left_i], axis=1), right)
    imag = dot(jnp.concatenate([left_i, left_r], axis=1), right)
    return real, imag


def phase_taper(fo_ref):
    rows = lax.broadcasted_iota(jnp.int32, (M, M), 0)
    columns = lax.broadcasted_iota(jnp.int32, (M, M), 1)
    total = (rows * fo_ref[0, 0] + columns * fo_ref[0, 1]) & (F - 1)
    cos_v, sin_v = cos_sin_turns(total.astype(F32) * (1.0 / F))
    row = lax.broadcasted_iota(jnp.int32, (M, 1), 0).astype(F32)
    column = lax.broadcasted_iota(jnp.int32, (1, M), 1).astype(F32)
    _, row_sin = cos_sin_turns((row + 0.5) * (0.5 / M))
    _, column_sin = cos_sin_turns((column + 0.5) * (0.5 / M))
    taper2 = (0.6 + 0.4 * row_sin) * (0.6 + 0.4 * column_sin)
    return cos_v * taper2, sin_v * taper2


def forward_kernel(js, me_ref, fo_hbm, so_hbm, facet_ref, basis_ref, out_ref, spec_ref, *rest):
    facet_buf, basis_buf, fo_ref, so_ref, sems = rest
    copies = [
        pltpu.make_async_copy(fo_hbm, fo_ref, sems.at[4]),
        pltpu.make_async_copy(so_hbm, so_ref, sems.at[5]),
    ]
    for k in range(2):
        copies.append(pltpu.make_async_copy(basis_ref.at[k], basis_buf.at[k], sems.at[2 * k]))
        copies.append(pltpu.make_async_copy(facet_ref.at[0, k], facet_buf.at[k], sems.at[2 * k + 1]))
    for copy in copies:
        copy.start()
    for copy in copies[:2]:
        copy.wait()
    phase = phase_taper(fo_ref)
    for copy in copies[2:]:
        copy.wait()
    br, bi = basis_buf[0], basis_buf[1]
    hr, hi = mul_left(facet_buf[0], facet_buf[1], br, bi)
    spectrum = mul_right(br, bi, hr.astype(BF), hi.astype(BF))
    columns = F // M
    for plane in range(2):
        for c in range(columns):
            part = spectrum[plane][:, c * M : (c + 1) * M]
            spec_ref[plane, c, :F] = part
            spec_ref[plane, c, F:] = part[:M]
            if c == 0:
                spec_ref[plane, columns, :F] = part
                spec_ref[plane, columns, F:] = part[:M]
    extract([js], [out_ref], me_ref, phase, so_ref, spec_ref)


def extract_kernel(sends, me_ref, fo_ref, so_ref, spec_ref, *outs):
    outs = outs[-len(sends) :]
    extract(sends, outs, me_ref, phase_taper(fo_ref), so_ref, spec_ref)


def extract(sends, outs, me_ref, phase, so_ref, spec_ref):
    pc, ps = phase
    me = me_ref[0]

    def block(out_ref, item, j):
        owner = j ^ me
        sx, sy = so_ref[0, owner], so_ref[1, owner]
        lane = sy // M
        shift = (2 * M - (sy & (M - 1))) & (2 * M - 1)
        parts = []
        for plane in range(2):
            left = spec_ref[plane, lane, pl.ds(sx, M), :]
            right = spec_ref[plane, lane + 1, pl.ds(sx, M), :]
            wide = jnp.concatenate([left, right], axis=1)
            parts.append(pltpu.roll(wide, shift, 1)[:, :M])
        wr, wi = parts
        out_ref[item, 0] = (pc * wr - ps * wi).astype(BF)
        out_ref[item, 1] = (pc * wi + ps * wr).astype(BF)

    for out_ref, js in zip(outs, sends):
        for_blocks(block, out_ref, js)


def for_blocks(block, ref, js):
    step = js[1] - js[0] if len(js) > 1 else 1
    if len(js) > 1 and js == list(range(js[0], js[0] + step * len(js), step)):

        def body(item, carry):
            block(ref, item, item * step + js[0])
            return carry

        lax.fori_loop(0, len(js), body, 0)
    else:
        for item, j in enumerate(js):
            block(ref, item, j)


def band_kernel(odd, me_ref, to_ref, kt_hbm, *rest):
    kvt_ref, kut_ref, zero_ref, kt_ref, sem = rest[-5:]
    slots = kut_ref.shape[0]
    zero_ref[...] = jnp.zeros_like(zero_ref)

    @pl.when((me_ref[0] & 1) == odd)
    def _():
        load = pltpu.make_async_copy(kt_hbm, kt_ref, sem)
        load.start()
        load.wait()
        for t in range(slots):
            ou, ov = to_ref[0, t], to_ref[1, t]
            rows = slice(t * TV, (t + 1) * TV)
            kut_ref[t] = kt_ref[pl.ds(2 * TV - ou, SG), :].astype(BF)
            kvt_ref[:, rows] = kt_ref[pl.ds(2 * TV - ov, SG), :].astype(BF)


def screen_kernel(w_ref, to_ref, _, kwide_hbm, *rest):
    loads = (len(rest) - 5) // 2
    sources, screen_ref = rest[:loads], rest[loads]
    targets, (zero_ref, ku_ref, kwide_ref, sems) = rest[loads + 1 : -4], rest[-4:]
    wide_load = pltpu.make_async_copy(kwide_hbm, kwide_ref, sems.at[loads])
    wide_load.start()
    zero_ref[...] = jnp.zeros_like(zero_ref)
    copies = [pltpu.make_async_copy(sources[k], targets[k], sems.at[k]) for k in range(loads)]
    for copy in copies:
        copy.start()
    w = w_ref[0, 0]
    row = lax.broadcasted_iota(jnp.int32, (SG, 1), 0).astype(F32) - SG / 2.0
    column = lax.broadcasted_iota(jnp.int32, (1, SG), 1).astype(F32) - SG / 2.0
    row2 = row * row * (1.0 / (SG * SG)) + 1.0
    column2 = column * column * (1.0 / (SG * SG))
    cos_v, sin_v = cos_sin_turns((jnp.sqrt(row2 + column2) - 1.0) * w)
    screen_ref[0] = cos_v
    screen_ref[1] = sin_v
    wide_load.wait()
    for t in range(ku_ref.shape[0] // TV):
        ku_ref[t * TV : (t + 1) * TV] = pltpu.roll(kwide_ref[...], to_ref[0, t], 1).astype(BF)
    for copy in copies:
        copy.wait()


def subgrid_kernel(picks, tc_ref, *rest):
    parts = len(picks)
    sums = rest[:parts]
    (obs_ref, pad_ref, padt_ref, screen_ref, kvt_ref, kut_ref, ku_ref) = rest[parts : parts + 7]
    (out_ref, coef_ref, model_ref, rows_ref, z_ref, res_ref, sems) = rest[parts + 7 :]
    slots = obs_ref.shape[0]
    count = tc_ref[0, 0]

    def total(plane):
        value = sums[0][picks[0], plane].astype(F32)
        for ref, item in zip(sums[1:], picks[1:]):
            value = value + ref[item, plane].astype(F32)
        return value.astype(BF)

    pr, pi = pad_ref[0], pad_ref[1]
    inner_r, inner_i = mul_right(pr, pi, total(0), total(1))
    tr, ti = padt_ref[0], padt_ref[1]
    image_r, image_i = mul_left(inner_r.astype(BF), inner_i.astype(BF), tr, ti)
    sc, ss = screen_ref[0], screen_ref[1]
    model_ref[:SG] = (sc * image_r - ss * image_i).astype(BF)
    model_ref[SG:] = (sc * image_i + ss * image_r).astype(BF)

    model = model_ref[...]
    for t0 in range(0, slots, 2):
        pair = dot(model, kvt_ref[:, t0 * TV : (t0 + 2) * TV]).astype(BF)
        for t in (t0, t0 + 1):
            lanes = slice((t - t0) * TV, (t - t0 + 1) * TV)
            rows_ref[:, 2 * t * TV : (2 * t + 1) * TV] = pair[:SG, lanes]
            rows_ref[:, (2 * t + 1) * TV : (2 * t + 2) * TV] = pair[SG:, lanes]
    copies = []
    for t in range(slots):
        predicted = dot(ku_ref[t * TV : (t + 1) * TV], rows_ref[:, 2 * t * TV : (2 * t + 2) * TV])
        live = count > t
        for plane in range(2):
            value = obs_ref[t, plane].astype(F32) - predicted[:, plane * TV : (plane + 1) * TV]
            res_ref[t, plane] = jnp.where(live, value, 0.0).astype(BF)
        if t % 4 == 3:
            copies.append(
                pltpu.make_async_copy(
                    res_ref.at[pl.ds(t - 3, 4)], out_ref.at[pl.ds(t - 3, 4)], sems.at[t // 4]
                )
            )
            copies[-1].start()
    for t in range(slots):
        z = dot(kut_ref[t], jnp.concatenate([res_ref[t, 0], res_ref[t, 1]], axis=1)).astype(BF)
        z_ref[:SG, t * TV : (t + 1) * TV] = z[:, :TV]
        z_ref[SG:, t * TV : (t + 1) * TV] = z[:, TV:]

    kvt = kvt_ref[...]
    ar = dot_nt(z_ref[:SG], kvt)
    ai = dot_nt(z_ref[SG:], kvt)
    screened_r = (sc * ar + ss * ai).astype(BF)
    screened_i = (sc * ai - ss * ar).astype(BF)
    reduced_r, reduced_i = mul_right(tr, -ti, screened_r, screened_i)
    coef_r, coef_i = mul_left(reduced_r.astype(BF), reduced_i.astype(BF), pr, -pi)
    coef_ref[0, 0] = coef_r.astype(BF)
    coef_ref[0, 1] = coef_i.astype(BF)
    for copy in copies:
        copy.wait()


def grid_blocks(pieces, refs, me_ref, fo_ref, so_ref, grid_ref):
    pc, ps = phase_taper(fo_ref)
    me = me_ref[0]
    blank = jnp.zeros((M, M), F32)

    def block(in_ref, item, j):
        owner = j ^ me
        sx, sy = so_ref[0, owner], so_ref[1, owner]
        lane = sy // M
        shift = sy & (M - 1)
        cr, ci = in_ref[item, 0].astype(F32), in_ref[item, 1].astype(F32)
        values = (pc * cr + ps * ci, pc * ci - ps * cr)
        for plane in range(2):
            wide = pltpu.roll(jnp.concatenate([values[plane], blank], axis=1), shift, 1)
            grid_ref[plane, lane, pl.ds(sx, M), :] += wide[:, :M]
            grid_ref[plane, lane + 1, pl.ds(sx, M), :] += wide[:, M:]

    for in_ref, js in zip(refs, pieces):
        for_blocks(block, in_ref, js)


def first_grid_kernel(pieces, me_ref, fo_ref, so_ref, basis_hbm, *rest):
    grid_ref, zero_ref, basis_ref, sem = rest[-4:]
    load = pltpu.make_async_copy(basis_hbm, basis_ref, sem)
    load.start()
    zero_ref[...] = jnp.zeros_like(zero_ref)
    grid_ref[...] = jnp.zeros_like(grid_ref)
    grid_blocks(pieces, rest[:-4], me_ref, fo_ref, so_ref, grid_ref)
    load.wait()


def next_grid_kernel(pieces, me_ref, fo_ref, so_ref, *rest):
    grid_ref, _, zero_ref = rest[-3:]
    zero_ref[...] = jnp.zeros_like(zero_ref)
    grid_blocks(pieces, rest[:-3], me_ref, fo_ref, so_ref, grid_ref)


def backward_kernel(pieces, me_ref, fo_ref, so_ref, basis_ref, *rest):
    grid_ref, out_ref, _, out_buf, sems = rest[len(pieces) :]
    grid_blocks(pieces, rest[: len(pieces)], me_ref, fo_ref, so_ref, grid_ref)
    columns = F // M
    folded = []
    for plane in range(2):
        strips = []
        for c in range(columns):
            strip = grid_ref[plane, c]
            if c == 0:
                strip = strip + grid_ref[plane, columns]
            top = strip[:M] + strip[F:]
            strips.append(jnp.concatenate([top.astype(BF), strip[M:F].astype(BF)], axis=0))
        folded.append(jnp.concatenate(strips, axis=1))
    br, bi = basis_ref[0], basis_ref[1]
    hr, hi = mul_right(br, -bi, *folded)
    hr, hi = hr.astype(BF), hi.astype(BF)
    size = F // OUT_CHUNKS
    copies = []
    for k in range(OUT_CHUNKS):
        rows = slice(k * size, (k + 1) * size)
        real, imag = mul_left(hr[rows], hi[rows], br, -bi)
        for plane, value in enumerate((real, imag)):
            out_buf[plane, rows] = value.astype(BF)
            copy = pltpu.make_async_copy(
                out_buf.at[plane, pl.ds(k * size, size)],
                out_ref.at[0, plane, pl.ds(k * size, size)],
                sems.at[2 * k + plane],
            )
            copy.start()
            copies.append(copy)
    for copy in copies:
        copy.wait()


SMEM = pl.BlockSpec(memory_space=pltpu.SMEM)
VMEM = pl.BlockSpec(memory_space=pltpu.VMEM)
ANY = pl.BlockSpec(memory_space=pl.ANY)


def params(mib):
    return pltpu.CompilerParams(vmem_limit_bytes=mib * 1024 * 1024)


def near(value):
    return pltpu.with_memory_space_constraint(value, pltpu.VMEM)


def far(value):
    return pltpu.with_memory_space_constraint(value, pltpu.HBM)


def held(shape, dtype=BF):
    return pltpu.VMEM(shape, dtype)


def exchange(value, mask, n):
    return lax.ppermute(value, "facet", [(i, i ^ mask) for i in range(n)])


def digit_levels(n):
    levels, base = [], 1
    while base < n:
        radix = 2 if base < 4 or n // base < 4 else 4
        levels.append((base, radix))
        base *= radix
    return levels


def reduce_sends(n):
    sends = []
    for base, radix in digit_levels(n):
        for g in range(radix - 1, 0, -1):
            js = [j for j in range(0, n, base) if (j // base) % radix == g]
            groups = [js[1::2], js[::2]] if base == 1 else [js]
            sends += [(group, g * base) for group in groups]
    return sends


def pick(value, items):
    step = items[1] - items[0] if len(items) > 1 else 1
    if items == list(range(items[0], items[0] + step * len(items), step)):
        if len(items) == value.shape[0]:
            return value
        return lax.slice_in_dim(value, items[0], items[-1] + 1, step)
    return jnp.concatenate([value[i : i + 1] for i in items])


def join(pieces):
    return [j for js, _ in pieces for j in js], jnp.concatenate([value for _, value in pieces])


def per_device(facets, facet_offsets, subgrid_offsets, w_terms, tile_count, tile_offsets, observed):
    n = lax.axis_size("facet")
    slots = observed.shape[0]
    me = lax.axis_index("facet").astype(jnp.int32).reshape(1)
    corners = far(subgrid_offsets.T)
    tile_corners = far(tile_offsets.T)
    facet_offsets = far(facet_offsets)
    basis = far(jnp.asarray(basis_tables()))
    pad_np = padding_tables(n)
    kern_np = kernel_table()
    kt_np = np.zeros((6 * TV, TV), np.float32)
    kt_np[2 * TV : 4 * TV] = kern_np.astype(np.float32).T
    kwide_np = np.zeros((TV, SG), np.float32)
    kwide_np[:, : 2 * TV] = kern_np.astype(np.float32)
    grid_shape = (2, F // M + 1, F + M, M)

    sends = reduce_sends(n)
    first, spec = pl.pallas_call(
        functools.partial(forward_kernel, sends[0][0]),
        out_shape=[held((len(sends[0][0]), 2, M, M)), held(grid_shape, F32)],
        in_specs=[SMEM] + [ANY] * 4,
        out_specs=[VMEM] * 2,
        scratch_shapes=[
            pltpu.VMEM((2, F, F), BF),
            pltpu.VMEM((2, F, F), BF),
            pltpu.SMEM(facet_offsets.shape, jnp.int32),
            pltpu.SMEM(corners.shape, jnp.int32),
            pltpu.SemaphoreType.DMA((6,)),
        ],
        compiler_params=params(16),
        name="forward",
    )(me, facet_offsets, corners, far(facets), basis)
    def make_blocks(lists, after):
        return pl.pallas_call(
            functools.partial(extract_kernel, lists),
            out_shape=[held((len(js), 2, M, M)) for js in lists],
            in_specs=[SMEM] * 3 + [VMEM] * (1 + len(after)),
            out_specs=[VMEM] * len(lists),
            compiler_params=params(8),
            name="extract",
        )(me, facet_offsets, corners, near(spec), *[near(value) for value in after])

    def make_bands(odd, bands, after):
        shapes = [(SG, slots * TV), (slots, SG, TV)]
        return pl.pallas_call(
            functools.partial(band_kernel, odd),
            out_shape=[held(shape) for shape in shapes] + [held((1, M), F32)],
            in_specs=[SMEM] * 2 + [ANY] + [VMEM] * (len(bands) + len(after)),
            out_specs=[VMEM] * 3,
            scratch_shapes=[
                pltpu.VMEM(kt_np.shape, F32),
                pltpu.SemaphoreType.DMA(()),
            ],
            input_output_aliases={3 + k: k for k in range(len(bands))},
            compiler_params=params(8),
            name="bands",
        )(
            me,
            tile_corners,
            far(jnp.asarray(kt_np)),
            *[near(value) for value in list(bands) + after],
        )

    def make_screen(after):
        loads = [observed, pad_np, pad_np.transpose(0, 2, 1), subgrid_offsets.T, facet_offsets]
        return pl.pallas_call(
            screen_kernel,
            out_shape=[held((2, SG, SG), F32)] + [held(load.shape, load.dtype) for load in loads]
            + [held((1, M), F32), held((slots * TV, SG))],
            in_specs=[SMEM] * 2 + [VMEM] + [ANY] * (1 + len(loads)),
            out_specs=[VMEM] * (3 + len(loads)),
            scratch_shapes=[pltpu.VMEM(kwide_np.shape, F32), pltpu.SemaphoreType.DMA((len(loads) + 1,))],
            compiler_params=params(8),
            name="screen",
        )(
            w_terms.reshape(1, 1),
            tile_corners,
            near(after),
            far(jnp.asarray(kwide_np)),
            *[far(jnp.asarray(load)) for load in loads],
        )

    arrived = []

    def send(js, mask, value, token=None):
        total = value.astype(F32)
        if token is not None:
            total = total + token
        for got_js, got in arrived:
            if set(js) <= set(got_js):
                total = total + pick(got, [got_js.index(j) for j in js]).astype(F32)
            else:
                assert not set(js) & set(got_js)
        value = total.astype(BF)
        arrived.append(([j ^ mask for j in js], exchange(value, mask, n)))
        return value

    (urgent, _), (lazy, _), (beside, _) = sends[:3]
    send(urgent, 1, first)
    beside_own, lazy_own = make_blocks([beside, lazy], [])
    *bands, token = make_bands(0, [], [beside_own])
    value = send(beside, 2, beside_own, token)
    send(lazy, 1, lazy_own)
    own = make_blocks([js for js, _ in sends[3:]] + [[0]], [value])
    screen, tiles, pad, padt, late_corners, late_facet_offsets, token, ku = make_screen(value)
    for (js, mask), value in zip(sends[3:], own):
        value = send(js, mask, value, token)
    kvt, kut, _ = make_bands(1, bands, [value])
    corners, facet_offsets = near(late_corners), near(late_facet_offsets)
    last = [(js, got) for js, got in arrived if 0 in js]

    residual, coefficient = pl.pallas_call(
        functools.partial(subgrid_kernel, [0] + [js.index(0) for js, _ in last]),
        out_shape=[pltpu.HBM(observed.shape, BF), held((1, 2, M, M))],
        in_specs=[SMEM] + [VMEM] * (len(last) + 8),
        out_specs=[ANY, VMEM],
        scratch_shapes=[
            pltpu.VMEM((2 * SG, SG), BF),
            pltpu.VMEM((SG, 2 * slots * TV), BF),
            pltpu.VMEM((2 * SG, slots * TV), BF),
            pltpu.VMEM(observed.shape, BF),
            pltpu.SemaphoreType.DMA((slots // 4,)),
        ],
        compiler_params=params(24),
        name="subgrid",
    )(
        tile_count.reshape(1, 1),
        near(own[-1]),
        *[near(got) for _, got in last],
        *[near(value) for value in (tiles, pad, padt, screen, kvt, kut, ku)],
    )

    early = ([0], coefficient)
    for base, radix in reversed(digit_levels(n)[2:]):
        js, value = early
        masks = [g * base for g in range(radix - 1, 0, -1)]
        more = [([j ^ mask for j in js], exchange(value, mask, n)) for mask in masks]
        early = join([early] + more)

    def hop(part, mask):
        return [j ^ mask for j in part[0]], exchange(part[1], mask, n)

    late = hop(early, 2)
    ready = [early]
    def next_grid(ready, grid):
        return pl.pallas_call(
            functools.partial(next_grid_kernel, [js for js, _ in ready]),
            out_shape=[held(grid_shape, F32), held((1, M), F32)],
            in_specs=[SMEM] * 3 + [VMEM] * (len(ready) + 1),
            out_specs=[VMEM] * 2,
            input_output_aliases={3 + len(ready): 0},
            compiler_params=params(8),
            name="grid_next",
        )(me, facet_offsets, corners, *[near(value) for _, value in ready], near(grid))

    grid, token, basis_near = pl.pallas_call(
        functools.partial(first_grid_kernel, [js for js, _ in ready]),
        out_shape=[held(grid_shape, F32), held((1, M), F32), held(basis.shape)],
        in_specs=[SMEM] * 3 + [ANY] + [VMEM] * len(ready),
        out_specs=[VMEM] * 3,
        scratch_shapes=[pltpu.SemaphoreType.DMA(())],
        compiler_params=params(8),
        name="grid_first",
    )(me, facet_offsets, corners, basis, *[near(value) for _, value in ready])
    other = hop(early, 1)
    late = (late[0], (late[1].astype(F32) + token).astype(BF))
    late_other = hop(late, 1)
    grid, _ = next_grid([other, late], grid)
    update = pl.pallas_call(
        functools.partial(backward_kernel, [late_other[0]]),
        out_shape=[pltpu.HBM(facets.shape, BF), held(grid_shape, F32)],
        in_specs=[SMEM] * 3 + [VMEM] * 3,
        out_specs=[ANY, VMEM],
        input_output_aliases={5: 1},
        scratch_shapes=[
            pltpu.VMEM((2, F, F), BF),
            pltpu.SemaphoreType.DMA((2 * OUT_CHUNKS,)),
        ],
        compiler_params=params(16),
        name="backward",
    )(me, facet_offsets, corners, near(basis_near), near(late_other[1]), near(grid))[0]
    return (residual, update)


def solution(mesh):
    placed = (
        P(("groups", "facet"), None, None, None),
        P(("groups", "facet"), None),
        P("groups", None),
        P(("groups", "facet")),
        P(("groups", "facet")),
        P(("groups", "facet"), None),
        P(("groups", "facet"), None, None, None),
    )
    return jax.shard_map(
        per_device,
        mesh=mesh,
        in_specs=placed,
        out_specs=(
            P(("groups", "facet"), None, None, None),
            P(("groups", "facet"), None, None, None),
        ),
        check_vma=False,
    )
```

```python
import functools
import math

import jax
import jax.numpy as jnp
import ml_dtypes
import numpy as np
from jax import lax
from jax.experimental import pallas as pl
from jax.experimental.pallas import tpu as pltpu
from jax.sharding import PartitionSpec as P

F = 512
M = 128
SG = 512
TV = 128
BF = jnp.bfloat16
F32 = jnp.float32
TWO_PI = 2.0 * math.pi
OUT_CHUNKS = 2


def basis_tables():
    index = np.arange(F, dtype=np.int64)
    angle = -TWO_PI * ((index[:, None] * index[None, :]) % F) / F
    table = np.stack([np.cos(angle), np.sin(angle)]) / math.sqrt(F)
    return table.astype(ml_dtypes.bfloat16)


def padding_tables(facet_count):
    product = (np.arange(SG)[:, None] * np.arange(M)[None, :]) % SG
    angle = TWO_PI * product / SG
    scale = (M * math.sqrt(facet_count)) ** (-0.5)
    table = np.stack([np.cos(angle), np.sin(angle)]) * scale
    return table.astype(ml_dtypes.bfloat16)


def kernel_table():
    rows = np.arange(TV, dtype=np.float64)[:, None]
    columns = np.arange(2 * TV, dtype=np.float64)[None, :]
    distance = columns - 2.0 * rows - 1.0
    value = 0.75 * np.exp(-((distance / 1.5) ** 2))
    return np.where(np.abs(distance) <= 4.0, value, 0.0).astype(ml_dtypes.bfloat16)


def taper_square():
    position = np.arange(M, dtype=np.float64)
    taper = 0.6 + 0.4 * np.sin(math.pi * (position + 0.5) / M)
    return (taper[:, None] * taper[None, :]).astype(np.float32)


def turn_polynomials():
    nodes = 0.5 * np.cos(math.pi * (np.arange(400) + 0.5) / 800)
    square = nodes * nodes
    powers = np.stack([square**k for k in range(8)], axis=1)
    cos_c = np.linalg.lstsq(powers, np.cos(TWO_PI * nodes), rcond=None)[0]
    sin_c = np.linalg.lstsq(powers, np.sin(TWO_PI * nodes) / nodes, rcond=None)[0]
    return [float(c) for c in cos_c], [float(c) for c in sin_c]


COS_C, SIN_C = turn_polynomials()


def cos_sin_turns(turns):
    rest = turns - jnp.floor(turns + 0.5)
    square = rest * rest
    cos_v = jnp.full_like(square, COS_C[7])
    sin_v = jnp.full_like(square, SIN_C[7])
    for k in range(6, -1, -1):
        cos_v = cos_v * square + COS_C[k]
        sin_v = sin_v * square + SIN_C[k]
    return cos_v, sin_v * rest


def dot(left, right):
    return jnp.dot(left, right, preferred_element_type=F32)


def dot_nt(left, right):
    return lax.dot_general(left, right, (((1,), (1,)), ((), ())), preferred_element_type=F32)


def mul_left(left_r, left_i, right_r, right_i):
    left = jnp.concatenate([left_r, left_i], axis=1)
    real = dot(left, jnp.concatenate([right_r, -right_i], axis=0))
    imag = dot(left, jnp.concatenate([right_i, right_r], axis=0))
    return real, imag


def mul_right(left_r, left_i, right_r, right_i):
    right = jnp.concatenate([right_r, right_i], axis=0)
    real = dot(jnp.concatenate([left_r, -left_i], axis=1), right)
    imag = dot(jnp.concatenate([left_i, left_r], axis=1), right)
    return real, imag


def phase_taper(fo_ref):
    rows = lax.broadcasted_iota(jnp.int32, (M, M), 0)
    columns = lax.broadcasted_iota(jnp.int32, (M, M), 1)
    total = (rows * fo_ref[0, 0] + columns * fo_ref[0, 1]) & (F - 1)
    cos_v, sin_v = cos_sin_turns(total.astype(F32) * (1.0 / F))
    row = lax.broadcasted_iota(jnp.int32, (M, 1), 0).astype(F32)
    column = lax.broadcasted_iota(jnp.int32, (1, M), 1).astype(F32)
    _, row_sin = cos_sin_turns((row + 0.5) * (0.5 / M))
    _, column_sin = cos_sin_turns((column + 0.5) * (0.5 / M))
    taper2 = (0.6 + 0.4 * row_sin) * (0.6 + 0.4 * column_sin)
    return cos_v * taper2, sin_v * taper2


def forward_kernel(js, me_ref, fo_hbm, so_hbm, facet_ref, basis_ref, out_ref, spec_ref, *rest):
    facet_buf, basis_buf, fo_ref, so_ref, sems = rest
    copies = [
        pltpu.make_async_copy(fo_hbm, fo_ref, sems.at[4]),
        pltpu.make_async_copy(so_hbm, so_ref, sems.at[5]),
    ]
    for k in range(2):
        copies.append(pltpu.make_async_copy(basis_ref.at[k], basis_buf.at[k], sems.at[2 * k]))
        copies.append(pltpu.make_async_copy(facet_ref.at[0, k], facet_buf.at[k], sems.at[2 * k + 1]))
    for copy in copies:
        copy.start()
    for copy in copies[:2]:
        copy.wait()
    phase = phase_taper(fo_ref)
    for copy in copies[2:]:
        copy.wait()
    br, bi = basis_buf[0], basis_buf[1]
    hr, hi = mul_left(facet_buf[0], facet_buf[1], br, bi)
    spectrum = mul_right(br, bi, hr.astype(BF), hi.astype(BF))
    columns = F // M
    for plane in range(2):
        for c in range(columns):
            part = spectrum[plane][:, c * M : (c + 1) * M]
            spec_ref[plane, c, :F] = part
            spec_ref[plane, c, F:] = part[:M]
            if c == 0:
                spec_ref[plane, columns, :F] = part
                spec_ref[plane, columns, F:] = part[:M]
    extract([js], [out_ref], me_ref, phase, so_ref, spec_ref)


def extract_kernel(sends, me_ref, fo_ref, so_ref, spec_ref, *outs):
    outs = outs[-len(sends) :]
    extract(sends, outs, me_ref, phase_taper(fo_ref), so_ref, spec_ref)


def extract(sends, outs, me_ref, phase, so_ref, spec_ref):
    pc, ps = phase
    me = me_ref[0]

    def block(out_ref, item, j):
        owner = j ^ me
        sx, sy = so_ref[0, owner], so_ref[1, owner]
        lane = sy // M
        shift = (2 * M - (sy & (M - 1))) & (2 * M - 1)
        parts = []
        for plane in range(2):
            left = spec_ref[plane, lane, pl.ds(sx, M), :]
            right = spec_ref[plane, lane + 1, pl.ds(sx, M), :]
            wide = jnp.concatenate([left, right], axis=1)
            parts.append(pltpu.roll(wide, shift, 1)[:, :M])
        wr, wi = parts
        out_ref[item, 0] = (pc * wr - ps * wi).astype(BF)
        out_ref[item, 1] = (pc * wi + ps * wr).astype(BF)

    for out_ref, js in zip(outs, sends):
        for_blocks(block, out_ref, js)


def for_blocks(block, ref, js):
    step = js[1] - js[0] if len(js) > 1 else 1
    if len(js) > 1 and js == list(range(js[0], js[0] + step * len(js), step)):

        def body(item, carry):
            block(ref, item, item * step + js[0])
            return carry

        lax.fori_loop(0, len(js), body, 0)
    else:
        for item, j in enumerate(js):
            block(ref, item, j)


def band_kernel(odd, me_ref, to_ref, kt_hbm, *rest):
    kvt_ref, kut_ref, zero_ref, kt_ref, sem = rest[-5:]
    slots = kut_ref.shape[0]
    zero_ref[...] = jnp.zeros_like(zero_ref)

    @pl.when((me_ref[0] & 1) == odd)
    def _():
        load = pltpu.make_async_copy(kt_hbm, kt_ref, sem)
        load.start()
        load.wait()
        for t in range(slots):
            ou, ov = to_ref[0, t], to_ref[1, t]
            rows = slice(t * TV, (t + 1) * TV)
            kut_ref[t] = kt_ref[pl.ds(2 * TV - ou, SG), :].astype(BF)
            kvt_ref[:, rows] = kt_ref[pl.ds(2 * TV - ov, SG), :].astype(BF)


def screen_kernel(w_ref, to_ref, _, kwide_hbm, *rest):
    loads = (len(rest) - 5) // 2
    sources, screen_ref = rest[:loads], rest[loads]
    targets, (zero_ref, ku_ref, kwide_ref, sems) = rest[loads + 1 : -4], rest[-4:]
    wide_load = pltpu.make_async_copy(kwide_hbm, kwide_ref, sems.at[loads])
    wide_load.start()
    zero_ref[...] = jnp.zeros_like(zero_ref)
    copies = [pltpu.make_async_copy(sources[k], targets[k], sems.at[k]) for k in range(loads)]
    for copy in copies:
        copy.start()
    w = w_ref[0, 0]
    row = lax.broadcasted_iota(jnp.int32, (SG, 1), 0).astype(F32) - SG / 2.0
    column = lax.broadcasted_iota(jnp.int32, (1, SG), 1).astype(F32) - SG / 2.0
    row2 = row * row * (1.0 / (SG * SG)) + 1.0
    column2 = column * column * (1.0 / (SG * SG))
    cos_v, sin_v = cos_sin_turns((jnp.sqrt(row2 + column2) - 1.0) * w)
    screen_ref[0] = cos_v
    screen_ref[1] = sin_v
    wide_load.wait()
    for t in range(ku_ref.shape[0] // TV):
        ku_ref[t * TV : (t + 1) * TV] = pltpu.roll(kwide_ref[...], to_ref[0, t], 1).astype(BF)
    for copy in copies:
        copy.wait()


def subgrid_kernel(picks, tc_ref, *rest):
    parts = len(picks)
    sums = rest[:parts]
    (obs_ref, pad_ref, padt_ref, screen_ref, kvt_ref, kut_ref, ku_ref) = rest[parts : parts + 7]
    (out_ref, coef_ref, model_ref, rows_ref, z_ref, res_ref, sems) = rest[parts + 7 :]
    slots = obs_ref.shape[0]
    count = tc_ref[0, 0]

    def total(plane):
        value = sums[0][picks[0], plane].astype(F32)
        for ref, item in zip(sums[1:], picks[1:]):
            value = value + ref[item, plane].astype(F32)
        return value.astype(BF)

    pr, pi = pad_ref[0], pad_ref[1]
    inner_r, inner_i = mul_right(pr, pi, total(0), total(1))
    tr, ti = padt_ref[0], padt_ref[1]
    image_r, image_i = mul_left(inner_r.astype(BF), inner_i.astype(BF), tr, ti)
    sc, ss = screen_ref[0], screen_ref[1]
    model_ref[:SG] = (sc * image_r - ss * image_i).astype(BF)
    model_ref[SG:] = (sc * image_i + ss * image_r).astype(BF)

    model = model_ref[...]
    for t0 in range(0, slots, 2):
        pair = dot(model, kvt_ref[:, t0 * TV : (t0 + 2) * TV]).astype(BF)
        for t in (t0, t0 + 1):
            lanes = slice((t - t0) * TV, (t - t0 + 1) * TV)
            rows_ref[:, 2 * t * TV : (2 * t + 1) * TV] = pair[:SG, lanes]
            rows_ref[:, (2 * t + 1) * TV : (2 * t + 2) * TV] = pair[SG:, lanes]
    copies = []
    for t in range(slots):
        predicted = dot(ku_ref[t * TV : (t + 1) * TV], rows_ref[:, 2 * t * TV : (2 * t + 2) * TV])
        live = count > t
        for plane in range(2):
            value = obs_ref[t, plane].astype(F32) - predicted[:, plane * TV : (plane + 1) * TV]
            res_ref[t, plane] = jnp.where(live, value, 0.0).astype(BF)
        if t % 4 == 3:
            copies.append(
                pltpu.make_async_copy(
                    res_ref.at[pl.ds(t - 3, 4)], out_ref.at[pl.ds(t - 3, 4)], sems.at[t // 4]
                )
            )
            copies[-1].start()
    for t in range(slots):
        z = dot(kut_ref[t], jnp.concatenate([res_ref[t, 0], res_ref[t, 1]], axis=1)).astype(BF)
        z_ref[:SG, t * TV : (t + 1) * TV] = z[:, :TV]
        z_ref[SG:, t * TV : (t + 1) * TV] = z[:, TV:]

    kvt = kvt_ref[...]
    ar = dot_nt(z_ref[:SG], kvt)
    ai = dot_nt(z_ref[SG:], kvt)
    screened_r = (sc * ar + ss * ai).astype(BF)
    screened_i = (sc * ai - ss * ar).astype(BF)
    reduced_r, reduced_i = mul_right(tr, -ti, screened_r, screened_i)
    coef_r, coef_i = mul_left(reduced_r.astype(BF), reduced_i.astype(BF), pr, -pi)
    coef_ref[0, 0] = coef_r.astype(BF)
    coef_ref[0, 1] = coef_i.astype(BF)
    for copy in copies:
        copy.wait()


def grid_blocks(pieces, refs, me_ref, fo_ref, so_ref, grid_ref):
    pc, ps = phase_taper(fo_ref)
    me = me_ref[0]
    blank = jnp.zeros((M, M), F32)

    def block(in_ref, item, j):
        owner = j ^ me
        sx, sy = so_ref[0, owner], so_ref[1, owner]
        lane = sy // M
        shift = sy & (M - 1)
        cr, ci = in_ref[item, 0].astype(F32), in_ref[item, 1].astype(F32)
        values = (pc * cr + ps * ci, pc * ci - ps * cr)
        for plane in range(2):
            wide = pltpu.roll(jnp.concatenate([values[plane], blank], axis=1), shift, 1)
            grid_ref[plane, lane, pl.ds(sx, M), :] += wide[:, :M]
            grid_ref[plane, lane + 1, pl.ds(sx, M), :] += wide[:, M:]

    for in_ref, js in zip(refs, pieces):
        for_blocks(block, in_ref, js)


def first_grid_kernel(pieces, me_ref, fo_ref, so_ref, basis_hbm, *rest):
    grid_ref, zero_ref, basis_ref, sem = rest[-4:]
    load = pltpu.make_async_copy(basis_hbm, basis_ref, sem)
    load.start()
    zero_ref[...] = jnp.zeros_like(zero_ref)
    grid_ref[...] = jnp.zeros_like(grid_ref)
    grid_blocks(pieces, rest[:-4], me_ref, fo_ref, so_ref, grid_ref)
    load.wait()


def next_grid_kernel(pieces, me_ref, fo_ref, so_ref, *rest):
    grid_ref, _, zero_ref = rest[-3:]
    zero_ref[...] = jnp.zeros_like(zero_ref)
    grid_blocks(pieces, rest[:-3], me_ref, fo_ref, so_ref, grid_ref)


def backward_kernel(pieces, me_ref, fo_ref, so_ref, basis_ref, *rest):
    grid_ref, out_ref, _, out_buf, sems = rest[len(pieces) :]
    grid_blocks(pieces, rest[: len(pieces)], me_ref, fo_ref, so_ref, grid_ref)
    columns = F // M
    folded = []
    for plane in range(2):
        strips = []
        for c in range(columns):
            strip = grid_ref[plane, c]
            if c == 0:
                strip = strip + grid_ref[plane, columns]
            top = strip[:M] + strip[F:]
            strips.append(jnp.concatenate([top.astype(BF), strip[M:F].astype(BF)], axis=0))
        folded.append(jnp.concatenate(strips, axis=1))
    br, bi = basis_ref[0], basis_ref[1]
    hr, hi = mul_right(br, -bi, *folded)
    hr, hi = hr.astype(BF), hi.astype(BF)
    size = F // OUT_CHUNKS
    copies = []
    for k in range(OUT_CHUNKS):
        rows = slice(k * size, (k + 1) * size)
        real, imag = mul_left(hr[rows], hi[rows], br, -bi)
        for plane, value in enumerate((real, imag)):
            out_buf[plane, rows] = value.astype(BF)
            copy = pltpu.make_async_copy(
                out_buf.at[plane, pl.ds(k * size, size)],
                out_ref.at[0, plane, pl.ds(k * size, size)],
                sems.at[2 * k + plane],
            )
            copy.start()
            copies.append(copy)
    for copy in copies:
        copy.wait()


SMEM = pl.BlockSpec(memory_space=pltpu.SMEM)
VMEM = pl.BlockSpec(memory_space=pltpu.VMEM)
ANY = pl.BlockSpec(memory_space=pl.ANY)


def params(mib):
    return pltpu.CompilerParams(vmem_limit_bytes=mib * 1024 * 1024)


def near(value):
    return pltpu.with_memory_space_constraint(value, pltpu.VMEM)


def far(value):
    return pltpu.with_memory_space_constraint(value, pltpu.HBM)


def held(shape, dtype=BF):
    return pltpu.VMEM(shape, dtype)


def exchange(value, mask, n):
    return lax.ppermute(value, "facet", [(i, i ^ mask) for i in range(n)])


def digit_levels(n):
    levels, base = [], 1
    while base < n:
        radix = 2 if base < 4 or n // base < 4 else 4
        levels.append((base, radix))
        base *= radix
    return levels


def reduce_sends(n):
    sends = []
    for base, radix in digit_levels(n):
        for g in range(radix - 1, 0, -1):
            js = [j for j in range(0, n, base) if (j // base) % radix == g]
            groups = [js[1::2], js[::2]] if base == 1 else [js]
            sends += [(group, g * base) for group in groups]
    return sends


def pick(value, items):
    step = items[1] - items[0] if len(items) > 1 else 1
    if items == list(range(items[0], items[0] + step * len(items), step)):
        if len(items) == value.shape[0]:
            return value
        return lax.slice_in_dim(value, items[0], items[-1] + 1, step)
    return jnp.concatenate([value[i : i + 1] for i in items])


def join(pieces):
    return [j for js, _ in pieces for j in js], jnp.concatenate([value for _, value in pieces])


def per_device(facets, facet_offsets, subgrid_offsets, w_terms, tile_count, tile_offsets, observed):
    n = lax.axis_size("facet")
    slots = observed.shape[0]
    me = lax.axis_index("facet").astype(jnp.int32).reshape(1)
    corners = far(subgrid_offsets.T)
    tile_corners = far(tile_offsets.T)
    facet_offsets = far(facet_offsets)
    basis = far(jnp.asarray(basis_tables()))
    pad_np = padding_tables(n)
    kern_np = kernel_table()
    kt_np = np.zeros((6 * TV, TV), np.float32)
    kt_np[2 * TV : 4 * TV] = kern_np.astype(np.float32).T
    kwide_np = np.zeros((TV, SG), np.float32)
    kwide_np[:, : 2 * TV] = kern_np.astype(np.float32)
    grid_shape = (2, F // M + 1, F + M, M)

    sends = reduce_sends(n)
    first, spec = pl.pallas_call(
        functools.partial(forward_kernel, sends[0][0]),
        out_shape=[held((len(sends[0][0]), 2, M, M)), held(grid_shape, F32)],
        in_specs=[SMEM] + [ANY] * 4,
        out_specs=[VMEM] * 2,
        scratch_shapes=[
            pltpu.VMEM((2, F, F), BF),
            pltpu.VMEM((2, F, F), BF),
            pltpu.SMEM(facet_offsets.shape, jnp.int32),
            pltpu.SMEM(corners.shape, jnp.int32),
            pltpu.SemaphoreType.DMA((6,)),
        ],
        compiler_params=params(16),
        name="forward",
    )(me, facet_offsets, corners, far(facets), basis)
    def make_blocks(lists, after):
        return pl.pallas_call(
            functools.partial(extract_kernel, lists),
            out_shape=[held((len(js), 2, M, M)) for js in lists],
            in_specs=[SMEM] * 3 + [VMEM] * (1 + len(after)),
            out_specs=[VMEM] * len(lists),
            compiler_params=params(8),
            name="extract",
        )(me, facet_offsets, corners, near(spec), *[near(value) for value in after])

    def make_bands(odd, bands, after):
        shapes = [(SG, slots * TV), (slots, SG, TV)]
        return pl.pallas_call(
            functools.partial(band_kernel, odd),
            out_shape=[held(shape) for shape in shapes] + [held((1, M), F32)],
            in_specs=[SMEM] * 2 + [ANY] + [VMEM] * (len(bands) + len(after)),
            out_specs=[VMEM] * 3,
            scratch_shapes=[
                pltpu.VMEM(kt_np.shape, F32),
                pltpu.SemaphoreType.DMA(()),
            ],
            input_output_aliases={3 + k: k for k in range(len(bands))},
            compiler_params=params(8),
            name="bands",
        )(
            me,
            tile_corners,
            far(jnp.asarray(kt_np)),
            *[near(value) for value in list(bands) + after],
        )

    def make_screen(after):
        loads = [observed, pad_np, pad_np.transpose(0, 2, 1), subgrid_offsets.T, facet_offsets]
        return pl.pallas_call(
            screen_kernel,
            out_shape=[held((2, SG, SG), F32)] + [held(load.shape, load.dtype) for load in loads]
            + [held((1, M), F32), held((slots * TV, SG))],
            in_specs=[SMEM] * 2 + [VMEM] + [ANY] * (1 + len(loads)),
            out_specs=[VMEM] * (3 + len(loads)),
            scratch_shapes=[pltpu.VMEM(kwide_np.shape, F32), pltpu.SemaphoreType.DMA((len(loads) + 1,))],
            compiler_params=params(8),
            name="screen",
        )(
            w_terms.reshape(1, 1),
            tile_corners,
            near(after),
            far(jnp.asarray(kwide_np)),
            *[far(jnp.asarray(load)) for load in loads],
        )

    arrived = []

    def send(js, mask, value, token=None):
        total = value.astype(F32)
        if token is not None:
            total = total + token
        for got_js, got in arrived:
            if set(js) <= set(got_js):
                total = total + pick(got, [got_js.index(j) for j in js]).astype(F32)
            else:
                assert not set(js) & set(got_js)
        value = total.astype(BF)
        arrived.append(([j ^ mask for j in js], exchange(value, mask, n)))
        return value

    (urgent, _), (lazy, _), (beside, _) = sends[:3]
    send(urgent, 1, first)
    beside_own, lazy_own = make_blocks([beside, lazy], [])
    *bands, token = make_bands(0, [], [beside_own])
    value = send(beside, 2, beside_own, token)
    send(lazy, 1, lazy_own)
    own = make_blocks([js for js, _ in sends[3:]] + [[0]], [value])
    screen, tiles, pad, padt, late_corners, late_facet_offsets, token, ku = make_screen(value)
    for (js, mask), value in zip(sends[3:], own):
        value = send(js, mask, value, token)
    kvt, kut, _ = make_bands(1, bands, [value])
    corners, facet_offsets = near(late_corners), near(late_facet_offsets)
    last = [(js, got) for js, got in arrived if 0 in js]

    residual, coefficient = pl.pallas_call(
        functools.partial(subgrid_kernel, [0] + [js.index(0) for js, _ in last]),
        out_shape=[pltpu.HBM(observed.shape, BF), held((1, 2, M, M))],
        in_specs=[SMEM] + [VMEM] * (len(last) + 8),
        out_specs=[ANY, VMEM],
        scratch_shapes=[
            pltpu.VMEM((2 * SG, SG), BF),
            pltpu.VMEM((SG, 2 * slots * TV), BF),
            pltpu.VMEM((2 * SG, slots * TV), BF),
            pltpu.VMEM(observed.shape, BF),
            pltpu.SemaphoreType.DMA((slots // 4,)),
        ],
        compiler_params=params(24),
        name="subgrid",
    )(
        tile_count.reshape(1, 1),
        near(own[-1]),
        *[near(got) for _, got in last],
        *[near(value) for value in (tiles, pad, padt, screen, kvt, kut, ku)],
    )

    early = ([0], coefficient)
    for base, radix in reversed(digit_levels(n)[2:]):
        js, value = early
        masks = [g * base for g in range(radix - 1, 0, -1)]
        more = [([j ^ mask for j in js], exchange(value, mask, n)) for mask in masks]
        early = join([early] + more)

    def hop(part, mask):
        return [j ^ mask for j in part[0]], exchange(part[1], mask, n)

    late = hop(early, 2)
    ready = [early]
    def next_grid(ready, grid):
        return pl.pallas_call(
            functools.partial(next_grid_kernel, [js for js, _ in ready]),
            out_shape=[held(grid_shape, F32), held((1, M), F32)],
            in_specs=[SMEM] * 3 + [VMEM] * (len(ready) + 1),
            out_specs=[VMEM] * 2,
            input_output_aliases={3 + len(ready): 0},
            compiler_params=params(8),
            name="grid_next",
        )(me, facet_offsets, corners, *[near(value) for _, value in ready], near(grid))

    grid, token, basis_near = pl.pallas_call(
        functools.partial(first_grid_kernel, [js for js, _ in ready]),
        out_shape=[held(grid_shape, F32), held((1, M), F32), held(basis.shape)],
        in_specs=[SMEM] * 3 + [ANY] + [VMEM] * len(ready),
        out_specs=[VMEM] * 3,
        scratch_shapes=[pltpu.SemaphoreType.DMA(())],
        compiler_params=params(8),
        name="grid_first",
    )(me, facet_offsets, corners, basis, *[near(value) for _, value in ready])
    other = hop(early, 1)
    late = (late[0], (late[1].astype(F32) + token).astype(BF))
    late_other = hop(late, 1)
    grid, _ = next_grid([other, late], grid)
    update = pl.pallas_call(
        functools.partial(backward_kernel, [late_other[0]]),
        out_shape=[pltpu.HBM(facets.shape, BF), held(grid_shape, F32)],
        in_specs=[SMEM] * 3 + [VMEM] * 3,
        out_specs=[ANY, VMEM],
        input_output_aliases={5: 1},
        scratch_shapes=[
            pltpu.VMEM((2, F, F), BF),
            pltpu.SemaphoreType.DMA((2 * OUT_CHUNKS,)),
        ],
        compiler_params=params(16),
        name="backward",
    )(me, facet_offsets, corners, near(basis_near), near(late_other[1]), near(grid))[0]
    return (residual, update)


def solution(mesh):
    placed = (
        P(("groups", "facet"), None, None, None),
        P(("groups", "facet"), None),
        P("groups", None),
        P(("groups", "facet")),
        P(("groups", "facet")),
        P(("groups", "facet"), None),
        P(("groups", "facet"), None, None, None),
    )
    return jax.shard_map(
        per_device,
        mesh=mesh,
        in_specs=placed,
        out_specs=(
            P(("groups", "facet"), None, None, None),
            P(("groups", "facet"), None, None, None),
        ),
        check_vma=False,
    )
```
